32 devices in a mesh: tile: 8 (over z, x), pos: 4 (over y, core).
Axes of the slice: x: 2, y: 2, z: 4, core: 2. Of those that a mesh axis runs over, the one named last changes fastest.
Arguments:
- probe_field: float32 [2, 256, 256], replicated, may hold values from -6 to 6
- specimen: bfloat16 [2, 2, 4096, 512], P(None, None, 'tile'), may hold values from -6 to 6
- amplitude: bfloat16 [256, 256, 256], P(('tile', 'pos')), may hold values from 0 to 2
- scan_anchor: int32 [256, 2], P(('tile', 'pos')), may hold values from 0 to 3840, as said below
- counts: int32 [32], P(('tile', 'pos')), may hold values from 2 to 8, as said below
Outputs:
- object_grad: float32 [2, 2, 4096, 512], P(None, None, 'tile')
- probe_grad: float32 [2, 256, 256], replicated
The draws below stay inside these ranges and needn't reach their ends.
Inputs may be any that keep to these rules, and one draw needn't show every extreme that they name: `scan_anchor`: slot q's patch row r lies in the tile of index t = q // 32: t * 512 <= r < (t + 1) * 512, and the patch lies inside the object. Live slots of a device are its first counts slots; some device is full in every draw.
All inputs are finite; a program needn't handle non-finite values.
Results may differ from the reference program's by a relative error of at most 0.012.
Values may be sent and summed in bfloat16 or wider, within the bound.
No kernel may reach another device: no remote copies, remote signals or barrier semaphores. Data moves between devices by JAX's collectives and lax.ppermute only.
A program may use at most 64 MiB of HBM per device.

```python
import math
import jax
import jax.numpy as jnp
from jax import lax

N = 256
SLICES = 2
TH = 512
TW = 512
POS_DEV = 8
NROWS = 4096
PER_TILE = 32
POSITIONS = 256
N_TILE = 8
N_POS = 4


def draw_scan_anchor(key, part):
    key = jax.random.fold_in(key, 11)
    slot_index = jnp.arange(POSITIONS, dtype=jnp.int32)
    tile_index = slot_index // PER_TILE
    offset_row = jax.random.randint(jax.random.fold_in(key, 1), (POSITIONS,), 0, TH)
    row_start = jnp.minimum(tile_index * TH + offset_row, NROWS - N)
    col_start = jax.random.randint(jax.random.fold_in(key, 2), (POSITIONS,), 0, TW - N + 1)
    row_start = jnp.where(slot_index == 0, 0, row_start)
    row_start = jnp.where(slot_index == (N_TILE - 1) * PER_TILE, NROWS - N, row_start)
    col_start = jnp.where(slot_index == 0, TW - N, col_start)
    return jnp.stack([row_start, col_start], 1).astype(jnp.int32)


def draw_counts(key, part):
    key = jax.random.fold_in(key, 7)
    lowest = min(2, POS_DEV)
    baseline = jax.random.randint(jax.random.fold_in(key, 1), (N_TILE, N_POS), lowest, POS_DEV // 2 + 1)
    busy_tile = jax.random.randint(jax.random.fold_in(key, 2), (N_TILE,), 0, 3) == 0
    busy_tile = jnp.logical_or(busy_tile, jnp.arange(N_TILE) == 0)
    busy_pos = jax.random.randint(jax.random.fold_in(key, 3), (N_TILE,), 0, N_POS)
    marked = jnp.logical_and(jnp.arange(N_POS)[None, :] == busy_pos[:, None], busy_tile[:, None])
    return jnp.where(marked, POS_DEV, baseline).reshape(N_TILE * N_POS).astype(jnp.int32)


def block_scale(own_key, extent, shards, least, largest):
    def one(dim, shards_of):
        heights = jax.random.uniform(jax.random.fold_in(jax.random.fold_in(own_key, 6), dim), (shards_of,), jnp.float32, least / len(shards), largest / len(shards))
        return jnp.repeat(jnp.exp(heights), extent[dim] // shards_of).reshape((-1,) + (1,) * (len(extent) - dim - 1))

    gain = one(*shards[0])
    for cut in shards[1:]:
        gain = gain * one(*cut)
    return gain


def noise(stream_key, dims, deviation, limit, pieces=(), kind=jnp.bfloat16):
    gain = block_scale(stream_key, dims, pieces, -0.22, 0.18) if pieces else 1.0
    values = jax.random.normal(stream_key, dims, jnp.float32) * deviation * gain
    return jnp.minimum(jnp.maximum(values, -limit), limit).astype(kind)


def setup_inputs(seed: int = 0) -> dict:
    key_list = jax.random.split(jax.random.key(seed), 6)
    probe_field = noise(key_list[0], (2, N, N), 1.0, 6.0, (), jnp.float32)
    specimen = noise(key_list[1], (2, SLICES, NROWS, TW), 1.0, 6.0, ((2, 8),))
    amplitude = jnp.clip(2.0 * jax.random.uniform(key_list[2], (POSITIONS, N, N), jnp.float32) ** block_scale(key_list[2], (POSITIONS, N, N), ((0, 32),), -0.2, 0.2), 0.0, 2.0).astype(jnp.bfloat16)
    scan_anchor = draw_scan_anchor(jax.random.fold_in(key_list[5], 71), 0)
    counts = draw_counts(jax.random.fold_in(key_list[5], 71), 0)
    return {"probe_field": probe_field, "specimen": specimen, "amplitude": amplitude, "scan_anchor": scan_anchor, "counts": counts}


PROP_COEF = 0.5
AMP_EPS = 0.05

def make_tables(patch_edge):
    index_row = jnp.arange(patch_edge, dtype=jnp.int32)
    product = index_row[:, None] * index_row[None, :] % patch_edge
    angles = product.astype(jnp.float32) * (2.0 * math.pi / patch_edge)
    cosine = jnp.cos(angles) / math.sqrt(patch_edge)
    sine_part = jnp.sin(angles) / math.sqrt(patch_edge)
    table_one = jnp.concatenate([jnp.concatenate([cosine, sine_part], 1), jnp.concatenate([-sine_part, cosine], 1)], 0)
    table_two = jnp.concatenate([jnp.concatenate([cosine, -sine_part], 1), jnp.concatenate([sine_part, cosine], 1)], 0)
    return (table_one.astype(jnp.bfloat16), table_two.astype(jnp.bfloat16))

def make_kernel(patch_edge):
    index_row = jnp.arange(patch_edge, dtype=jnp.int32)
    centred = jnp.where(index_row < patch_edge // 2, index_row, index_row - patch_edge)
    square = centred * centred
    summed = (square[:, None] + square[None, :]).astype(jnp.float32)
    angles = summed * (PROP_COEF * math.pi / patch_edge)
    return (jnp.cos(angles), -jnp.sin(angles))

def transform(wave, left_table, right_table):
    patch_edge = wave[0].shape[0]
    stacked = jnp.concatenate([wave[0], wave[1]], 0).astype(jnp.bfloat16)
    middle = jnp.dot(left_table, stacked, preferred_element_type=jnp.float32).astype(jnp.bfloat16)
    joined = jnp.concatenate([middle[:patch_edge], middle[patch_edge:]], 1)
    result = jnp.dot(joined, right_table, preferred_element_type=jnp.float32)
    return (result[:, :patch_edge], result[:, patch_edge:])

def complex_mul(left_pair, right_pair):
    return (left_pair[0] * right_pair[0] - left_pair[1] * right_pair[1], left_pair[0] * right_pair[1] + left_pair[1] * right_pair[0])

def conj_mul(left_pair, right_pair):
    return (left_pair[0] * right_pair[0] + left_pair[1] * right_pair[1], left_pair[0] * right_pair[1] - left_pair[1] * right_pair[0])

def position_grads(probe_field, patch_re, patch_im, measured, table_one, table_two, kernel):
    slices = patch_re.shape[0]
    arriving = [(probe_field[0], probe_field[1])]
    leaving = arriving[0]
    for slice_index in range(slices):
        leaving = complex_mul(arriving[slice_index], (patch_re[slice_index], patch_im[slice_index]))
        if slice_index + 1 < slices:
            spectrum = complex_mul(kernel, transform(leaving, table_one, table_two))
            arriving.append(transform(spectrum, table_two, table_one))
    far_re, far_im = transform(leaving, table_one, table_two)
    modulus = jnp.sqrt(far_re * far_re + far_im * far_im + AMP_EPS)
    factor = 1.0 - measured.astype(jnp.float32) / modulus
    adjoint = transform((factor * far_re, factor * far_im), table_two, table_one)
    grads_re = [None] * slices
    grads_im = [None] * slices
    for slice_index in range(slices - 1, -1, -1):
        grads_re[slice_index], grads_im[slice_index] = conj_mul(arriving[slice_index], adjoint)
        adjoint = conj_mul((patch_re[slice_index], patch_im[slice_index]), adjoint)
        if slice_index > 0:
            spectrum = conj_mul(kernel, transform(adjoint, table_one, table_two))
            adjoint = transform(spectrum, table_two, table_one)
    return (jnp.stack(grads_re), jnp.stack(grads_im), adjoint)

def reference(probe_field, specimen, amplitude, scan_anchor, counts):
    table_one, table_two = make_tables(N)
    kernel = make_kernel(N)
    zero_index = jnp.zeros((), jnp.int32)

    def visit(step_index, carry):
        slot_now = jnp.asarray(step_index).astype(jnp.int32)
        live = slot_now % POS_DEV < counts[slot_now // POS_DEV]

        def active(inner):
            row_start = scan_anchor[slot_now, 0].astype(jnp.int32)
            col_start = scan_anchor[slot_now, 1].astype(jnp.int32)
            corner = (zero_index, zero_index, row_start, col_start)
            patch_now = lax.dynamic_slice(specimen, corner, (2, SLICES, N, N)).astype(jnp.float32)
            grad_re, grad_im, probe_term = position_grads(probe_field, patch_now[0], patch_now[1], amplitude[slot_now], table_one, table_two, kernel)
            current = lax.dynamic_slice(inner[0], corner, (2, SLICES, N, N))
            updated = lax.dynamic_update_slice(inner[0], current + jnp.stack([grad_re, grad_im]), corner)
            return (updated, inner[1] + jnp.stack([probe_term[0], probe_term[1]]))

        def unchanged(inner):
            return inner
        return lax.cond(live, active, unchanged, carry)
    start_carry = (jnp.zeros(specimen.shape, jnp.float32), jnp.zeros(probe_field.shape, jnp.float32))
    object_grad, probe_grad = lax.fori_loop(0, POSITIONS, visit, start_carry)
    return (object_grad, probe_grad)
```

```python
import math

import jax
import jax.numpy as jnp
import ml_dtypes
import numpy as np
from jax import lax
from jax.experimental import pallas as pl
from jax.experimental.pallas import tpu as pltpu
from jax.sharding import PartitionSpec as P

PROP_COEF = 0.5
AMP_EPS = 0.05
LANES = 128
CHUNK = 32


def fixed_tables(edge):
    index = np.arange(edge)
    angles = (np.outer(index, index) % edge) * (2.0 * math.pi / edge)
    cosine = (np.cos(angles) / math.sqrt(edge)).astype(ml_dtypes.bfloat16).astype(np.float64)
    sine = (np.sin(angles) / math.sqrt(edge)).astype(ml_dtypes.bfloat16).astype(np.float64)
    forward = cosine - 1j * sine
    centred = np.where(index < edge // 2, index, index - edge)
    ramp = np.exp(-1j * (PROP_COEF * math.pi / edge) * centred * centred)
    spread = (np.conj(forward) * ramp[None, :]) @ forward

    def left_form(matrix):
        return np.block([[matrix.real, -matrix.imag], [matrix.imag, matrix.real]])

    tables = []
    for matrix in (spread, forward):
        tables += [left_form(matrix), left_form(matrix).T]
    return [jnp.asarray(table.astype(ml_dtypes.bfloat16)) for table in tables]


def slots_kernel(
    meta,
    anchor,
    probe,
    spec,
    rim,
    amp,
    left_a,
    right_a,
    left_f,
    right_f,
    send,
    keep,
    keep_probe,
    wide,
    acc,
    probe_acc,
    rolled,
    arriving,
    field,
    stack,
    joined,
):
    edge = probe.shape[1]
    tile_rows = spec.shape[2]
    slices = spec.shape[1]
    col_tiles = spec.shape[3] // LANES
    parts = edge // LANES
    live = meta[0]
    base_row = meta[1]
    half = meta[2]
    lane = lax.broadcasted_iota(jnp.int32, (CHUNK, LANES), 1)

    for part in range(2):
        for s in range(slices):
            for t in range(col_tiles):
                cols = pl.ds(t * LANES, LANES)
                wide[part, s, t, pl.ds(0, tile_rows), :] = spec[part, s, :, cols].astype(
                    jnp.float32
                )
                wide[part, s, t, pl.ds(tile_rows, edge), :] = rim[part, s, :, cols].astype(
                    jnp.float32
                )
                acc[part, s, t] = jnp.zeros(acc.shape[3:], jnp.float32)
    probe_acc[...] = jnp.zeros(probe_acc.shape, jnp.float32)

    def two_sided(left, right, out):
        for part in range(2):
            rows = pl.ds(part * edge, edge)
            joined[:, rows] = jnp.dot(
                left[rows, :], stack[...], preferred_element_type=jnp.float32
            ).astype(jnp.bfloat16)
        for part in range(2):
            out[part] = jnp.dot(
                joined[...],
                right[:, pl.ds(part * edge, edge)],
                preferred_element_type=jnp.float32,
            )

    def visit(slot, carry):
        row = anchor[slot, 0] - base_row
        col = anchor[slot, 1]
        first = jnp.minimum(col // LANES, col_tiles - parts - 1)
        shift = col - first * LANES
        turn = jnp.where(shift >= LANES, 0, shift)
        back = jnp.where(turn == 0, 0, LANES - turn)
        own = lane >= shift

        def patch(part, s, i, j):
            rows = pl.ds(row + i, CHUNK)
            main = wide[part, s, first + j, rows, :]
            if j > 0:
                return main
            return jnp.where(own, main, wide[part, s, first + parts, rows, :])

        def place(part, s, i, j, value):
            rows = pl.ds(row + i, CHUNK)
            if j > 0:
                acc[part, s, first + j, rows, :] += value
            else:
                acc[part, s, first, rows, :] += jnp.where(own, value, 0.0)
                acc[part, s, first + parts, rows, :] += jnp.where(own, 0.0, value)

        def put(i, j, re, im):
            cols = pl.ds(j * LANES, LANES)
            stack[pl.ds(i, CHUNK), cols] = re.astype(jnp.bfloat16)
            stack[pl.ds(edge + i, CHUNK), cols] = im.astype(jnp.bfloat16)

        def tiles():
            for i in range(0, edge, CHUNK):
                for j in range(parts):
                    yield i, j, pl.ds(i, CHUNK), pl.ds(j * LANES, LANES)

        for i in range(0, edge, CHUNK):
            rows = pl.ds(i, CHUNK)
            turned = [
                [
                    pltpu.roll(probe[part, rows, pl.ds(j * LANES, LANES)], turn, 1)
                    for j in range(parts)
                ]
                for part in range(2)
            ]
            for j in range(parts):
                u_re, u_im = [
                    jnp.where(own, turned[part][j], turned[part][j - 1]) for part in range(2)
                ]
                rolled[0, rows, pl.ds(j * LANES, LANES)] = u_re
                rolled[1, rows, pl.ds(j * LANES, LANES)] = u_im
                o_re, o_im = patch(0, 0, i, j), patch(1, 0, i, j)
                put(i, j, u_re * o_re - u_im * o_im, u_re * o_im + u_im * o_re)
        two_sided(left_a, right_a, arriving)
        for i, j, rows, cols in tiles():
            u_re, u_im = arriving[0, rows, cols], arriving[1, rows, cols]
            o_re, o_im = patch(0, 1, i, j), patch(1, 1, i, j)
            put(i, j, u_re * o_re - u_im * o_im, u_re * o_im + u_im * o_re)
        two_sided(left_f, right_f, field)
        for i, j, rows, cols in tiles():
            far_re, far_im = field[0, rows, cols], field[1, rows, cols]
            measured = amp[slot, rows, cols].astype(jnp.float32)
            ratio = measured * lax.rsqrt(far_re * far_re + far_im * far_im + AMP_EPS)
            put(i, j, far_re - ratio * far_re, ratio * far_im - far_im)
        two_sided(left_f, right_f, field)
        for i, j, rows, cols in tiles():
            u_re, u_im = arriving[0, rows, cols], arriving[1, rows, cols]
            w_re, w_im = field[0, rows, cols], field[1, rows, cols]
            place(0, 1, i, j, u_re * w_re - u_im * w_im)
            place(1, 1, i, j, u_re * w_im + u_im * w_re)
            o_re, o_im = patch(0, 1, i, j), patch(1, 1, i, j)
            put(i, j, o_re * w_re - o_im * w_im, o_re * w_im + o_im * w_re)
        two_sided(left_a, right_a, field)
        for i in range(0, edge, CHUNK):
            rows = pl.ds(i, CHUNK)
            turned = [[None] * parts for _ in range(2)]
            for j in range(parts):
                cols = pl.ds(j * LANES, LANES)
                u_re, u_im = rolled[0, rows, cols], rolled[1, rows, cols]
                w_re, w_im = field[0, rows, cols], field[1, rows, cols]
                place(0, 0, i, j, u_re * w_re - u_im * w_im)
                place(1, 0, i, j, u_re * w_im + u_im * w_re)
                o_re, o_im = patch(0, 0, i, j), patch(1, 0, i, j)
                turned[0][j] = pltpu.roll(o_re * w_re - o_im * w_im, back, 1)
                turned[1][j] = pltpu.roll(o_re * w_im + o_im * w_re, back, 1)
            near = lane < LANES - shift
            for part in range(2):
                for j in range(parts):
                    after = turned[part][(j + 1) % parts]
                    probe_acc[part, rows, pl.ds(j * LANES, LANES)] += jnp.where(
                        near, turned[part][j], after
                    )
        return carry

    lax.fori_loop(0, live, visit, 0)

    other = 1 - half
    total = tile_rows + edge
    for part in range(2):
        sign = 1.0 if part == 0 else -1.0
        for t in range(col_tiles):
            cols = pl.ds(t * LANES, LANES)
            send[pl.ds(part * total, total), cols] = (sign * acc[part, other, t]).astype(
                jnp.bfloat16
            )
            keep[part, :, cols] = sign * acc[part, half, t]
    side = send.shape[1] // edge
    deep = edge // side
    flip = jnp.where(other == 1, -1.0, 1.0)
    for piece in range(side):
        send[pl.ds(2 * total, deep), pl.ds(piece * edge, edge)] = (
            flip * probe_acc[other, pl.ds(piece * deep, deep), :]
        ).astype(jnp.bfloat16)
    keep_probe[...] = -flip * probe_acc[half]


def run_slots(meta, anchor, probe, spec, rim, amp, tables):
    edge = probe.shape[1]
    _, slices, tile_rows, width = spec.shape
    col_tiles = width // LANES
    total = tile_rows + edge
    side = width // edge
    vmem = pl.BlockSpec(memory_space=pltpu.VMEM)
    smem = pl.BlockSpec(memory_space=pltpu.SMEM)
    return pl.pallas_call(
        slots_kernel,
        out_shape=(
            jax.ShapeDtypeStruct((2 * total + edge // side, width), jnp.bfloat16),
            jax.ShapeDtypeStruct((2, total, width), jnp.float32),
            jax.ShapeDtypeStruct((edge, edge), jnp.float32),
        ),
        in_specs=[smem, smem] + [vmem] * 8,
        out_specs=(vmem, vmem, vmem),
        scratch_shapes=[
            pltpu.VMEM((2, slices, col_tiles, total, LANES), jnp.float32),
            pltpu.VMEM((2, slices, col_tiles, total, LANES), jnp.float32),
            pltpu.VMEM((2, edge, edge), jnp.float32),
            pltpu.VMEM((2, edge, edge), jnp.float32),
            pltpu.VMEM((2, edge, edge), jnp.float32),
            pltpu.VMEM((2, edge, edge), jnp.float32),
            pltpu.VMEM((2 * edge, edge), jnp.bfloat16),
            pltpu.VMEM((edge, 2 * edge), jnp.bfloat16),
        ],
        compiler_params=pltpu.CompilerParams(vmem_limit_bytes=48 * 1024 * 1024),
        name="slots",
    )(meta, anchor, probe, spec, rim, amp, *tables)


def traded(value, axis, distance):
    count = lax.axis_size(axis)
    return lax.ppermute(value, axis, [(i, i ^ distance) for i in range(count)])


def passed_along(value, axis, steps):
    count = lax.axis_size(axis)
    initial, last = (max(0, -steps), min(count, count - steps))
    return lax.ppermute(value, axis, [(source, source + steps) for source in range(initial, last)])


def body(probe_field, specimen, amplitude, scan_anchor, counts):
    edge = probe_field.shape[1]
    _, slices, tile_rows, width = specimen.shape
    total = tile_rows + edge
    side = width // edge
    deep = edge // side
    half = lax.axis_index("pos") % 2
    base_row = lax.axis_index("tile") * tile_rows
    meta = jnp.stack([counts[0], base_row, half]).astype(jnp.int32)
    rim = passed_along(specimen[:, :, :edge, :], "tile", -1)
    sent, kept, kept_probe = run_slots(
        meta, scan_anchor, probe_field, specimen, rim, amplitude, fixed_tables(edge)
    )
    got = traded(sent, "pos", 1)
    grad = kept + got[: 2 * total].reshape(2, total, width).astype(jnp.float32)
    got_probe = jnp.concatenate(
        [got[2 * total :, p * edge : (p + 1) * edge] for p in range(side)], 0
    )
    probe_part = kept_probe + got_probe.astype(jnp.float32)
    below = passed_along(grad[:, tile_rows:].astype(jnp.bfloat16), "tile", 1)
    lower = grad[:, edge:tile_rows].astype(jnp.bfloat16)
    lower = (lower.astype(jnp.float32) + traded(lower, "pos", 2).astype(jnp.float32)).astype(
        jnp.bfloat16
    )
    upper = (grad[:, :edge] + below.astype(jnp.float32)).astype(jnp.bfloat16)
    upper = (upper.astype(jnp.float32) + traded(upper, "pos", 2).astype(jnp.float32)).astype(
        jnp.bfloat16
    )
    distance = 2
    while distance < lax.axis_size("pos"):
        outgoing = probe_part.astype(jnp.bfloat16)
        probe_part = outgoing.astype(jnp.float32) + traded(outgoing, "pos", distance).astype(
            jnp.float32
        )
        distance *= 2
    distance = 1
    while distance < lax.axis_size("tile"):
        outgoing = probe_part.astype(jnp.bfloat16)
        probe_part = outgoing.astype(jnp.float32) + traded(outgoing, "tile", distance).astype(
            jnp.float32
        )
        distance *= 2
    mine = jnp.concatenate([upper, lower], 1)
    theirs = traded(mine, "pos", 1)
    tile_grad = jnp.where(
        half == 0, jnp.stack([mine, theirs], 1), jnp.stack([theirs, mine], 1)
    ).astype(jnp.float32)
    probe_mine = probe_part.astype(jnp.bfloat16)
    probe_theirs = traded(probe_mine, "pos", 1)
    probe_total = jnp.where(
        half == 0, jnp.stack([probe_mine, probe_theirs]), jnp.stack([probe_theirs, probe_mine])
    ).astype(jnp.float32)
    return (tile_grad, probe_total)


def solution(mesh):
    return jax.shard_map(
        body,
        mesh=mesh,
        in_specs=(
            P(),
            P(None, None, "tile", None),
            P(("tile", "pos"), None, None),
            P(("tile", "pos"), None),
            P(("tile", "pos")),
        ),
        out_specs=(P(None, None, "tile", None), P()),
        check_vma=False,
    )
```

```python
import math

import jax
import jax.numpy as jnp
import ml_dtypes
import numpy as np
from jax import lax
from jax.experimental import pallas as pl
from jax.experimental.pallas import tpu as pltpu
from jax.sharding import PartitionSpec as P

PROP_COEF = 0.5
AMP_EPS = 0.05
LANES = 128
CHUNK = 32


def fixed_tables(edge):
    index = np.arange(edge)
    angles = (np.outer(index, index) % edge) * (2.0 * math.pi / edge)
    cosine = (np.cos(angles) / math.sqrt(edge)).astype(ml_dtypes.bfloat16).astype(np.float64)
    sine = (np.sin(angles) / math.sqrt(edge)).astype(ml_dtypes.bfloat16).astype(np.float64)
    forward = cosine - 1j * sine
    centred = np.where(index < edge // 2, index, index - edge)
    ramp = np.exp(-1j * (PROP_COEF * math.pi / edge) * centred * centred)
    spread = (np.conj(forward) * ramp[None, :]) @ forward

    def left_form(matrix):
        return np.block([[matrix.real, -matrix.imag], [matrix.imag, matrix.real]])

    tables = []
    for matrix in (spread, forward):
        tables += [left_form(matrix), left_form(matrix).T]
    return [jnp.asarray(table.astype(ml_dtypes.bfloat16)) for table in tables]


def interleaved(first, second):
    marks = [(k / len(first), 0, k) for k in range(len(first))]
    marks += [((k + 0.5) / len(second), 1, k) for k in range(len(second))]
    for _, which, k in sorted(marks):
        (first, second)[which][k]()


def slot_stages(slot, alive, base_row, refs, work):
    anchor, probe, amp, tables, wide, acc, probe_acc = refs
    rolled, arriving, field, stack, joined = work
    left_a, right_a, left_f, right_f = tables
    edge = probe.shape[1]
    col_tiles = wide.shape[2]
    parts = edge // LANES
    lane = lax.broadcasted_iota(jnp.int32, (CHUNK, LANES), 1)
    row = anchor[slot, 0] - base_row
    col = anchor[slot, 1]
    first = jnp.minimum(col // LANES, col_tiles - parts - 1)
    shift = col - first * LANES
    turn = jnp.where(shift >= LANES, 0, shift)
    back = jnp.where(turn == 0, 0, LANES - turn)
    own = lane >= shift
    near = lane < LANES - shift

    def patch(part, s, i, j):
        rows = pl.ds(row + i, CHUNK)
        main = wide[part, s, first + j, rows, :]
        if j > 0:
            return main
        return jnp.where(own, main, wide[part, s, first + parts, rows, :])

    def place(part, s, i, j, value):
        rows = pl.ds(row + i, CHUNK)
        if j > 0:
            acc[part, s, first + j, rows, :] += value
        else:
            acc[part, s, first, rows, :] += jnp.where(own, value, 0.0)
            acc[part, s, first + parts, rows, :] += jnp.where(own, 0.0, value)

    def put(i, j, re, im):
        cols = pl.ds(j * LANES, LANES)
        stack[pl.ds(i, CHUNK), cols] = re.astype(jnp.bfloat16)
        stack[pl.ds(edge + i, CHUNK), cols] = im.astype(jnp.bfloat16)

    def halves():
        return [(j, pl.ds(j * LANES, LANES)) for j in range(parts)]

    def enter(i):
        rows = pl.ds(i, CHUNK)
        turned = [
            [pltpu.roll(probe[part, rows, cols], turn, 1) for j, cols in halves()]
            for part in range(2)
        ]
        for j, cols in halves():
            u_re, u_im = [
                jnp.where(own, turned[part][j], turned[part][j - 1]) for part in range(2)
            ]
            rolled[0, rows, cols] = u_re
            rolled[1, rows, cols] = u_im
            o_re, o_im = patch(0, 0, i, j), patch(1, 0, i, j)
            put(i, j, u_re * o_re - u_im * o_im, u_re * o_im + u_im * o_re)

    def second_slice(i):
        rows = pl.ds(i, CHUNK)
        for j, cols in halves():
            u_re, u_im = arriving[0, rows, cols], arriving[1, rows, cols]
            o_re, o_im = patch(0, 1, i, j), patch(1, 1, i, j)
            put(i, j, u_re * o_re - u_im * o_im, u_re * o_im + u_im * o_re)

    def residual(i):
        rows = pl.ds(i, CHUNK)
        for j, cols in halves():
            far_re, far_im = field[0, rows, cols], field[1, rows, cols]
            measured = amp[slot, rows, cols].astype(jnp.float32) * alive
            ratio = measured * lax.rsqrt(far_re * far_re + far_im * far_im + AMP_EPS)
            put(i, j, (alive - ratio) * far_re, (ratio - alive) * far_im)

    def second_grad(i):
        rows = pl.ds(i, CHUNK)
        for j, cols in halves():
            u_re, u_im = arriving[0, rows, cols], arriving[1, rows, cols]
            w_re, w_im = field[0, rows, cols], field[1, rows, cols]
            place(0, 1, i, j, u_re * w_re - u_im * w_im)
            place(1, 1, i, j, u_re * w_im + u_im * w_re)
            o_re, o_im = patch(0, 1, i, j), patch(1, 1, i, j)
            put(i, j, o_re * w_re - o_im * w_im, o_re * w_im + o_im * w_re)

    def first_grad(i):
        rows = pl.ds(i, CHUNK)
        turned = [[None] * parts for _ in range(2)]
        for j, cols in halves():
            u_re, u_im = rolled[0, rows, cols], rolled[1, rows, cols]
            w_re, w_im = field[0, rows, cols], field[1, rows, cols]
            place(0, 0, i, j, u_re * w_re - u_im * w_im)
            place(1, 0, i, j, u_re * w_im + u_im * w_re)
            o_re, o_im = patch(0, 0, i, j), patch(1, 0, i, j)
            turned[0][j] = pltpu.roll(o_re * w_re - o_im * w_im, back, 1)
            turned[1][j] = pltpu.roll(o_re * w_im + o_im * w_re, back, 1)
        for part in range(2):
            for j, cols in halves():
                after = turned[part][(j + 1) % parts]
                probe_acc[part, rows, cols] += jnp.where(near, turned[part][j], after)

    def two_sided(left, right, out):
        def rows_of(part):
            span = pl.ds(part * edge, edge)
            joined[:, span] = jnp.dot(
                left[span, :], stack[...], preferred_element_type=jnp.float32
            ).astype(jnp.bfloat16)

        def cols_of(part):
            out[part] = jnp.dot(
                joined[...],
                right[:, pl.ds(part * edge, edge)],
                preferred_element_type=jnp.float32,
            )

        return [lambda p=p: rows_of(p) for p in range(2)] + [
            lambda p=p: cols_of(p) for p in range(2)
        ]

    def each(step):
        return [lambda i=i: step(i) for i in range(0, edge, CHUNK)]

    return [
        each(enter),
        two_sided(left_a, right_a, arriving),
        each(second_slice),
        two_sided(left_f, right_f, field),
        each(residual),
        two_sided(left_f, right_f, field),
        each(second_grad),
        two_sided(left_a, right_a, field),
        each(first_grad),
    ]


def listed(order, anchor, live, base_row, edge, tile_rows, second_call):
    slots = anchor.shape[0]
    inner = [
        jnp.where((q < live) & (anchor[q, 0] - base_row + edge <= tile_rows), 1, 0)
        for q in range(slots)
    ]
    early = sum(inner) // 2 * 2
    taken = jnp.int32(0)
    rank = jnp.int32(0)
    order[0] = 0
    for q in range(slots):
        ahead = jnp.where(rank < early, inner[q], 0)
        rank = rank + inner[q]
        take = jnp.where(q < live, 1 - ahead, 0) if second_call else ahead
        order[taken] = q
        taken = taken + take
    return taken


def run_pairs(order, total, base_row, refs, work):
    def visit(step, carry):
        a = order[2 * step]
        b_lives = 2 * step + 1 < total
        b = jnp.where(b_lives, order[2 * step + 1], a)
        ones = slot_stages(a, 1.0, base_row, refs, work[0])
        twos = slot_stages(b, jnp.where(b_lives, 1.0, 0.0), base_row, refs, work[1])
        for step_now in ones[0]:
            step_now()
        for k in range(1, len(ones)):
            if k % 2:
                interleaved(ones[k], twos[k - 1])
            else:
                interleaved(twos[k - 1], ones[k])
        for step_now in twos[-1]:
            step_now()
        return carry

    lax.fori_loop(0, (total + 1) // 2, visit, 0)


def widen(wide, source, start, part, s_from, s_to):
    rows = source.shape[-2]
    for t in range(wide.shape[2]):
        wide[part, s_to, t, pl.ds(start, rows), :] = source[
            part, s_from, :, pl.ds(t * LANES, LANES)
        ].astype(jnp.float32)


def early_kernel(
    meta, anchor, probe, spec, amp, la, ra, lf, rf, acc, probe_acc, order, wide, *work
):
    slices, tile_rows = spec.shape[1:3]
    for part in range(2):
        for s in range(slices):
            widen(wide, spec, 0, part, s, s)
            for t in range(wide.shape[2]):
                acc[part, s, t] = jnp.zeros(acc.shape[3:], jnp.float32)
    probe_acc[...] = jnp.zeros(probe_acc.shape, jnp.float32)
    total = listed(order, anchor, meta[0], meta[1], probe.shape[1], tile_rows, False)
    refs = (anchor, probe, amp, (la, ra, lf, rf), wide, acc, probe_acc)
    run_pairs(order, total, meta[1], refs, (work[:5], work[5:]))


def late_kernel(
    meta,
    anchor,
    probe,
    spec,
    rim_own,
    rim_other,
    acc_in,
    probe_in,
    amp,
    la,
    ra,
    lf,
    rf,
    send_low,
    send_top,
    keep_low,
    keep_top,
    keep_probe,
    order,
    wide,
    acc,
    probe_acc,
    *work,
):
    slices, tile_rows, width = spec.shape[1:]
    edge = probe.shape[1]
    half = meta[2]
    other = 1 - half
    col_tiles = width // LANES
    for part in range(2):
        for s in range(slices):
            widen(wide, spec, 0, part, s, s)
            for t in range(col_tiles):
                acc[part, s, t, pl.ds(0, tile_rows), :] = acc_in[part, s, t]
                acc[part, s, t, pl.ds(tile_rows, edge), :] = jnp.zeros((edge, LANES), jnp.float32)
        widen(wide, rim_own, tile_rows, part, 0, half)
        widen(wide, rim_other, tile_rows, part, 0, other)
    probe_acc[...] = probe_in[...]
    total = listed(order, anchor, meta[0], meta[1], edge, tile_rows, True)
    refs = (anchor, probe, amp, (la, ra, lf, rf), wide, acc, probe_acc)
    run_pairs(order, total, meta[1], refs, (work[:5], work[5:]))

    low = pl.ds(edge, tile_rows)
    top = pl.ds(0, edge)
    for part in range(2):
        sign = 1.0 if part == 0 else -1.0
        for t in range(col_tiles):
            cols = pl.ds(t * LANES, LANES)
            send_low[part, :, cols] = (sign * acc[part, other, t, low, :]).astype(jnp.bfloat16)
            keep_low[part, :, cols] = sign * acc[part, half, t, low, :]
            send_top[pl.ds(part * edge, edge), cols] = (sign * acc[part, other, t, top, :]).astype(
                jnp.bfloat16
            )
            keep_top[part, :, cols] = sign * acc[part, half, t, top, :]
    side = width // edge
    deep = edge // side
    flip = jnp.where(other == 1, -1.0, 1.0)
    for piece in range(side):
        send_top[pl.ds(2 * edge, deep), pl.ds(piece * edge, edge)] = (
            flip * probe_acc[other, pl.ds(piece * deep, deep), :]
        ).astype(jnp.bfloat16)
    keep_probe[...] = -flip * probe_acc[half]


VMEM = pl.BlockSpec(memory_space=pltpu.VMEM)
SMEM = pl.BlockSpec(memory_space=pltpu.SMEM)


def scratch(slots, slices, col_tiles, rows, edge):
    one = [
        pltpu.VMEM((2, edge, edge), jnp.float32),
        pltpu.VMEM((2, edge, edge), jnp.float32),
        pltpu.VMEM((2, edge, edge), jnp.float32),
        pltpu.VMEM((2 * edge, edge), jnp.bfloat16),
        pltpu.VMEM((edge, 2 * edge), jnp.bfloat16),
    ]
    order = pltpu.SMEM((slots + 1,), jnp.int32)
    return [order, pltpu.VMEM((2, slices, col_tiles, rows, LANES), jnp.float32)], one + one


def run_early(meta, anchor, probe, spec, amp, tables):
    edge = probe.shape[1]
    _, slices, tile_rows, width = spec.shape
    col_tiles = width // LANES
    lead, work = scratch(anchor.shape[0], slices, col_tiles, tile_rows, edge)
    return pl.pallas_call(
        early_kernel,
        out_shape=(
            jax.ShapeDtypeStruct((2, slices, col_tiles, tile_rows, LANES), jnp.float32),
            jax.ShapeDtypeStruct((2, edge, edge), jnp.float32),
        ),
        in_specs=[SMEM, SMEM] + [VMEM] * 7,
        out_specs=(VMEM, VMEM),
        scratch_shapes=lead + work,
        compiler_params=pltpu.CompilerParams(vmem_limit_bytes=40 * 1024 * 1024),
        name="early_slots",
    )(meta, anchor, probe, spec, amp, *tables)


def run_late(meta, anchor, probe, spec, rim_own, rim_other, acc, probe_acc, amp, tables):
    edge = probe.shape[1]
    _, slices, tile_rows, width = spec.shape
    col_tiles = width // LANES
    total = tile_rows + edge
    side = width // edge
    lead, work = scratch(anchor.shape[0], slices, col_tiles, total, edge)
    return pl.pallas_call(
        late_kernel,
        out_shape=(
            jax.ShapeDtypeStruct((2, tile_rows, width), jnp.bfloat16),
            jax.ShapeDtypeStruct((2 * edge + edge // side, width), jnp.bfloat16),
            jax.ShapeDtypeStruct((2, tile_rows, width), jnp.float32),
            jax.ShapeDtypeStruct((2, edge, width), jnp.float32),
            jax.ShapeDtypeStruct((edge, edge), jnp.float32),
        ),
        in_specs=[SMEM, SMEM] + [VMEM] * 11,
        out_specs=(VMEM,) * 5,
        scratch_shapes=lead
        + [
            pltpu.VMEM((2, slices, col_tiles, total, LANES), jnp.float32),
            pltpu.VMEM((2, edge, edge), jnp.float32),
        ]
        + work,
        compiler_params=pltpu.CompilerParams(vmem_limit_bytes=48 * 1024 * 1024),
        name="late_slots",
    )(meta, anchor, probe, spec, rim_own, rim_other, acc, probe_acc, amp, *tables)


def traded(value, axis, distance):
    count = lax.axis_size(axis)
    return lax.ppermute(value, axis, [(i, i ^ distance) for i in range(count)])


def passed_along(value, axis, steps):
    count = lax.axis_size(axis)
    initial, last = (max(0, -steps), min(count, count - steps))
    return lax.ppermute(value, axis, [(source, source + steps) for source in range(initial, last)])


def narrow_sum(own, got):
    return (own.astype(jnp.float32) + got.astype(jnp.float32)).astype(jnp.bfloat16)


def body(probe_field, specimen, amplitude, scan_anchor, counts):
    edge = probe_field.shape[1]
    _, slices, tile_rows, width = specimen.shape
    side = width // edge
    half = lax.axis_index("pos") % 2
    base_row = lax.axis_index("tile") * tile_rows
    meta = jnp.stack([counts[0], base_row, half]).astype(jnp.int32)
    tables = fixed_tables(edge)
    rim_own = passed_along(
        lax.dynamic_slice(specimen, (0, half, 0, 0), (2, 1, edge, width)), "tile", -1
    )
    rim_other = traded(rim_own, "pos", 1)
    acc, probe_acc = run_early(meta, scan_anchor, probe_field, specimen, amplitude, tables)
    sent_low, sent_top, kept_low, kept_top, kept_probe = run_late(
        meta,
        scan_anchor,
        probe_field,
        specimen,
        rim_own,
        rim_other,
        acc,
        probe_acc,
        amplitude,
        tables,
    )
    got_low = traded(sent_low, "pos", 1)
    got_top = traded(sent_top, "pos", 1)
    low = (kept_low + got_low.astype(jnp.float32)).astype(jnp.bfloat16)
    below = passed_along(low[:, tile_rows - edge :], "tile", 1)
    lower = low[:, : tile_rows - edge]
    lower_got = traded(lower, "pos", 2)
    top = kept_top + got_top[: 2 * edge].reshape(2, edge, width).astype(jnp.float32)
    got_probe = jnp.concatenate(
        [got_top[2 * edge :, p * edge : (p + 1) * edge] for p in range(side)], 0
    )
    probe_part = (kept_probe + got_probe.astype(jnp.float32)).astype(jnp.bfloat16)
    probe_part = narrow_sum(probe_part, traded(probe_part, "pos", 2))
    probe_part = narrow_sum(probe_part, traded(probe_part, "tile", 1))
    below, probe_part = lax.optimization_barrier((below, probe_part))
    upper = (top + below.astype(jnp.float32)).astype(jnp.bfloat16)
    upper_got = traded(upper, "pos", 2)
    distance = 2
    while distance < lax.axis_size("tile"):
        probe_part = narrow_sum(probe_part, traded(probe_part, "tile", distance))
        distance *= 2
    lower = narrow_sum(lower, lower_got)
    lower_theirs = traded(lower, "pos", 1)
    probe_theirs = traded(probe_part, "pos", 1)
    upper_got, lower_theirs, probe_theirs = lax.optimization_barrier(
        (upper_got, lower_theirs, probe_theirs)
    )
    upper = narrow_sum(upper, upper_got)
    upper_theirs = traded(upper, "pos", 1)
    mine = jnp.concatenate([upper, lower], 1)
    theirs = jnp.concatenate([upper_theirs, lower_theirs], 1)
    tile_grad = jnp.where(
        half == 0, jnp.stack([mine, theirs], 1), jnp.stack([theirs, mine], 1)
    ).astype(jnp.float32)
    probe_total = jnp.where(
        half == 0, jnp.stack([probe_part, probe_theirs]), jnp.stack([probe_theirs, probe_part])
    ).astype(jnp.float32)
    return (tile_grad, probe_total)


def solution(mesh):
    return jax.shard_map(
        body,
        mesh=mesh,
        in_specs=(
            P(),
            P(None, None, "tile", None),
            P(("tile", "pos"), None, None),
            P(("tile", "pos"), None),
            P(("tile", "pos")),
        ),
        out_specs=(P(None, None, "tile", None), P()),
        check_vma=False,
    )
```

```python
import math

import jax
import jax.numpy as jnp
import ml_dtypes
import numpy as np
from jax import lax
from jax.experimental import pallas as pl
from jax.experimental.pallas import tpu as pltpu
from jax.sharding import PartitionSpec as P

PROP_COEF = 0.5
AMP_EPS = 0.05
LANES = 128
CHUNK = 32


def fixed_tables(edge):
    index = np.arange(edge)
    angles = (np.outer(index, index) % edge) * (2.0 * math.pi / edge)
    cosine = (np.cos(angles) / math.sqrt(edge)).astype(ml_dtypes.bfloat16).astype(np.float64)
    sine = (np.sin(angles) / math.sqrt(edge)).astype(ml_dtypes.bfloat16).astype(np.float64)
    forward = cosine - 1j * sine
    centred = np.where(index < edge // 2, index, index - edge)
    ramp = np.exp(-1j * (PROP_COEF * math.pi / edge) * centred * centred)
    spread = (np.conj(forward) * ramp[None, :]) @ forward

    def left_form(matrix):
        return np.block([[matrix.real, -matrix.imag], [matrix.imag, matrix.real]])

    tables = []
    for matrix in (spread, forward):
        tables += [left_form(matrix), left_form(matrix).T]
    return [jnp.asarray(table.astype(ml_dtypes.bfloat16)) for table in tables]


def interleaved(first, second):
    marks = [(k / len(first), 0, k) for k in range(len(first))]
    marks += [((k + 0.5) / len(second), 1, k) for k in range(len(second))]
    for _, which, k in sorted(marks):
        (first, second)[which][k]()


def slot_stages(slot, alive, base_row, refs, work):
    anchor, probe, amp, tables, wide, acc, probe_acc = refs
    rolled, arriving, field, stack, joined = work
    left_a, right_a, left_f, right_f = tables
    edge = probe.shape[1]
    col_tiles = wide.shape[2]
    parts = edge // LANES
    lane = lax.broadcasted_iota(jnp.int32, (CHUNK, LANES), 1)
    row = anchor[slot, 0] - base_row
    col = anchor[slot, 1]
    first = jnp.minimum(col // LANES, col_tiles - parts - 1)
    shift = col - first * LANES
    turn = jnp.where(shift >= LANES, 0, shift)
    back = jnp.where(turn == 0, 0, LANES - turn)
    own = lane >= shift
    near = lane < LANES - shift

    def patch(part, s, i, j):
        rows = pl.ds(row + i, CHUNK)
        main = wide[part, s, first + j, rows, :]
        if j > 0:
            return main
        return jnp.where(own, main, wide[part, s, first + parts, rows, :])

    def place(part, s, i, j, value):
        rows = pl.ds(row + i, CHUNK)
        if j > 0:
            acc[part, s, first + j, rows, :] += value
        else:
            acc[part, s, first, rows, :] += jnp.where(own, value, 0.0)
            acc[part, s, first + parts, rows, :] += jnp.where(own, 0.0, value)

    def put(i, j, re, im):
        cols = pl.ds(j * LANES, LANES)
        stack[pl.ds(i, CHUNK), cols] = re.astype(jnp.bfloat16)
        stack[pl.ds(edge + i, CHUNK), cols] = im.astype(jnp.bfloat16)

    def halves():
        return [(j, pl.ds(j * LANES, LANES)) for j in range(parts)]

    def enter(i):
        rows = pl.ds(i, CHUNK)
        turned = [
            [pltpu.roll(probe[part, rows, cols], turn, 1) for j, cols in halves()]
            for part in range(2)
        ]
        for j, cols in halves():
            u_re, u_im = [
                jnp.where(own, turned[part][j], turned[part][j - 1]) for part in range(2)
            ]
            rolled[0, rows, cols] = u_re
            rolled[1, rows, cols] = u_im
            o_re, o_im = patch(0, 0, i, j), patch(1, 0, i, j)
            put(i, j, u_re * o_re - u_im * o_im, u_re * o_im + u_im * o_re)

    def second_slice(i):
        rows = pl.ds(i, CHUNK)
        for j, cols in halves():
            u_re, u_im = arriving[0, rows, cols], arriving[1, rows, cols]
            o_re, o_im = patch(0, 1, i, j), patch(1, 1, i, j)
            put(i, j, u_re * o_re - u_im * o_im, u_re * o_im + u_im * o_re)

    def residual(i):
        rows = pl.ds(i, CHUNK)
        for j, cols in halves():
            far_re, far_im = field[0, rows, cols], field[1, rows, cols]
            measured = amp[slot, rows, cols].astype(jnp.float32) * alive
            ratio = measured * lax.rsqrt(far_re * far_re + far_im * far_im + AMP_EPS)
            put(i, j, (alive - ratio) * far_re, (ratio - alive) * far_im)

    def second_grad(i):
        rows = pl.ds(i, CHUNK)
        for j, cols in halves():
            u_re, u_im = arriving[0, rows, cols], arriving[1, rows, cols]
            w_re, w_im = field[0, rows, cols], field[1, rows, cols]
            place(0, 1, i, j, u_re * w_re - u_im * w_im)
            place(1, 1, i, j, u_re * w_im + u_im * w_re)
            o_re, o_im = patch(0, 1, i, j), patch(1, 1, i, j)
            put(i, j, o_re * w_re - o_im * w_im, o_re * w_im + o_im * w_re)

    def first_grad(i):
        rows = pl.ds(i, CHUNK)
        turned = [[None] * parts for _ in range(2)]
        for j, cols in halves():
            u_re, u_im = rolled[0, rows, cols], rolled[1, rows, cols]
            w_re, w_im = field[0, rows, cols], field[1, rows, cols]
            place(0, 0, i, j, u_re * w_re - u_im * w_im)
            place(1, 0, i, j, u_re * w_im + u_im * w_re)
            o_re, o_im = patch(0, 0, i, j), patch(1, 0, i, j)
            turned[0][j] = pltpu.roll(o_re * w_re - o_im * w_im, back, 1)
            turned[1][j] = pltpu.roll(o_re * w_im + o_im * w_re, back, 1)
        for part in range(2):
            for j, cols in halves():
                after = turned[part][(j + 1) % parts]
                probe_acc[part, rows, cols] += jnp.where(near, turned[part][j], after)

    def two_sided(left, right, out):
        def rows_of(part):
            span = pl.ds(part * edge, edge)
            joined[:, span] = jnp.dot(
                left[span, :], stack[...], preferred_element_type=jnp.float32
            ).astype(jnp.bfloat16)

        def cols_of(part):
            out[part] = jnp.dot(
                joined[...],
                right[:, pl.ds(part * edge, edge)],
                preferred_element_type=jnp.float32,
            )

        return [lambda p=p: rows_of(p) for p in range(2)] + [
            lambda p=p: cols_of(p) for p in range(2)
        ]

    def each(step):
        return [lambda i=i: step(i) for i in range(0, edge, CHUNK)]

    return [
        each(enter),
        two_sided(left_a, right_a, arriving),
        each(second_slice),
        two_sided(left_f, right_f, field),
        each(residual),
        two_sided(left_f, right_f, field),
        each(second_grad),
        two_sided(left_a, right_a, field),
        each(first_grad),
    ]


def listed(order, anchor, live, base_row, edge, tile_rows, second_call):
    slots = anchor.shape[0]
    inner = [
        jnp.where((q < live) & (anchor[q, 0] - base_row + edge <= tile_rows), 1, 0)
        for q in range(slots)
    ]
    early = sum(inner) // 2 * 2
    taken = jnp.int32(0)
    rank = jnp.int32(0)
    order[0] = 0
    for q in range(slots):
        ahead = jnp.where(rank < early, inner[q], 0)
        rank = rank + inner[q]
        take = jnp.where(q < live, 1 - ahead, 0) if second_call else ahead
        order[taken] = q
        taken = taken + take
    return taken


def run_pairs(order, total, base_row, refs, work):
    def visit(step, carry):
        a = order[2 * step]
        b_lives = 2 * step + 1 < total
        b = jnp.where(b_lives, order[2 * step + 1], a)
        ones = slot_stages(a, 1.0, base_row, refs, work[0])
        twos = slot_stages(b, jnp.where(b_lives, 1.0, 0.0), base_row, refs, work[1])
        for step_now in ones[0]:
            step_now()
        for k in range(1, len(ones)):
            if k % 2:
                interleaved(ones[k], twos[k - 1])
            else:
                interleaved(twos[k - 1], ones[k])
        for step_now in twos[-1]:
            step_now()
        return carry

    lax.fori_loop(0, (total + 1) // 2, visit, 0)


def widen(wide, source, start, part, s_from, s_to):
    rows = source.shape[-2]
    for t in range(wide.shape[2]):
        wide[part, s_to, t, pl.ds(start, rows), :] = source[
            part, s_from, :, pl.ds(t * LANES, LANES)
        ].astype(jnp.float32)


def fetch(copies, sems):
    started = {}
    for k, (group, source, target) in enumerate(copies):
        copy = pltpu.make_async_copy(source, target, sems.at[k])
        copy.start()
        started.setdefault(group, []).append(copy)

    def wait(group):
        for copy in started[group]:
            copy.wait()

    return wait


def early_kernel(
    meta,
    anchor,
    probe_hbm,
    spec_hbm,
    amp_hbm,
    la_hbm,
    ra_hbm,
    lf_hbm,
    rf_hbm,
    acc,
    probe_acc,
    order,
    sems,
    probe,
    spec,
    amp,
    la,
    ra,
    lf,
    rf,
    wide,
    *work,
):
    wait = fetch(
        [
            ("spec", spec_hbm, spec),
            ("rest", probe_hbm, probe),
            ("rest", la_hbm, la),
            ("rest", ra_hbm, ra),
            ("rest", lf_hbm, lf),
            ("rest", rf_hbm, rf),
            ("rest", amp_hbm, amp),
        ],
        sems,
    )
    slices, tile_rows = spec.shape[1:3]
    for part in range(2):
        for s in range(slices):
            for t in range(wide.shape[2]):
                acc[part, s, t] = jnp.zeros(acc.shape[3:], jnp.float32)
    probe_acc[...] = jnp.zeros(probe_acc.shape, jnp.float32)
    total = listed(order, anchor, meta[0], meta[1], probe.shape[1], tile_rows, False)
    wait("spec")
    for part in range(2):
        for s in range(slices):
            widen(wide, spec, 0, part, s, s)
    wait("rest")
    refs = (anchor, probe, amp, (la, ra, lf, rf), wide, acc, probe_acc)
    run_pairs(order, total, meta[1], refs, (work[:5], work[5:]))


def late_kernel(
    meta,
    anchor,
    probe_hbm,
    spec_hbm,
    rim_own_any,
    rim_other_any,
    acc_any,
    probe_acc_any,
    amp_hbm,
    la_hbm,
    ra_hbm,
    lf_hbm,
    rf_hbm,
    send_low,
    send_top,
    keep_low,
    keep_top,
    keep_probe,
    order,
    sems,
    probe,
    spec,
    amp,
    la,
    ra,
    lf,
    rf,
    wide,
    rim_own,
    rim_other,
    acc,
    probe_acc,
    *work,
):
    slices, tile_rows, width = spec.shape[1:]
    edge = probe.shape[1]
    wait = fetch(
        [
            ("spec", spec_hbm, spec),
            ("rim", rim_own_any, rim_own),
            ("rim", rim_other_any, rim_other),
            ("acc", acc_any, acc.at[:, :, :, pl.ds(0, tile_rows), :]),
            ("acc", probe_acc_any, probe_acc),
            ("rest", probe_hbm, probe),
            ("rest", la_hbm, la),
            ("rest", ra_hbm, ra),
            ("rest", lf_hbm, lf),
            ("rest", rf_hbm, rf),
            ("rest", amp_hbm, amp),
        ],
        sems,
    )
    half = meta[2]
    other = 1 - half
    col_tiles = width // LANES
    for part in range(2):
        for s in range(slices):
            for t in range(col_tiles):
                acc[part, s, t, pl.ds(tile_rows, edge), :] = jnp.zeros((edge, LANES), jnp.float32)
    total = listed(order, anchor, meta[0], meta[1], edge, tile_rows, True)
    wait("spec")
    for part in range(2):
        for s in range(slices):
            widen(wide, spec, 0, part, s, s)
    wait("rim")
    for part in range(2):
        widen(wide, rim_own, tile_rows, part, 0, half)
        widen(wide, rim_other, tile_rows, part, 0, other)
    wait("acc")
    wait("rest")
    refs = (anchor, probe, amp, (la, ra, lf, rf), wide, acc, probe_acc)
    run_pairs(order, total, meta[1], refs, (work[:5], work[5:]))

    low = pl.ds(edge, tile_rows)
    top = pl.ds(0, edge)
    for part in range(2):
        sign = 1.0 if part == 0 else -1.0
        for t in range(col_tiles):
            cols = pl.ds(t * LANES, LANES)
            send_low[part, :, cols] = (sign * acc[part, other, t, low, :]).astype(jnp.bfloat16)
            keep_low[part, :, cols] = sign * acc[part, half, t, low, :]
            send_top[pl.ds(part * edge, edge), cols] = (sign * acc[part, other, t, top, :]).astype(
                jnp.bfloat16
            )
            keep_top[part, :, cols] = sign * acc[part, half, t, top, :]
    side = width // edge
    deep = edge // side
    flip = jnp.where(other == 1, -1.0, 1.0)
    for piece in range(side):
        send_top[pl.ds(2 * edge, deep), pl.ds(piece * edge, edge)] = (
            flip * probe_acc[other, pl.ds(piece * deep, deep), :]
        ).astype(jnp.bfloat16)
    keep_probe[...] = -flip * probe_acc[half]


VMEM = pl.BlockSpec(memory_space=pltpu.VMEM)
SMEM = pl.BlockSpec(memory_space=pltpu.SMEM)
HBM = pl.BlockSpec(memory_space=pltpu.HBM)
ANY = pl.BlockSpec(memory_space=pl.ANY)


def scratch(slots, slices, width, tile_rows, rows, edge, copies):
    planes = pltpu.VMEM((2, edge, edge), jnp.float32)
    table = pltpu.VMEM((2 * edge, 2 * edge), jnp.bfloat16)
    stack = pltpu.VMEM((2 * edge, edge), jnp.bfloat16)
    joined = pltpu.VMEM((edge, 2 * edge), jnp.bfloat16)
    lead = [
        pltpu.SMEM((slots + 1,), jnp.int32),
        pltpu.SemaphoreType.DMA((copies,)),
        planes,
        pltpu.VMEM((2, slices, tile_rows, width), jnp.bfloat16),
        pltpu.VMEM((slots, edge, edge), jnp.bfloat16),
        table,
        table,
        table,
        table,
        pltpu.VMEM((2, slices, width // LANES, rows, LANES), jnp.float32),
    ]
    return lead, [planes, planes, planes, stack, joined] * 2


def run_early(meta, anchor, probe, spec, amp, tables):
    edge = probe.shape[1]
    _, slices, tile_rows, width = spec.shape
    lead, work = scratch(anchor.shape[0], slices, width, tile_rows, tile_rows, edge, 7)
    return pl.pallas_call(
        early_kernel,
        out_shape=(
            jax.ShapeDtypeStruct((2, slices, width // LANES, tile_rows, LANES), jnp.float32),
            jax.ShapeDtypeStruct((2, edge, edge), jnp.float32),
        ),
        in_specs=[SMEM, SMEM] + [HBM] * 7,
        out_specs=(VMEM, VMEM),
        scratch_shapes=lead + work,
        compiler_params=pltpu.CompilerParams(vmem_limit_bytes=32 * 1024 * 1024),
        name="early_slots",
    )(meta, anchor, probe, spec, amp, *tables)


def run_late(meta, anchor, probe, spec, rim_own, rim_other, acc, probe_acc, amp, tables):
    edge = probe.shape[1]
    _, slices, tile_rows, width = spec.shape
    total = tile_rows + edge
    side = width // edge
    lead, work = scratch(anchor.shape[0], slices, width, tile_rows, total, edge, 11)
    rim = pltpu.VMEM((2, 1, edge, width), jnp.bfloat16)
    return pl.pallas_call(
        late_kernel,
        out_shape=(
            jax.ShapeDtypeStruct((2, tile_rows, width), jnp.bfloat16),
            jax.ShapeDtypeStruct((2 * edge + edge // side, width), jnp.bfloat16),
            jax.ShapeDtypeStruct((2, tile_rows, width), jnp.float32),
            jax.ShapeDtypeStruct((2, edge, width), jnp.float32),
            jax.ShapeDtypeStruct((edge, edge), jnp.float32),
        ),
        in_specs=[SMEM, SMEM, HBM, HBM] + [ANY] * 4 + [HBM] * 5,
        out_specs=(VMEM,) * 5,
        scratch_shapes=lead
        + [
            rim,
            rim,
            pltpu.VMEM((2, slices, width // LANES, total, LANES), jnp.float32),
            pltpu.VMEM((2, edge, edge), jnp.float32),
        ]
        + work,
        compiler_params=pltpu.CompilerParams(vmem_limit_bytes=36 * 1024 * 1024),
        name="late_slots",
    )(meta, anchor, probe, spec, rim_own, rim_other, acc, probe_acc, amp, *tables)


def write_rows(meta, own, theirs, start, shape, base=None):
    slices, rows, width = shape[1], own.shape[1], own.shape[2]

    def kernel(meta, own, theirs, *rest):
        out, wide, sems = rest[-3:]
        half = meta[2]
        wide[half] = own[...].astype(jnp.float32)
        wide[1 - half] = theirs[...].astype(jnp.float32)
        copies = [
            pltpu.make_async_copy(
                wide.at[s, part], out.at[part, s, pl.ds(start, rows), :], sems.at[2 * s + part]
            )
            for s in range(slices)
            for part in range(2)
        ]
        for copy in copies:
            copy.start()
        for copy in copies:
            copy.wait()

    extra = [] if base is None else [base]
    return pl.pallas_call(
        kernel,
        out_shape=jax.ShapeDtypeStruct(shape, jnp.float32),
        in_specs=[SMEM, VMEM, VMEM] + [HBM] * len(extra),
        out_specs=HBM,
        input_output_aliases={} if base is None else {3: 0},
        scratch_shapes=[
            pltpu.VMEM((slices, 2, rows, width), jnp.float32),
            pltpu.SemaphoreType.DMA((2 * slices,)),
        ],
        compiler_params=pltpu.CompilerParams(vmem_limit_bytes=16 * 1024 * 1024),
        name="write_rows",
    )(meta, own, theirs, *extra)


def traded(value, axis, distance):
    count = lax.axis_size(axis)
    return lax.ppermute(value, axis, [(i, i ^ distance) for i in range(count)])


def passed_along(value, axis, steps):
    count = lax.axis_size(axis)
    initial, last = (max(0, -steps), min(count, count - steps))
    return lax.ppermute(value, axis, [(source, source + steps) for source in range(initial, last)])


def narrow_sum(own, got):
    return (own.astype(jnp.float32) + got.astype(jnp.float32)).astype(jnp.bfloat16)


def body(probe_field, specimen, amplitude, scan_anchor, counts):
    edge = probe_field.shape[1]
    _, slices, tile_rows, width = specimen.shape
    side = width // edge
    half = lax.axis_index("pos") % 2
    base_row = lax.axis_index("tile") * tile_rows
    meta = jnp.stack([counts[0], base_row, half]).astype(jnp.int32)
    tables = fixed_tables(edge)
    rim_own = passed_along(
        lax.dynamic_slice(specimen, (0, half, 0, 0), (2, 1, edge, width)), "tile", -1
    )
    acc, probe_acc = run_early(meta, scan_anchor, probe_field, specimen, amplitude, tables)
    rim_own, probe_acc = lax.optimization_barrier((rim_own, probe_acc))
    rim_other = traded(rim_own, "pos", 1)
    sent_low, sent_top, kept_low, kept_top, kept_probe = run_late(
        meta,
        scan_anchor,
        probe_field,
        specimen,
        rim_own,
        rim_other,
        acc,
        probe_acc,
        amplitude,
        tables,
    )
    got_low = traded(sent_low, "pos", 1)
    got_top = traded(sent_top, "pos", 1)
    low = (kept_low + got_low.astype(jnp.float32)).astype(jnp.bfloat16)
    got_top, low = lax.optimization_barrier((got_top, low))
    lower = low[:, : tile_rows - edge]
    lower_got = traded(lower, "pos", 2)
    below = passed_along(low[:, tile_rows - edge :], "tile", 1)
    top = kept_top + got_top[: 2 * edge].reshape(2, edge, width).astype(jnp.float32)
    got_probe = jnp.concatenate(
        [got_top[2 * edge :, p * edge : (p + 1) * edge] for p in range(side)], 0
    )
    probe_part = (kept_probe + got_probe.astype(jnp.float32)).astype(jnp.bfloat16)
    probe_part = narrow_sum(probe_part, traded(probe_part, "pos", 2))
    probe_part = narrow_sum(probe_part, traded(probe_part, "tile", 1))
    below, probe_part = lax.optimization_barrier((below, probe_part))
    upper = (top + below.astype(jnp.float32)).astype(jnp.bfloat16)
    lower_got, upper = lax.optimization_barrier((lower_got, upper))
    upper_got = traded(upper, "pos", 2)
    distance = 2
    while distance < lax.axis_size("tile"):
        probe_part = narrow_sum(probe_part, traded(probe_part, "tile", distance))
        distance *= 2
    lower = narrow_sum(lower, lower_got)
    lower_theirs = traded(lower, "pos", 1)
    tile_grad = write_rows(meta, lower, lower_theirs, edge, specimen.shape)
    probe_theirs = traded(probe_part, "pos", 1)
    probe_total = jnp.where(
        half == 0, jnp.stack([probe_part, probe_theirs]), jnp.stack([probe_theirs, probe_part])
    ).astype(jnp.float32)
    upper_got, tile_grad, probe_total = lax.optimization_barrier(
        (upper_got, tile_grad, probe_total)
    )
    upper = narrow_sum(upper, upper_got)
    upper_theirs = traded(upper, "pos", 1)
    tile_grad = write_rows(meta, upper, upper_theirs, 0, specimen.shape, tile_grad)
    return (tile_grad, probe_total)


def solution(mesh):
    return jax.shard_map(
        body,
        mesh=mesh,
        in_specs=(
            P(),
            P(None, None, "tile", None),
            P(("tile", "pos"), None, None),
            P(("tile", "pos"), None),
            P(("tile", "pos")),
        ),
        out_specs=(P(None, None, "tile", None), P()),
        check_vma=False,
    )
```

```python
import math

import jax
import jax.numpy as jnp
import ml_dtypes
import numpy as np
from jax import lax
from jax.experimental import pallas as pl
from jax.experimental.pallas import tpu as pltpu
from jax.sharding import PartitionSpec as P

PROP_COEF = 0.5
AMP_EPS = 0.05
LANES = 128
CHUNK = 32


def fixed_tables(edge):
    index = np.arange(edge)
    angles = (np.outer(index, index) % edge) * (2.0 * math.pi / edge)
    cosine = (np.cos(angles) / math.sqrt(edge)).astype(ml_dtypes.bfloat16).astype(np.float64)
    sine = (np.sin(angles) / math.sqrt(edge)).astype(ml_dtypes.bfloat16).astype(np.float64)
    forward = cosine - 1j * sine
    centred = np.where(index < edge // 2, index, index - edge)
    ramp = np.exp(-1j * (PROP_COEF * math.pi / edge) * centred * centred)
    spread = (np.conj(forward) * ramp[None, :]) @ forward

    def left_form(matrix):
        return np.block([[matrix.real, -matrix.imag], [matrix.imag, matrix.real]])

    tables = []
    for matrix in (spread, forward):
        tables += [left_form(matrix), left_form(matrix).T]
    return [jnp.asarray(table.astype(ml_dtypes.bfloat16)) for table in tables]


def interleaved(first, second):
    marks = [(k / len(first), 0, k) for k in range(len(first))]
    marks += [((k + 0.5) / len(second), 1, k) for k in range(len(second))]
    for _, which, k in sorted(marks):
        (first, second)[which][k]()


def slot_stages(slot, alive, base_row, refs, work):
    anchor, probe, amp, tables, wide, acc, probe_acc = refs
    rolled, arriving, field, stack, joined = work
    left_a, right_a, left_f, right_f = tables
    edge = probe.shape[1]
    col_tiles = wide.shape[2]
    parts = edge // LANES
    lane = lax.broadcasted_iota(jnp.int32, (CHUNK, LANES), 1)
    row = anchor[slot, 0] - base_row
    col = anchor[slot, 1]
    first = jnp.minimum(col // LANES, col_tiles - parts - 1)
    shift = col - first * LANES
    turn = jnp.where(shift >= LANES, 0, shift)
    back = jnp.where(turn == 0, 0, LANES - turn)
    own = lane >= shift
    near = lane < LANES - shift

    def patch(part, s, i, j):
        rows = pl.ds(row + i, CHUNK)
        main = wide[part, s, first + j, rows, :]
        if j > 0:
            return main
        return jnp.where(own, main, wide[part, s, first + parts, rows, :])

    def place(part, s, i, j, value):
        rows = pl.ds(row + i, CHUNK)
        if j > 0:
            acc[part, s, first + j, rows, :] += value
        else:
            acc[part, s, first, rows, :] += jnp.where(own, value, 0.0)
            acc[part, s, first + parts, rows, :] += jnp.where(own, 0.0, value)

    def put(i, j, re, im):
        cols = pl.ds(j * LANES, LANES)
        stack[pl.ds(i, CHUNK), cols] = re.astype(jnp.bfloat16)
        stack[pl.ds(edge + i, CHUNK), cols] = im.astype(jnp.bfloat16)

    def halves():
        return [(j, pl.ds(j * LANES, LANES)) for j in range(parts)]

    def enter(i):
        rows = pl.ds(i, CHUNK)
        turned = [
            [pltpu.roll(probe[part, rows, cols], turn, 1) for j, cols in halves()]
            for part in range(2)
        ]
        for j, cols in halves():
            u_re, u_im = [
                jnp.where(own, turned[part][j], turned[part][j - 1]) for part in range(2)
            ]
            rolled[0, rows, cols] = u_re
            rolled[1, rows, cols] = u_im
            o_re, o_im = patch(0, 0, i, j), patch(1, 0, i, j)
            put(i, j, u_re * o_re - u_im * o_im, u_re * o_im + u_im * o_re)

    def second_slice(i):
        rows = pl.ds(i, CHUNK)
        for j, cols in halves():
            u_re, u_im = arriving[0, rows, cols], arriving[1, rows, cols]
            o_re, o_im = patch(0, 1, i, j), patch(1, 1, i, j)
            put(i, j, u_re * o_re - u_im * o_im, u_re * o_im + u_im * o_re)

    def residual(i):
        rows = pl.ds(i, CHUNK)
        for j, cols in halves():
            far_re, far_im = field[0, rows, cols], field[1, rows, cols]
            measured = amp[slot, rows, cols].astype(jnp.float32) * alive
            ratio = measured * lax.rsqrt(far_re * far_re + far_im * far_im + AMP_EPS)
            put(i, j, (alive - ratio) * far_re, (ratio - alive) * far_im)

    def second_grad(i):
        rows = pl.ds(i, CHUNK)
        for j, cols in halves():
            u_re, u_im = arriving[0, rows, cols], arriving[1, rows, cols]
            w_re, w_im = field[0, rows, cols], field[1, rows, cols]
            place(0, 1, i, j, u_re * w_re - u_im * w_im)
            place(1, 1, i, j, u_re * w_im + u_im * w_re)
            o_re, o_im = patch(0, 1, i, j), patch(1, 1, i, j)
            put(i, j, o_re * w_re - o_im * w_im, o_re * w_im + o_im * w_re)

    def first_grad(i):
        rows = pl.ds(i, CHUNK)
        turned = [[None] * parts for _ in range(2)]
        for j, cols in halves():
            u_re, u_im = rolled[0, rows, cols], rolled[1, rows, cols]
            w_re, w_im = field[0, rows, cols], field[1, rows, cols]
            place(0, 0, i, j, u_re * w_re - u_im * w_im)
            place(1, 0, i, j, u_re * w_im + u_im * w_re)
            o_re, o_im = patch(0, 0, i, j), patch(1, 0, i, j)
            turned[0][j] = pltpu.roll(o_re * w_re - o_im * w_im, back, 1)
            turned[1][j] = pltpu.roll(o_re * w_im + o_im * w_re, back, 1)
        for part in range(2):
            for j, cols in halves():
                after = turned[part][(j + 1) % parts]
                probe_acc[part, rows, cols] += jnp.where(near, turned[part][j], after)

    def two_sided(left, right, out):
        def rows_of(part):
            span = pl.ds(part * edge, edge)
            joined[:, span] = jnp.dot(
                left[span, :], stack[...], preferred_element_type=jnp.float32
            ).astype(jnp.bfloat16)

        def cols_of(part):
            out[part] = jnp.dot(
                joined[...],
                right[:, pl.ds(part * edge, edge)],
                preferred_element_type=jnp.float32,
            )

        return [lambda p=p: rows_of(p) for p in range(2)] + [
            lambda p=p: cols_of(p) for p in range(2)
        ]

    def each(step):
        return [lambda i=i: step(i) for i in range(0, edge, CHUNK)]

    return [
        each(enter),
        two_sided(left_a, right_a, arriving),
        each(second_slice),
        two_sided(left_f, right_f, field),
        each(residual),
        two_sided(left_f, right_f, field),
        each(second_grad),
        two_sided(left_a, right_a, field),
        each(first_grad),
    ]


def listed(order, anchor, live, base_row, edge, tile_rows, second_call):
    slots = anchor.shape[0]
    inner = [
        jnp.where((q < live) & (anchor[q, 0] - base_row + edge <= tile_rows), 1, 0)
        for q in range(slots)
    ]
    early = sum(inner) // 2 * 2
    taken = jnp.int32(0)
    rank = jnp.int32(0)
    order[0] = 0
    for q in range(slots):
        ahead = jnp.where(rank < early, inner[q], 0)
        rank = rank + inner[q]
        take = jnp.where(q < live, 1 - ahead, 0) if second_call else ahead
        order[taken] = q
        taken = taken + take
    return taken


def run_pairs(order, total, base_row, refs, work):
    def visit(step, carry):
        a = order[2 * step]
        b_lives = 2 * step + 1 < total
        b = jnp.where(b_lives, order[2 * step + 1], a)
        ones = slot_stages(a, 1.0, base_row, refs, work[0])
        twos = slot_stages(b, jnp.where(b_lives, 1.0, 0.0), base_row, refs, work[1])
        for step_now in ones[0]:
            step_now()
        for k in range(1, len(ones)):
            if k % 2:
                interleaved(ones[k], twos[k - 1])
            else:
                interleaved(twos[k - 1], ones[k])
        for step_now in twos[-1]:
            step_now()
        return carry

    lax.fori_loop(0, (total + 1) // 2, visit, 0)


def widen(wide, source, start, part, s_from, s_to):
    rows = source.shape[-2]
    for t in range(wide.shape[2]):
        wide[part, s_to, t, pl.ds(start, rows), :] = source[
            part, s_from, :, pl.ds(t * LANES, LANES)
        ].astype(jnp.float32)


def fetch(copies, sems):
    started = {}
    for k, (group, source, target) in enumerate(copies):
        copy = pltpu.make_async_copy(source, target, sems.at[k])
        copy.start()
        started.setdefault(group, []).append(copy)

    def wait(group):
        for copy in started[group]:
            copy.wait()

    return wait


def early_kernel(
    meta,
    anchor,
    probe_hbm,
    spec_hbm,
    amp_hbm,
    la_hbm,
    ra_hbm,
    lf_hbm,
    rf_hbm,
    acc,
    probe_acc,
    order,
    sems,
    probe,
    spec,
    amp,
    la,
    ra,
    lf,
    rf,
    wide,
    *work,
):
    wait = fetch(
        [
            ("spec", spec_hbm, spec),
            ("rest", probe_hbm, probe),
            ("rest", la_hbm, la),
            ("rest", ra_hbm, ra),
            ("rest", lf_hbm, lf),
            ("rest", rf_hbm, rf),
            ("rest", amp_hbm, amp),
        ],
        sems,
    )
    slices, tile_rows = spec.shape[1:3]
    for part in range(2):
        for s in range(slices):
            for t in range(wide.shape[2]):
                acc[part, s, t] = jnp.zeros(acc.shape[3:], jnp.float32)
    probe_acc[...] = jnp.zeros(probe_acc.shape, jnp.float32)
    total = listed(order, anchor, meta[0], meta[1], probe.shape[1], tile_rows, False)
    wait("spec")
    for part in range(2):
        for s in range(slices):
            widen(wide, spec, 0, part, s, s)
    wait("rest")
    refs = (anchor, probe, amp, (la, ra, lf, rf), wide, acc, probe_acc)
    run_pairs(order, total, meta[1], refs, (work[:5], work[5:]))


def late_kernel(
    meta,
    anchor,
    probe_hbm,
    spec_hbm,
    rim_own_any,
    rim_other_any,
    acc_any,
    probe_acc_any,
    amp_hbm,
    la_hbm,
    ra_hbm,
    lf_hbm,
    rf_hbm,
    send_low,
    send_top,
    keep_low,
    keep_top,
    keep_probe,
    order,
    sems,
    probe,
    spec,
    amp,
    la,
    ra,
    lf,
    rf,
    wide,
    rim_own,
    rim_other,
    acc,
    probe_acc,
    *work,
):
    slices, tile_rows, width = spec.shape[1:]
    edge = probe.shape[1]
    wait = fetch(
        [
            ("spec", spec_hbm, spec),
            ("rim", rim_own_any, rim_own),
            ("rim", rim_other_any, rim_other),
            ("acc", acc_any, acc.at[:, :, :, pl.ds(0, tile_rows), :]),
            ("acc", probe_acc_any, probe_acc),
            ("rest", probe_hbm, probe),
            ("rest", la_hbm, la),
            ("rest", ra_hbm, ra),
            ("rest", lf_hbm, lf),
            ("rest", rf_hbm, rf),
            ("rest", amp_hbm, amp),
        ],
        sems,
    )
    half = meta[2]
    other = 1 - half
    col_tiles = width // LANES
    for part in range(2):
        for s in range(slices):
            for t in range(col_tiles):
                acc[part, s, t, pl.ds(tile_rows, edge), :] = jnp.zeros((edge, LANES), jnp.float32)
    total = listed(order, anchor, meta[0], meta[1], edge, tile_rows, True)
    wait("spec")
    for part in range(2):
        for s in range(slices):
            widen(wide, spec, 0, part, s, s)
    wait("rim")
    for part in range(2):
        widen(wide, rim_own, tile_rows, part, 0, half)
        widen(wide, rim_other, tile_rows, part, 0, other)
    wait("acc")
    wait("rest")
    refs = (anchor, probe, amp, (la, ra, lf, rf), wide, acc, probe_acc)
    run_pairs(order, total, meta[1], refs, (work[:5], work[5:]))

    low = pl.ds(edge, tile_rows)
    top = pl.ds(0, edge)
    for part in range(2):
        sign = 1.0 if part == 0 else -1.0
        for t in range(col_tiles):
            cols = pl.ds(t * LANES, LANES)
            send_low[part, :, cols] = (sign * acc[part, other, t, low, :]).astype(jnp.bfloat16)
            keep_low[part, :, cols] = sign * acc[part, half, t, low, :]
            send_top[pl.ds(part * edge, edge), cols] = (sign * acc[part, other, t, top, :]).astype(
                jnp.bfloat16
            )
            keep_top[part, :, cols] = sign * acc[part, half, t, top, :]
    side = width // edge
    deep = edge // side
    flip = jnp.where(other == 1, -1.0, 1.0)
    for piece in range(side):
        send_top[pl.ds(2 * edge, deep), pl.ds(piece * edge, edge)] = (
            flip * probe_acc[other, pl.ds(piece * deep, deep), :]
        ).astype(jnp.bfloat16)
    keep_probe[...] = -flip * probe_acc[half]


VMEM = pl.BlockSpec(memory_space=pltpu.VMEM)
SMEM = pl.BlockSpec(memory_space=pltpu.SMEM)
HBM = pl.BlockSpec(memory_space=pltpu.HBM)
ANY = pl.BlockSpec(memory_space=pl.ANY)


def scratch(slots, slices, width, tile_rows, rows, edge, copies):
    planes = pltpu.VMEM((2, edge, edge), jnp.float32)
    table = pltpu.VMEM((2 * edge, 2 * edge), jnp.bfloat16)
    stack = pltpu.VMEM((2 * edge, edge), jnp.bfloat16)
    joined = pltpu.VMEM((edge, 2 * edge), jnp.bfloat16)
    lead = [
        pltpu.SMEM((slots + 1,), jnp.int32),
        pltpu.SemaphoreType.DMA((copies,)),
        planes,
        pltpu.VMEM((2, slices, tile_rows, width), jnp.bfloat16),
        pltpu.VMEM((slots, edge, edge), jnp.bfloat16),
        table,
        table,
        table,
        table,
        pltpu.VMEM((2, slices, width // LANES, rows, LANES), jnp.float32),
    ]
    return lead, [planes, planes, planes, stack, joined] * 2


def run_early(meta, anchor, probe, spec, amp, tables):
    edge = probe.shape[1]
    _, slices, tile_rows, width = spec.shape
    lead, work = scratch(anchor.shape[0], slices, width, tile_rows, tile_rows, edge, 7)
    return pl.pallas_call(
        early_kernel,
        out_shape=(
            jax.ShapeDtypeStruct((2, slices, width // LANES, tile_rows, LANES), jnp.float32),
            jax.ShapeDtypeStruct((2, edge, edge), jnp.float32),
        ),
        in_specs=[SMEM, SMEM] + [HBM] * 7,
        out_specs=(VMEM, VMEM),
        scratch_shapes=lead + work,
        compiler_params=pltpu.CompilerParams(vmem_limit_bytes=62 * 1024 * 1024),
        name="early_slots",
    )(meta, anchor, probe, spec, amp, *tables)


def run_late(meta, anchor, probe, spec, rim_own, rim_other, acc, probe_acc, amp, tables):
    edge = probe.shape[1]
    _, slices, tile_rows, width = spec.shape
    total = tile_rows + edge
    side = width // edge
    lead, work = scratch(anchor.shape[0], slices, width, tile_rows, total, edge, 11)
    rim = pltpu.VMEM((2, 1, edge, width), jnp.bfloat16)
    return pl.pallas_call(
        late_kernel,
        out_shape=(
            jax.ShapeDtypeStruct((2, tile_rows, width), jnp.bfloat16),
            jax.ShapeDtypeStruct((2 * edge + edge // side, width), jnp.bfloat16),
            jax.ShapeDtypeStruct((2, tile_rows, width), jnp.float32),
            jax.ShapeDtypeStruct((2, edge, width), jnp.float32),
            jax.ShapeDtypeStruct((edge, edge), jnp.float32),
        ),
        in_specs=[SMEM, SMEM, HBM, HBM] + [ANY] * 4 + [HBM] * 5,
        out_specs=(VMEM,) * 5,
        scratch_shapes=lead
        + [
            rim,
            rim,
            pltpu.VMEM((2, slices, width // LANES, total, LANES), jnp.float32),
            pltpu.VMEM((2, edge, edge), jnp.float32),
        ]
        + work,
        compiler_params=pltpu.CompilerParams(vmem_limit_bytes=60 * 1024 * 1024),
        name="late_slots",
    )(meta, anchor, probe, spec, rim_own, rim_other, acc, probe_acc, amp, *tables)


def write_rows(meta, own, theirs, start, shape, base=None):
    slices, rows, width = shape[1], own.shape[1], own.shape[2]

    def kernel(meta, own, theirs, *rest):
        out, wide, sems = rest[-3:]
        half = meta[2]
        wide[half] = own[...].astype(jnp.float32)
        wide[1 - half] = theirs[...].astype(jnp.float32)
        copies = [
            pltpu.make_async_copy(
                wide.at[s, part], out.at[part, s, pl.ds(start, rows), :], sems.at[2 * s + part]
            )
            for s in range(slices)
            for part in range(2)
        ]
        for copy in copies:
            copy.start()
        for copy in copies:
            copy.wait()

    extra = [] if base is None else [base]
    return pl.pallas_call(
        kernel,
        out_shape=jax.ShapeDtypeStruct(shape, jnp.float32),
        in_specs=[SMEM, VMEM, VMEM] + [HBM] * len(extra),
        out_specs=HBM,
        input_output_aliases={} if base is None else {3: 0},
        scratch_shapes=[
            pltpu.VMEM((slices, 2, rows, width), jnp.float32),
            pltpu.SemaphoreType.DMA((2 * slices,)),
        ],
        compiler_params=pltpu.CompilerParams(vmem_limit_bytes=16 * 1024 * 1024),
        name="write_rows",
    )(meta, own, theirs, *extra)


def traded(value, axis, distance):
    count = lax.axis_size(axis)
    return lax.ppermute(value, axis, [(i, i ^ distance) for i in range(count)])


def passed_along(value, axis, steps):
    count = lax.axis_size(axis)
    initial, last = (max(0, -steps), min(count, count - steps))
    return lax.ppermute(value, axis, [(source, source + steps) for source in range(initial, last)])


def narrow_sum(own, got):
    return (own.astype(jnp.float32) + got.astype(jnp.float32)).astype(jnp.bfloat16)


def unfolded(value, edge):
    return jnp.concatenate([value[:, k : k + edge] for k in range(0, value.shape[1], edge)], 0)


def body(probe_field, specimen, amplitude, scan_anchor, counts):
    edge = probe_field.shape[1]
    _, slices, tile_rows, width = specimen.shape
    side = width // edge
    deep = edge // side
    half = lax.axis_index("pos") % 2
    base_row = lax.axis_index("tile") * tile_rows
    meta = jnp.stack([counts[0], base_row, half]).astype(jnp.int32)
    tables = fixed_tables(edge)
    rim_own = passed_along(
        lax.dynamic_slice(specimen, (0, half, 0, 0), (2, 1, edge, width)), "tile", -1
    )
    acc, probe_acc = run_early(meta, scan_anchor, probe_field, specimen, amplitude, tables)
    rim_own, probe_acc = lax.optimization_barrier((rim_own, probe_acc))
    rim_other = traded(rim_own, "pos", 1)
    sent_low, sent_top, kept_low, kept_top, kept_probe = run_late(
        meta,
        scan_anchor,
        probe_field,
        specimen,
        rim_own,
        rim_other,
        acc,
        probe_acc,
        amplitude,
        tables,
    )
    low = (kept_low + traded(sent_low, "pos", 1).astype(jnp.float32)).astype(jnp.bfloat16)
    sent_top, low = lax.optimization_barrier((sent_top, low))
    got_top = traded(sent_top, "pos", 1)
    below = passed_along(low[:, tile_rows - edge :], "tile", 1)
    lower = low[:, : tile_rows - edge]
    lower_got = traded(lower, "pos", 2)
    top = kept_top + got_top[: 2 * edge].reshape(2, edge, width).astype(jnp.float32)
    got_probe = unfolded(got_top[2 * edge :], edge)
    probe_part = (kept_probe + got_probe.astype(jnp.float32)).astype(jnp.bfloat16)
    distance = 2
    while distance < lax.axis_size("tile"):
        probe_part = narrow_sum(probe_part, traded(probe_part, "tile", distance))
        distance *= 2
    upper = (top + below.astype(jnp.float32)).astype(jnp.bfloat16)
    folded = jnp.concatenate([probe_part[p * deep : (p + 1) * deep] for p in range(side)], 1)
    upper = jnp.concatenate([upper.reshape(2 * edge, width), folded], 0)
    lower_got, upper = lax.optimization_barrier((lower_got, upper))
    upper_got = traded(upper, "pos", 2)
    lower = narrow_sum(lower, lower_got)
    lower_theirs = traded(lower, "pos", 1)
    tile_grad = write_rows(meta, lower, lower_theirs, edge, specimen.shape)
    upper_got, tile_grad = lax.optimization_barrier((upper_got, tile_grad))
    upper = narrow_sum(upper, upper_got)
    probe_part = unfolded(upper[2 * edge :], edge)
    probe_part = narrow_sum(probe_part, traded(probe_part, "tile", 1))
    upper = upper[: 2 * edge].reshape(2, edge, width)
    upper_theirs = traded(upper, "pos", 1)
    tile_grad = write_rows(meta, upper, upper_theirs, 0, specimen.shape, tile_grad)
    probe_theirs = traded(probe_part, "pos", 1)
    probe_total = jnp.where(
        half == 0, jnp.stack([probe_part, probe_theirs]), jnp.stack([probe_theirs, probe_part])
    ).astype(jnp.float32)
    return (tile_grad, probe_total)


def solution(mesh):
    return jax.shard_map(
        body,
        mesh=mesh,
        in_specs=(
            P(),
            P(None, None, "tile", None),
            P(("tile", "pos"), None, None),
            P(("tile", "pos"), None),
            P(("tile", "pos")),
        ),
        out_specs=(P(None, None, "tile", None), P()),
        check_vma=False,
    )
```

```python
import math

import jax
import jax.numpy as jnp
import ml_dtypes
import numpy as np
from jax import lax
from jax.experimental import pallas as pl
from jax.experimental.pallas import tpu as pltpu
from jax.sharding import PartitionSpec as P

PROP_COEF = 0.5
AMP_EPS = 0.05
LANES = 128
CHUNK = 32


def fixed_tables(edge):
    index = np.arange(edge)
    angles = (np.outer(index, index) % edge) * (2.0 * math.pi / edge)
    cosine = (np.cos(angles) / math.sqrt(edge)).astype(ml_dtypes.bfloat16).astype(np.float64)
    sine = (np.sin(angles) / math.sqrt(edge)).astype(ml_dtypes.bfloat16).astype(np.float64)
    forward = cosine - 1j * sine
    centred = np.where(index < edge // 2, index, index - edge)
    ramp = np.exp(-1j * (PROP_COEF * math.pi / edge) * centred * centred)
    spread = (np.conj(forward) * ramp[None, :]) @ forward
    planes = [
        plane for matrix in (spread, forward) for plane in (matrix.real, matrix.imag, -matrix.imag)
    ]
    return jnp.asarray(np.stack(planes).astype(ml_dtypes.bfloat16))


def lay_tables(planes, tables):
    edge = planes.shape[1]
    lo, hi = pl.ds(0, edge), pl.ds(edge, edge)
    for k in range(2):
        real, imag, negated = (planes[3 * k + i] for i in range(3))
        left, right = tables[2 * k : 2 * k + 2]
        left[lo, lo], left[lo, hi], left[hi, lo], left[hi, hi] = real, negated, imag, real
        right[lo, lo], right[lo, hi], right[hi, lo], right[hi, hi] = real, imag, negated, real


def interleaved(first, second):
    marks = [(k / len(first), 0, k) for k in range(len(first))]
    marks += [((k + 0.5) / len(second), 1, k) for k in range(len(second))]
    for _, which, k in sorted(marks):
        (first, second)[which][k]()


def slot_stages(slot, alive, base_row, refs, work):
    anchor, probe, amp, tables, wide, acc, probe_acc = refs
    rolled, arriving, field, stack, joined = work
    left_a, right_a, left_f, right_f = tables
    edge = probe.shape[1]
    col_tiles = wide.shape[2]
    parts = edge // LANES
    lane = lax.broadcasted_iota(jnp.int32, (CHUNK, LANES), 1)
    row = anchor[slot, 0] - base_row
    col = anchor[slot, 1]
    first = jnp.minimum(col // LANES, col_tiles - parts - 1)
    shift = col - first * LANES
    turn = jnp.where(shift >= LANES, 0, shift)
    back = jnp.where(turn == 0, 0, LANES - turn)
    own = lane >= shift
    near = lane < LANES - shift

    def patch(part, s, i, j):
        rows = pl.ds(row + i, CHUNK)
        main = wide[part, s, first + j, rows, :]
        if j > 0:
            return main
        return jnp.where(own, main, wide[part, s, first + parts, rows, :])

    def place(part, s, i, j, value):
        rows = pl.ds(row + i, CHUNK)
        if j > 0:
            acc[part, s, first + j, rows, :] += value
        else:
            acc[part, s, first, rows, :] += jnp.where(own, value, 0.0)
            acc[part, s, first + parts, rows, :] += jnp.where(own, 0.0, value)

    def put(i, j, re, im):
        cols = pl.ds(j * LANES, LANES)
        stack[pl.ds(i, CHUNK), cols] = re.astype(jnp.bfloat16)
        stack[pl.ds(edge + i, CHUNK), cols] = im.astype(jnp.bfloat16)

    def halves():
        return [(j, pl.ds(j * LANES, LANES)) for j in range(parts)]

    def enter(i):
        rows = pl.ds(i, CHUNK)
        turned = [
            [pltpu.roll(probe[part, rows, cols], turn, 1) for j, cols in halves()]
            for part in range(2)
        ]
        for j, cols in halves():
            u_re, u_im = [
                jnp.where(own, turned[part][j], turned[part][j - 1]) for part in range(2)
            ]
            rolled[0, rows, cols] = u_re
            rolled[1, rows, cols] = u_im
            o_re, o_im = patch(0, 0, i, j), patch(1, 0, i, j)
            put(i, j, u_re * o_re - u_im * o_im, u_re * o_im + u_im * o_re)

    def second_slice(i):
        rows = pl.ds(i, CHUNK)
        for j, cols in halves():
            u_re, u_im = arriving[0, rows, cols], arriving[1, rows, cols]
            o_re, o_im = patch(0, 1, i, j), patch(1, 1, i, j)
            put(i, j, u_re * o_re - u_im * o_im, u_re * o_im + u_im * o_re)

    def residual(i):
        rows = pl.ds(i, CHUNK)
        for j, cols in halves():
            far_re, far_im = field[0, rows, cols], field[1, rows, cols]
            measured = amp[slot, rows, cols].astype(jnp.float32) * alive
            ratio = measured * lax.rsqrt(far_re * far_re + far_im * far_im + AMP_EPS)
            put(i, j, (alive - ratio) * far_re, (ratio - alive) * far_im)

    def second_grad(i):
        rows = pl.ds(i, CHUNK)
        for j, cols in halves():
            u_re, u_im = arriving[0, rows, cols], arriving[1, rows, cols]
            w_re, w_im = field[0, rows, cols], field[1, rows, cols]
            place(0, 1, i, j, u_re * w_re - u_im * w_im)
            place(1, 1, i, j, u_re * w_im + u_im * w_re)
            o_re, o_im = patch(0, 1, i, j), patch(1, 1, i, j)
            put(i, j, o_re * w_re - o_im * w_im, o_re * w_im + o_im * w_re)

    def first_grad(i):
        rows = pl.ds(i, CHUNK)
        turned = [[None] * parts for _ in range(2)]
        for j, cols in halves():
            u_re, u_im = rolled[0, rows, cols], rolled[1, rows, cols]
            w_re, w_im = field[0, rows, cols], field[1, rows, cols]
            place(0, 0, i, j, u_re * w_re - u_im * w_im)
            place(1, 0, i, j, u_re * w_im + u_im * w_re)
            o_re, o_im = patch(0, 0, i, j), patch(1, 0, i, j)
            turned[0][j] = pltpu.roll(o_re * w_re - o_im * w_im, back, 1)
            turned[1][j] = pltpu.roll(o_re * w_im + o_im * w_re, back, 1)
        for part in range(2):
            for j, cols in halves():
                after = turned[part][(j + 1) % parts]
                probe_acc[part, rows, cols] += jnp.where(near, turned[part][j], after)

    def two_sided(left, right, out):
        def rows_of(part):
            span = pl.ds(part * edge, edge)
            joined[:, span] = jnp.dot(
                left[span, :], stack[...], preferred_element_type=jnp.float32
            ).astype(jnp.bfloat16)

        def cols_of(part):
            out[part] = jnp.dot(
                joined[...],
                right[:, pl.ds(part * edge, edge)],
                preferred_element_type=jnp.float32,
            )

        return [lambda p=p: rows_of(p) for p in range(2)] + [
            lambda p=p: cols_of(p) for p in range(2)
        ]

    def each(step):
        return [lambda i=i: step(i) for i in range(0, edge, CHUNK)]

    return [
        each(enter),
        two_sided(left_a, right_a, arriving),
        each(second_slice),
        two_sided(left_f, right_f, field),
        each(residual),
        two_sided(left_f, right_f, field),
        each(second_grad),
        two_sided(left_a, right_a, field),
        each(first_grad),
    ]


def listed(order, anchor, live, base_row, edge, tile_rows, second_call):
    slots = anchor.shape[0]
    inner = [
        jnp.where((q < live) & (anchor[q, 0] - base_row + edge <= tile_rows), 1, 0)
        for q in range(slots)
    ]
    early = sum(inner) // 2 * 2
    taken = jnp.int32(0)
    rank = jnp.int32(0)
    order[0] = 0
    for q in range(slots):
        ahead = jnp.where(rank < early, inner[q], 0)
        rank = rank + inner[q]
        take = jnp.where(q < live, 1 - ahead, 0) if second_call else ahead
        order[taken] = q
        taken = taken + take
    return taken


def run_pairs(order, total, base_row, refs, work):
    def visit(step, carry):
        a = order[2 * step]
        b_lives = 2 * step + 1 < total
        b = jnp.where(b_lives, order[2 * step + 1], a)
        ones = slot_stages(a, 1.0, base_row, refs, work[0])
        twos = slot_stages(b, jnp.where(b_lives, 1.0, 0.0), base_row, refs, work[1])
        for step_now in ones[0]:
            step_now()
        for k in range(1, len(ones)):
            if k % 2:
                interleaved(ones[k], twos[k - 1])
            else:
                interleaved(twos[k - 1], ones[k])
        for step_now in twos[-1]:
            step_now()
        return carry

    lax.fori_loop(0, (total + 1) // 2, visit, 0)


def widen(wide, source, start, part, s_from, s_to):
    rows = source.shape[-2]
    for t in range(wide.shape[2]):
        wide[part, s_to, t, pl.ds(start, rows), :] = source[
            part, s_from, :, pl.ds(t * LANES, LANES)
        ].astype(jnp.float32)


def fetch(copies, sems):
    started = {}
    for k, (group, source, target) in enumerate(copies):
        copy = pltpu.make_async_copy(source, target, sems.at[k])
        copy.start()
        started.setdefault(group, []).append(copy)

    def wait(group):
        for copy in started[group]:
            copy.wait()

    return wait


def early_kernel(
    meta,
    anchor,
    probe_any,
    spec_any,
    amp_any,
    planes_any,
    acc,
    probe_acc,
    order,
    sems,
    probe,
    spec,
    amp,
    planes,
    la,
    ra,
    lf,
    rf,
    wide,
    *work,
):
    wait = fetch(
        [
            ("spec", spec_any, spec),
            ("planes", planes_any, planes),
            ("rest", probe_any, probe),
            ("rest", amp_any, amp),
        ],
        sems,
    )
    tables = (la, ra, lf, rf)
    slices, tile_rows = spec.shape[1:3]
    for part in range(2):
        for s in range(slices):
            for t in range(wide.shape[2]):
                acc[part, s, t] = jnp.zeros(acc.shape[3:], jnp.float32)
    probe_acc[...] = jnp.zeros(probe_acc.shape, jnp.float32)
    total = listed(order, anchor, meta[0], meta[1], probe.shape[1], tile_rows, False)
    wait("spec")
    for part in range(2):
        for s in range(slices):
            widen(wide, spec, 0, part, s, s)
    wait("planes")
    lay_tables(planes, tables)
    wait("rest")
    refs = (anchor, probe, amp, tables, wide, acc, probe_acc)
    run_pairs(order, total, meta[1], refs, (work[:5], work[5:]))


def late_kernel(
    meta,
    anchor,
    probe_any,
    spec_any,
    rim_own_any,
    rim_other_any,
    acc_any,
    probe_acc_any,
    amp_any,
    planes_any,
    send_low,
    send_top,
    keep_low,
    keep_top,
    keep_probe,
    order,
    sems,
    probe,
    spec,
    amp,
    planes,
    la,
    ra,
    lf,
    rf,
    wide,
    rim_own,
    rim_other,
    acc,
    probe_acc,
    *work,
):
    slices, tile_rows, width = spec.shape[1:]
    edge = probe.shape[1]
    wait = fetch(
        [
            ("spec", spec_any, spec),
            ("planes", planes_any, planes),
            ("rim", rim_own_any, rim_own),
            ("rim", rim_other_any, rim_other),
            ("acc", acc_any, acc.at[:, :, :, pl.ds(0, tile_rows), :]),
            ("acc", probe_acc_any, probe_acc),
            ("rest", probe_any, probe),
            ("rest", amp_any, amp),
        ],
        sems,
    )
    tables = (la, ra, lf, rf)
    half = meta[2]
    other = 1 - half
    col_tiles = width // LANES
    for part in range(2):
        for s in range(slices):
            for t in range(col_tiles):
                acc[part, s, t, pl.ds(tile_rows, edge), :] = jnp.zeros((edge, LANES), jnp.float32)
    total = listed(order, anchor, meta[0], meta[1], edge, tile_rows, True)
    wait("spec")
    for part in range(2):
        for s in range(slices):
            widen(wide, spec, 0, part, s, s)
    wait("planes")
    lay_tables(planes, tables)
    wait("rim")
    for part in range(2):
        widen(wide, rim_own, tile_rows, part, 0, half)
        widen(wide, rim_other, tile_rows, part, 0, other)
    wait("acc")
    wait("rest")
    refs = (anchor, probe, amp, tables, wide, acc, probe_acc)
    run_pairs(order, total, meta[1], refs, (work[:5], work[5:]))

    low = pl.ds(edge, tile_rows)
    top = pl.ds(0, edge)
    for part in range(2):
        sign = 1.0 if part == 0 else -1.0
        for t in range(col_tiles):
            cols = pl.ds(t * LANES, LANES)
            send_low[pl.ds(part * tile_rows, tile_rows), cols] = (
                sign * acc[part, other, t, low, :]
            ).astype(jnp.bfloat16)
            keep_low[part, :, cols] = sign * acc[part, half, t, low, :]
            send_top[part, :, cols] = (sign * acc[part, other, t, top, :]).astype(jnp.bfloat16)
            keep_top[part, :, cols] = sign * acc[part, half, t, top, :]
    deep = keep_probe.shape[0]
    flip = jnp.where(other == 1, -1.0, 1.0)
    for piece in range(width // edge):
        rows, cols = pl.ds(piece * deep, deep), pl.ds(piece * edge, edge)
        send_low[pl.ds(2 * tile_rows, deep), cols] = (flip * probe_acc[other, rows, :]).astype(
            jnp.bfloat16
        )
        keep_probe[:, cols] = -flip * probe_acc[half, rows, :]


VMEM = pl.BlockSpec(memory_space=pltpu.VMEM)
SMEM = pl.BlockSpec(memory_space=pltpu.SMEM)
ANY = pl.BlockSpec(memory_space=pl.ANY)


def scratch(slots, slices, width, tile_rows, rows, edge, copies):
    planes = pltpu.VMEM((2, edge, edge), jnp.float32)
    table = pltpu.VMEM((2 * edge, 2 * edge), jnp.bfloat16)
    stack = pltpu.VMEM((2 * edge, edge), jnp.bfloat16)
    joined = pltpu.VMEM((edge, 2 * edge), jnp.bfloat16)
    lead = [
        pltpu.SMEM((slots + 1,), jnp.int32),
        pltpu.SemaphoreType.DMA((copies,)),
        planes,
        pltpu.VMEM((2, slices, tile_rows, width), jnp.bfloat16),
        pltpu.VMEM((slots, edge, edge), jnp.bfloat16),
        pltpu.VMEM((6, edge, edge), jnp.bfloat16),
        table,
        table,
        table,
        table,
        pltpu.VMEM((2, slices, width // LANES, rows, LANES), jnp.float32),
    ]
    return lead, [planes, planes, planes, stack, joined] * 2


def run_early(meta, anchor, probe, spec, amp, planes):
    edge = probe.shape[1]
    _, slices, tile_rows, width = spec.shape
    lead, work = scratch(anchor.shape[0], slices, width, tile_rows, tile_rows, edge, 4)
    return pl.pallas_call(
        early_kernel,
        out_shape=(
            jax.ShapeDtypeStruct((2, slices, width // LANES, tile_rows, LANES), jnp.float32),
            jax.ShapeDtypeStruct((2, edge, edge), jnp.float32),
        ),
        in_specs=[SMEM, SMEM] + [ANY] * 4,
        out_specs=(VMEM, VMEM),
        scratch_shapes=lead + work,
        compiler_params=pltpu.CompilerParams(vmem_limit_bytes=32 * 1024 * 1024),
        name="early_slots",
    )(meta, anchor, probe, spec, amp, planes)


def run_late(meta, anchor, probe, spec, rim_own, rim_other, acc, probe_acc, amp, planes):
    edge = probe.shape[1]
    _, slices, tile_rows, width = spec.shape
    total = tile_rows + edge
    deep = edge * edge // width
    lead, work = scratch(anchor.shape[0], slices, width, tile_rows, total, edge, 8)
    rim = pltpu.VMEM((2, 1, edge, width), jnp.bfloat16)
    return pl.pallas_call(
        late_kernel,
        out_shape=(
            jax.ShapeDtypeStruct((2 * tile_rows + deep, width), jnp.bfloat16),
            jax.ShapeDtypeStruct((2, edge, width), jnp.bfloat16),
            jax.ShapeDtypeStruct((2, tile_rows, width), jnp.float32),
            jax.ShapeDtypeStruct((2, edge, width), jnp.float32),
            jax.ShapeDtypeStruct((deep, width), jnp.float32),
        ),
        in_specs=[SMEM, SMEM] + [ANY] * 8,
        out_specs=(VMEM,) * 5,
        scratch_shapes=lead
        + [
            rim,
            rim,
            pltpu.VMEM((2, slices, width // LANES, total, LANES), jnp.float32),
            pltpu.VMEM((2, edge, edge), jnp.float32),
        ]
        + work,
        compiler_params=pltpu.CompilerParams(vmem_limit_bytes=36 * 1024 * 1024),
        name="late_slots",
    )(meta, anchor, probe, spec, rim_own, rim_other, acc, probe_acc, amp, planes)


def write_rows(meta, own, theirs, start, shape, base=None):
    slices, rows, width = shape[1], own.shape[1], own.shape[2]

    def kernel(meta, own, theirs, *rest):
        out, wide, sems = rest[-3:]
        half = meta[2]
        wide[half] = own[...].astype(jnp.float32)
        wide[1 - half] = theirs[...].astype(jnp.float32)
        copies = [
            pltpu.make_async_copy(
                wide.at[s, part], out.at[part, s, pl.ds(start, rows), :], sems.at[2 * s + part]
            )
            for s in range(slices)
            for part in range(2)
        ]
        for copy in copies:
            copy.start()
        for copy in copies:
            copy.wait()

    extra = [] if base is None else [base]
    return pl.pallas_call(
        kernel,
        out_shape=jax.ShapeDtypeStruct(shape, jnp.float32),
        in_specs=[SMEM, VMEM, VMEM] + [ANY] * len(extra),
        out_specs=ANY,
        input_output_aliases={} if base is None else {3: 0},
        scratch_shapes=[
            pltpu.VMEM((slices, 2, rows, width), jnp.float32),
            pltpu.SemaphoreType.DMA((2 * slices,)),
        ],
        compiler_params=pltpu.CompilerParams(vmem_limit_bytes=16 * 1024 * 1024),
        name="write_rows",
    )(meta, own, theirs, *extra)


def traded(value, axis, distance):
    count = lax.axis_size(axis)
    return lax.ppermute(value, axis, [(i, i ^ distance) for i in range(count)])


def passed_along(value, axis, steps):
    count = lax.axis_size(axis)
    initial, last = (max(0, -steps), min(count, count - steps))
    return lax.ppermute(value, axis, [(source, source + steps) for source in range(initial, last)])


def narrow_sum(own, got):
    return (own.astype(jnp.float32) + got.astype(jnp.float32)).astype(jnp.bfloat16)


def unfolded(value, edge):
    return jnp.concatenate([value[:, k : k + edge] for k in range(0, value.shape[1], edge)], 0)


def body(probe_field, specimen, amplitude, scan_anchor, counts):
    edge = probe_field.shape[1]
    _, slices, tile_rows, width = specimen.shape
    half = lax.axis_index("pos") % 2
    base_row = lax.axis_index("tile") * tile_rows
    meta = jnp.stack([counts[0], base_row, half]).astype(jnp.int32)
    planes = fixed_tables(edge)
    rim_own = passed_along(
        lax.dynamic_slice(specimen, (0, half, 0, 0), (2, 1, edge, width)), "tile", -1
    )
    acc, probe_acc = run_early(meta, scan_anchor, probe_field, specimen, amplitude, planes)
    rim_own, probe_acc = lax.optimization_barrier((rim_own, probe_acc))
    rim_other = traded(rim_own, "pos", 1)
    sent_low, sent_top, kept_low, kept_top, kept_probe = run_late(
        meta,
        scan_anchor,
        probe_field,
        specimen,
        rim_own,
        rim_other,
        acc,
        probe_acc,
        amplitude,
        planes,
    )
    got_low = traded(sent_low, "pos", 1)
    got_top = traded(sent_top, "pos", 1)
    low = kept_low + got_low[: 2 * tile_rows].reshape(kept_low.shape).astype(jnp.float32)
    low = low.astype(jnp.bfloat16)
    probe_part = (kept_probe + got_low[2 * tile_rows :].astype(jnp.float32)).astype(jnp.bfloat16)
    below = passed_along(low[:, tile_rows - edge :], "tile", 1)
    mid_rows = 2 * (tile_rows - edge)
    mid = jnp.concatenate([low[:, : tile_rows - edge].reshape(mid_rows, width), probe_part], 0)
    mid = narrow_sum(mid, traded(mid, "pos", 2))
    top = kept_top + got_top.astype(jnp.float32)
    upper = (top + below.astype(jnp.float32)).astype(jnp.bfloat16)
    mid, upper = lax.optimization_barrier((mid, upper))
    upper_got = traded(upper, "pos", 2)
    probe_part = mid[mid_rows:]
    distance = lax.axis_size("tile")
    while distance > 2:
        distance //= 2
        probe_part = narrow_sum(probe_part, traded(probe_part, "tile", distance))
    lower = mid[:mid_rows].reshape(2, tile_rows - edge, width)
    tile_grad = write_rows(meta, lower, traded(lower, "pos", 1), edge, specimen.shape)
    upper_got, tile_grad, probe_part = lax.optimization_barrier(
        (upper_got, tile_grad, probe_part)
    )
    probe_part = narrow_sum(probe_part, traded(probe_part, "tile", 1))
    upper = narrow_sum(upper, upper_got)
    tile_grad = write_rows(meta, upper, traded(upper, "pos", 1), 0, specimen.shape, tile_grad)
    probe_own, probe_theirs = [
        unfolded(value, edge) for value in (probe_part, traded(probe_part, "pos", 1))
    ]
    probe_total = jnp.where(
        half == 0, jnp.stack([probe_own, probe_theirs]), jnp.stack([probe_theirs, probe_own])
    ).astype(jnp.float32)
    return (tile_grad, probe_total)


def solution(mesh):
    return jax.shard_map(
        body,
        mesh=mesh,
        in_specs=(
            P(),
            P(None, None, "tile", None),
            P(("tile", "pos"), None, None),
            P(("tile", "pos"), None),
            P(("tile", "pos")),
        ),
        out_specs=(P(None, None, "tile", None), P()),
        check_vma=False,
    )
```

```python
import math

import jax
import jax.numpy as jnp
import ml_dtypes
import numpy as np
from jax import lax
from jax.experimental import pallas as pl
from jax.experimental.pallas import tpu as pltpu
from jax.sharding import PartitionSpec as P

PROP_COEF = 0.5
AMP_EPS = 0.05
LANES = 128
CHUNK = 32
EARLY_PAIRS = 2
SHARDS = 4


def fixed_tables(edge):
    index = np.arange(edge)
    angles = (np.outer(index, index) % edge) * (2.0 * math.pi / edge)
    cosine = (np.cos(angles) / math.sqrt(edge)).astype(ml_dtypes.bfloat16).astype(np.float64)
    sine = (np.sin(angles) / math.sqrt(edge)).astype(ml_dtypes.bfloat16).astype(np.float64)
    forward = cosine - 1j * sine
    centred = np.where(index < edge // 2, index, index - edge)
    ramp = np.exp(-1j * (PROP_COEF * math.pi / edge) * centred * centred)
    spread = (np.conj(forward) * ramp[None, :]) @ forward
    planes = [
        plane for matrix in (spread, forward) for plane in (matrix.real, matrix.imag, -matrix.imag)
    ]
    return jnp.asarray(np.stack(planes).astype(ml_dtypes.bfloat16))


def lay_tables(planes, tables):
    edge = planes.shape[1]
    lo, hi = pl.ds(0, edge), pl.ds(edge, edge)
    for k in range(2):
        real, imag, negated = (planes[3 * k + i] for i in range(3))
        left, right = tables[2 * k : 2 * k + 2]
        left[lo, lo], left[lo, hi], left[hi, lo], left[hi, hi] = real, negated, imag, real
        right[lo, lo], right[lo, hi], right[hi, lo], right[hi, hi] = real, imag, negated, real


def interleaved(first, second):
    marks = [(k / len(first), 0, k) for k in range(len(first))]
    marks += [((k + 0.5) / len(second), 1, k) for k in range(len(second))]
    for _, which, k in sorted(marks):
        (first, second)[which][k]()


def slot_stages(slot, alive, base_row, refs, work):
    anchor, probe, amp, tables, wide, acc, probe_acc = refs
    rolled, arriving, field, stack, joined = work
    left_a, right_a, left_f, right_f = tables
    edge = probe.shape[1]
    col_tiles = wide.shape[2]
    parts = edge // LANES
    lane = lax.broadcasted_iota(jnp.int32, (CHUNK, LANES), 1)
    row = anchor[slot, 0] - base_row
    col = anchor[slot, 1]
    first = jnp.minimum(col // LANES, col_tiles - parts - 1)
    shift = col - first * LANES
    turn = jnp.where(shift >= LANES, 0, shift)
    back = jnp.where(turn == 0, 0, LANES - turn)
    own = lane >= shift
    near = lane < LANES - shift

    def patch(part, s, i, j):
        rows = pl.ds(row + i, CHUNK)
        main = wide[part, s, first + j, rows, :]
        if j > 0:
            return main
        return jnp.where(own, main, wide[part, s, first + parts, rows, :])

    def place(part, s, i, j, value):
        rows = pl.ds(row + i, CHUNK)
        if j > 0:
            acc[part, s, first + j, rows, :] += value
        else:
            acc[part, s, first, rows, :] += jnp.where(own, value, 0.0)
            acc[part, s, first + parts, rows, :] += jnp.where(own, 0.0, value)

    def put(i, j, re, im):
        cols = pl.ds(j * LANES, LANES)
        stack[pl.ds(i, CHUNK), cols] = re.astype(jnp.bfloat16)
        stack[pl.ds(edge + i, CHUNK), cols] = im.astype(jnp.bfloat16)

    def halves():
        return [(j, pl.ds(j * LANES, LANES)) for j in range(parts)]

    def enter(i):
        rows = pl.ds(i, CHUNK)
        turned = [
            [pltpu.roll(probe[part, rows, cols], turn, 1) for j, cols in halves()]
            for part in range(2)
        ]
        for j, cols in halves():
            u_re, u_im = [
                jnp.where(own, turned[part][j], turned[part][j - 1]) for part in range(2)
            ]
            rolled[0, rows, cols] = u_re
            rolled[1, rows, cols] = u_im
            o_re, o_im = patch(0, 0, i, j), patch(1, 0, i, j)
            put(i, j, u_re * o_re - u_im * o_im, u_re * o_im + u_im * o_re)

    def second_slice(i):
        rows = pl.ds(i, CHUNK)
        for j, cols in halves():
            u_re, u_im = arriving[0, rows, cols], arriving[1, rows, cols]
            o_re, o_im = patch(0, 1, i, j), patch(1, 1, i, j)
            put(i, j, u_re * o_re - u_im * o_im, u_re * o_im + u_im * o_re)

    def residual(i):
        rows = pl.ds(i, CHUNK)
        for j, cols in halves():
            far_re, far_im = field[0, rows, cols], field[1, rows, cols]
            measured = amp[slot, rows, cols].astype(jnp.float32) * alive
            ratio = measured * lax.rsqrt(far_re * far_re + far_im * far_im + AMP_EPS)
            put(i, j, (alive - ratio) * far_re, (ratio - alive) * far_im)

    def second_grad(i):
        rows = pl.ds(i, CHUNK)
        for j, cols in halves():
            u_re, u_im = arriving[0, rows, cols], arriving[1, rows, cols]
            w_re, w_im = field[0, rows, cols], field[1, rows, cols]
            place(0, 1, i, j, u_re * w_re - u_im * w_im)
            place(1, 1, i, j, u_re * w_im + u_im * w_re)
            o_re, o_im = patch(0, 1, i, j), patch(1, 1, i, j)
            put(i, j, o_re * w_re - o_im * w_im, o_re * w_im + o_im * w_re)

    def first_grad(i):
        rows = pl.ds(i, CHUNK)
        turned = [[None] * parts for _ in range(2)]
        for j, cols in halves():
            u_re, u_im = rolled[0, rows, cols], rolled[1, rows, cols]
            w_re, w_im = field[0, rows, cols], field[1, rows, cols]
            place(0, 0, i, j, u_re * w_re - u_im * w_im)
            place(1, 0, i, j, u_re * w_im + u_im * w_re)
            o_re, o_im = patch(0, 0, i, j), patch(1, 0, i, j)
            turned[0][j] = pltpu.roll(o_re * w_re - o_im * w_im, back, 1)
            turned[1][j] = pltpu.roll(o_re * w_im + o_im * w_re, back, 1)
        for part in range(2):
            for j, cols in halves():
                after = turned[part][(j + 1) % parts]
                probe_acc[part, rows, cols] += jnp.where(near, turned[part][j], after)

    def two_sided(left, right, out):
        def rows_of(part):
            span = pl.ds(part * edge, edge)
            joined[:, span] = jnp.dot(
                left[span, :], stack[...], preferred_element_type=jnp.float32
            ).astype(jnp.bfloat16)

        def cols_of(part):
            out[part] = jnp.dot(
                joined[...],
                right[:, pl.ds(part * edge, edge)],
                preferred_element_type=jnp.float32,
            )

        return [lambda p=p: rows_of(p) for p in range(2)] + [
            lambda p=p: cols_of(p) for p in range(2)
        ]

    def each(step):
        return [lambda i=i: step(i) for i in range(0, edge, CHUNK)]

    return [
        each(enter),
        two_sided(left_a, right_a, arriving),
        each(second_slice),
        two_sided(left_f, right_f, field),
        each(residual),
        two_sided(left_f, right_f, field),
        each(second_grad),
        two_sided(left_a, right_a, field),
        each(first_grad),
    ]


def listed(order, anchor, live, base_row, edge, tile_rows, second_call):
    slots = anchor.shape[0]
    inner = [
        jnp.where((q < live) & (anchor[q, 0] - base_row + edge <= tile_rows), 1, 0)
        for q in range(slots)
    ]
    early = jnp.minimum(sum(inner) // 2, EARLY_PAIRS) * 2
    taken = jnp.int32(0)
    rank = jnp.int32(0)
    order[0] = 0
    for q in range(slots):
        ahead = jnp.where(rank < early, inner[q], 0)
        rank = rank + inner[q]
        take = jnp.where(q < live, 1 - ahead, 0) if second_call else ahead
        order[taken] = q
        taken = taken + take
    return taken


def run_pairs(order, total, base_row, refs, work):
    def visit(step, carry):
        a = order[2 * step]
        b_lives = 2 * step + 1 < total
        b = jnp.where(b_lives, order[2 * step + 1], a)
        ones = slot_stages(a, 1.0, base_row, refs, work[0])
        twos = slot_stages(b, jnp.where(b_lives, 1.0, 0.0), base_row, refs, work[1])
        for step_now in ones[0]:
            step_now()
        for k in range(1, len(ones)):
            if k % 2:
                interleaved(ones[k], twos[k - 1])
            else:
                interleaved(twos[k - 1], ones[k])
        for step_now in twos[-1]:
            step_now()
        return carry

    lax.fori_loop(0, (total + 1) // 2, visit, 0)


def widen(wide, source, start, part, s_from, s_to):
    rows = source.shape[-2]
    for t in range(wide.shape[2]):
        wide[part, s_to, t, pl.ds(start, rows), :] = source[
            part, s_from, :, pl.ds(t * LANES, LANES)
        ].astype(jnp.float32)


def fetch(copies, sems):
    started = {}
    for k, (group, source, target) in enumerate(copies):
        copy = pltpu.make_async_copy(source, target, sems.at[k])
        copy.start()
        started.setdefault(group, []).append(copy)

    def wait(group):
        for copy in started[group]:
            copy.wait()

    return wait


def early_kernel(
    meta,
    anchor,
    probe_any,
    spec_any,
    amp_any,
    planes_any,
    acc,
    probe_acc,
    order,
    sems,
    probe,
    spec,
    amp,
    planes,
    la,
    ra,
    lf,
    rf,
    wide,
    *work,
):
    wait = fetch(
        [
            ("spec", spec_any, spec),
            ("planes", planes_any, planes),
            ("rest", probe_any, probe),
            ("rest", amp_any, amp),
        ],
        sems,
    )
    tables = (la, ra, lf, rf)
    slices, tile_rows = spec.shape[1:3]
    for part in range(2):
        for s in range(slices):
            for t in range(wide.shape[2]):
                acc[part, s, t] = jnp.zeros(acc.shape[3:], jnp.float32)
    probe_acc[...] = jnp.zeros(probe_acc.shape, jnp.float32)
    total = listed(order, anchor, meta[0], meta[1], probe.shape[1], tile_rows, False)
    wait("spec")
    for part in range(2):
        for s in range(slices):
            widen(wide, spec, 0, part, s, s)
    wait("planes")
    lay_tables(planes, tables)
    wait("rest")
    refs = (anchor, probe, amp, tables, wide, acc, probe_acc)
    run_pairs(order, total, meta[1], refs, (work[:5], work[5:]))


def late_kernel(
    meta,
    anchor,
    probe_any,
    spec_any,
    rim_own_any,
    rim_other_any,
    acc_any,
    probe_acc_any,
    amp_any,
    planes_any,
    send_low,
    send_top,
    keep_low,
    keep_top,
    keep_probe,
    order,
    sems,
    probe,
    spec,
    amp,
    planes,
    la,
    ra,
    lf,
    rf,
    wide,
    rim_own,
    rim_other,
    acc,
    probe_acc,
    *work,
):
    slices, tile_rows, width = spec.shape[1:]
    edge = probe.shape[1]
    wait = fetch(
        [
            ("spec", spec_any, spec),
            ("planes", planes_any, planes),
            ("rim", rim_own_any, rim_own),
            ("rim", rim_other_any, rim_other),
            ("acc", acc_any, acc.at[:, :, :, pl.ds(0, tile_rows), :]),
            ("acc", probe_acc_any, probe_acc),
            ("rest", probe_any, probe),
            ("rest", amp_any, amp),
        ],
        sems,
    )
    tables = (la, ra, lf, rf)
    half = meta[2]
    other = 1 - half
    col_tiles = width // LANES
    for part in range(2):
        for s in range(slices):
            for t in range(col_tiles):
                acc[part, s, t, pl.ds(tile_rows, edge), :] = jnp.zeros((edge, LANES), jnp.float32)
    total = listed(order, anchor, meta[0], meta[1], edge, tile_rows, True)
    wait("spec")
    for part in range(2):
        for s in range(slices):
            widen(wide, spec, 0, part, s, s)
    wait("planes")
    lay_tables(planes, tables)
    wait("rim")
    for part in range(2):
        widen(wide, rim_own, tile_rows, part, 0, half)
        widen(wide, rim_other, tile_rows, part, 0, other)
    wait("acc")
    wait("rest")
    refs = (anchor, probe, amp, tables, wide, acc, probe_acc)
    run_pairs(order, total, meta[1], refs, (work[:5], work[5:]))

    low = pl.ds(edge, tile_rows)
    top = pl.ds(0, edge)
    for part in range(2):
        sign = 1.0 if part == 0 else -1.0
        for t in range(col_tiles):
            cols = pl.ds(t * LANES, LANES)
            send_low[pl.ds(part * tile_rows, tile_rows), cols] = (
                sign * acc[part, other, t, low, :]
            ).astype(jnp.bfloat16)
            keep_low[part, :, cols] = sign * acc[part, half, t, low, :]
            send_top[part, :, cols] = (sign * acc[part, other, t, top, :]).astype(jnp.bfloat16)
            keep_top[part, :, cols] = sign * acc[part, half, t, top, :]
    deep = keep_probe.shape[0]
    flip = jnp.where(other == 1, -1.0, 1.0)
    for piece in range(width // edge):
        rows, cols = pl.ds(piece * deep, deep), pl.ds(piece * edge, edge)
        send_low[pl.ds(2 * tile_rows, deep), cols] = (flip * probe_acc[other, rows, :]).astype(
            jnp.bfloat16
        )
        keep_probe[:, cols] = -flip * probe_acc[half, rows, :]


VMEM = pl.BlockSpec(memory_space=pltpu.VMEM)
SMEM = pl.BlockSpec(memory_space=pltpu.SMEM)
ANY = pl.BlockSpec(memory_space=pl.ANY)


def scratch(slots, slices, width, tile_rows, rows, edge, copies):
    planes = pltpu.VMEM((2, edge, edge), jnp.float32)
    table = pltpu.VMEM((2 * edge, 2 * edge), jnp.bfloat16)
    stack = pltpu.VMEM((2 * edge, edge), jnp.bfloat16)
    joined = pltpu.VMEM((edge, 2 * edge), jnp.bfloat16)
    lead = [
        pltpu.SMEM((slots + 1,), jnp.int32),
        pltpu.SemaphoreType.DMA((copies,)),
        planes,
        pltpu.VMEM((2, slices, tile_rows, width), jnp.bfloat16),
        pltpu.VMEM((slots, edge, edge), jnp.bfloat16),
        pltpu.VMEM((6, edge, edge), jnp.bfloat16),
        table,
        table,
        table,
        table,
        pltpu.VMEM((2, slices, width // LANES, rows, LANES), jnp.float32),
    ]
    return lead, [planes, planes, planes, stack, joined] * 2


def run_early(meta, anchor, probe, spec, amp, planes):
    edge = probe.shape[1]
    _, slices, tile_rows, width = spec.shape
    lead, work = scratch(anchor.shape[0], slices, width, tile_rows, tile_rows, edge, 4)
    return pl.pallas_call(
        early_kernel,
        out_shape=(
            jax.ShapeDtypeStruct((2, slices, width // LANES, tile_rows, LANES), jnp.float32),
            jax.ShapeDtypeStruct((2, edge, edge), jnp.float32),
        ),
        in_specs=[SMEM, SMEM] + [ANY] * 4,
        out_specs=(VMEM, VMEM),
        scratch_shapes=lead + work,
        compiler_params=pltpu.CompilerParams(vmem_limit_bytes=32 * 1024 * 1024),
        name="early_slots",
    )(meta, anchor, probe, spec, amp, planes)


def run_late(meta, anchor, probe, spec, rim_own, rim_other, acc, probe_acc, amp, planes):
    edge = probe.shape[1]
    _, slices, tile_rows, width = spec.shape
    total = tile_rows + edge
    deep = edge * edge // width
    lead, work = scratch(anchor.shape[0], slices, width, tile_rows, total, edge, 8)
    rim = pltpu.VMEM((2, 1, edge, width), jnp.bfloat16)
    return pl.pallas_call(
        late_kernel,
        out_shape=(
            jax.ShapeDtypeStruct((2 * tile_rows + deep, width), jnp.bfloat16),
            jax.ShapeDtypeStruct((2, edge, width), jnp.bfloat16),
            jax.ShapeDtypeStruct((2, tile_rows, width), jnp.float32),
            jax.ShapeDtypeStruct((2, edge, width), jnp.float32),
            jax.ShapeDtypeStruct((deep, width), jnp.float32),
        ),
        in_specs=[SMEM, SMEM] + [ANY] * 8,
        out_specs=(VMEM,) * 5,
        scratch_shapes=lead
        + [
            rim,
            rim,
            pltpu.VMEM((2, slices, width // LANES, total, LANES), jnp.float32),
            pltpu.VMEM((2, edge, edge), jnp.float32),
        ]
        + work,
        compiler_params=pltpu.CompilerParams(vmem_limit_bytes=36 * 1024 * 1024),
        name="late_slots",
    )(meta, anchor, probe, spec, rim_own, rim_other, acc, probe_acc, amp, planes)


def write_rows(meta, own, theirs, start, shape, base=None):
    slices, rows, width = shape[1], own.shape[1], own.shape[2]

    def kernel(meta, own, theirs, *rest):
        out, wide, sems = rest[-3:]
        half = meta[2]
        wide[half] = own[...].astype(jnp.float32)
        wide[1 - half] = theirs[...].astype(jnp.float32)
        copies = [
            pltpu.make_async_copy(
                wide.at[s, part], out.at[part, s, pl.ds(start, rows), :], sems.at[2 * s + part]
            )
            for s in range(slices)
            for part in range(2)
        ]
        for copy in copies:
            copy.start()
        for copy in copies:
            copy.wait()

    extra = [] if base is None else [base]
    return pl.pallas_call(
        kernel,
        out_shape=jax.ShapeDtypeStruct(shape, jnp.float32),
        in_specs=[SMEM, VMEM, VMEM] + [ANY] * len(extra),
        out_specs=ANY,
        input_output_aliases={} if base is None else {3: 0},
        scratch_shapes=[
            pltpu.VMEM((slices, 2, rows, width), jnp.float32),
            pltpu.SemaphoreType.DMA((2 * slices,)),
        ],
        compiler_params=pltpu.CompilerParams(vmem_limit_bytes=16 * 1024 * 1024),
        cost_estimate=pl.CostEstimate(
            flops=0, bytes_accessed=2 * slices * rows * width * 6, transcendentals=0
        ),
        name="write_rows",
    )(meta, own, theirs, *extra)


def traded(value, axis, distance):
    count = lax.axis_size(axis)
    return lax.ppermute(value, axis, [(i, i ^ distance) for i in range(count)])


def passed_along(value, axis, steps):
    count = lax.axis_size(axis)
    initial, last = (max(0, -steps), min(count, count - steps))
    return lax.ppermute(value, axis, [(source, source + steps) for source in range(initial, last)])


def narrow_sum(own, got):
    return (own.astype(jnp.float32) + got.astype(jnp.float32)).astype(jnp.bfloat16)


def unfolded(value, edge):
    return jnp.concatenate([value[:, k : k + edge] for k in range(0, value.shape[1], edge)], 0)


def split_probe(place, whole, first, group):
    width = whole.shape[1]
    rows = (whole.shape[0] - first) // group

    def kernel(place, whole, *shares):
        for d, share in enumerate(shares):
            start = pl.multiple_of(first + (place[0] ^ d) * rows, rows)
            share[...] = whole[pl.ds(start, rows), :]

    return pl.pallas_call(
        kernel,
        out_shape=(jax.ShapeDtypeStruct((rows, width), jnp.bfloat16),) * group,
        in_specs=[SMEM, VMEM],
        out_specs=(VMEM,) * group,
        compiler_params=pltpu.CompilerParams(vmem_limit_bytes=8 * 1024 * 1024),
        name="split_probe",
    )(place, whole)


def join_probe(place, shares):
    rows, width = shares[0].shape

    def kernel(place, *rest):
        out = rest[-1]
        for d, share in enumerate(rest[:-1]):
            out[pl.ds(pl.multiple_of((place[0] ^ d) * rows, rows), rows), :] = share[...]

    return pl.pallas_call(
        kernel,
        out_shape=jax.ShapeDtypeStruct((rows * len(shares), width), jnp.bfloat16),
        in_specs=[SMEM] + [VMEM] * len(shares),
        out_specs=VMEM,
        compiler_params=pltpu.CompilerParams(vmem_limit_bytes=8 * 1024 * 1024),
        name="join_probe",
    )(place, *shares)


def body(probe_field, specimen, amplitude, scan_anchor, counts):
    edge = probe_field.shape[1]
    _, slices, tile_rows, width = specimen.shape
    half = lax.axis_index("pos") % 2
    base_row = lax.axis_index("tile") * tile_rows
    meta = jnp.stack([counts[0], base_row, half]).astype(jnp.int32)
    planes = fixed_tables(edge)
    rim_own = passed_along(
        lax.dynamic_slice(specimen, (0, half, 0, 0), (2, 1, edge, width)), "tile", -1
    )
    acc, probe_acc = run_early(meta, scan_anchor, probe_field, specimen, amplitude, planes)
    rim_own, probe_acc = lax.optimization_barrier((rim_own, probe_acc))
    rim_other = traded(rim_own, "pos", 1)
    sent_low, sent_top, kept_low, kept_top, kept_probe = run_late(
        meta,
        scan_anchor,
        probe_field,
        specimen,
        rim_own,
        rim_other,
        acc,
        probe_acc,
        amplitude,
        planes,
    )
    got_low = traded(sent_low, "pos", 1)
    got_top = traded(sent_top, "pos", 1)
    low = kept_low + got_low[: 2 * tile_rows].reshape(kept_low.shape).astype(jnp.float32)
    low = low.astype(jnp.bfloat16)
    probe_part = (kept_probe + got_low[2 * tile_rows :].astype(jnp.float32)).astype(jnp.bfloat16)
    mid_rows = 2 * (tile_rows - edge)
    mid = jnp.concatenate([low[:, : tile_rows - edge].reshape(mid_rows, width), probe_part], 0)
    mid = narrow_sum(mid, traded(mid, "pos", 2))
    below = passed_along(low[:, tile_rows - edge :], "tile", 1)
    mid, below = lax.optimization_barrier((mid, below))
    top = kept_top + got_top.astype(jnp.float32)
    upper = (top + below.astype(jnp.float32)).astype(jnp.bfloat16)
    mid, upper = lax.optimization_barrier((mid, upper))
    upper_got = traded(upper, "pos", 2)
    tiles = lax.axis_size("tile")
    group = min(tiles // 2, SHARDS)
    place = (lax.axis_index("tile") // 2 % group).astype(jnp.int32).reshape(1)
    share, *others = split_probe(place, mid, mid_rows, group)
    share = share.astype(jnp.float32)
    for d, other in enumerate(others, 1):
        share = share + traded(other, "tile", 2 * d).astype(jnp.float32)
    share = share.astype(jnp.bfloat16)
    distance = 2 * group
    while distance < tiles:
        share = narrow_sum(share, traded(share, "tile", distance))
        distance *= 2
    share = narrow_sum(share, traded(share, "tile", 1))
    lower = mid[:mid_rows].reshape(2, tile_rows - edge, width)
    tile_grad = write_rows(meta, lower, traded(lower, "pos", 1), edge, specimen.shape)
    upper_got, tile_grad, share = lax.optimization_barrier((upper_got, tile_grad, share))
    upper = narrow_sum(upper, upper_got)
    tile_grad = write_rows(meta, upper, traded(upper, "pos", 1), 0, specimen.shape, tile_grad)
    probe_part = join_probe(
        place, [share] + [traded(share, "tile", 2 * d) for d in range(1, group)]
    )
    probe_theirs, tile_grad = lax.optimization_barrier((traded(probe_part, "pos", 1), tile_grad))
    probe_own, probe_theirs = [unfolded(value, edge) for value in (probe_part, probe_theirs)]
    probe_total = jnp.where(
        half == 0, jnp.stack([probe_own, probe_theirs]), jnp.stack([probe_theirs, probe_own])
    ).astype(jnp.float32)
    return (tile_grad, probe_total)


def solution(mesh):
    return jax.shard_map(
        body,
        mesh=mesh,
        in_specs=(
            P(),
            P(None, None, "tile", None),
            P(("tile", "pos"), None, None),
            P(("tile", "pos"), None),
            P(("tile", "pos")),
        ),
        out_specs=(P(None, None, "tile", None), P()),
        check_vma=False,
    )
```

```python
import math

import jax
import jax.numpy as jnp
import ml_dtypes
import numpy as np
from jax import lax
from jax.experimental import pallas as pl
from jax.experimental.pallas import tpu as pltpu
from jax.sharding import PartitionSpec as P

PROP_COEF = 0.5
AMP_EPS = 0.05
LANES = 128
CHUNK = 32
EARLY_PAIRS = 3
GIVEN = 2
SHARDS = 4


def fixed_tables(edge):
    index = np.arange(edge)
    angles = (np.outer(index, index) % edge) * (2.0 * math.pi / edge)
    cosine = (np.cos(angles) / math.sqrt(edge)).astype(ml_dtypes.bfloat16).astype(np.float64)
    sine = (np.sin(angles) / math.sqrt(edge)).astype(ml_dtypes.bfloat16).astype(np.float64)
    forward = cosine - 1j * sine
    centred = np.where(index < edge // 2, index, index - edge)
    ramp = np.exp(-1j * (PROP_COEF * math.pi / edge) * centred * centred)
    spread = (np.conj(forward) * ramp[None, :]) @ forward
    planes = [
        plane for matrix in (spread, forward) for plane in (matrix.real, matrix.imag, -matrix.imag)
    ]
    return jnp.asarray(np.stack(planes).astype(ml_dtypes.bfloat16))


def lay_tables(planes, tables):
    edge = planes.shape[1]
    lo, hi = pl.ds(0, edge), pl.ds(edge, edge)
    for k in range(2):
        real, imag, negated = (planes[3 * k + i] for i in range(3))
        left, right = tables[2 * k : 2 * k + 2]
        left[lo, lo], left[lo, hi], left[hi, lo], left[hi, hi] = real, negated, imag, real
        right[lo, lo], right[lo, hi], right[hi, lo], right[hi, hi] = real, imag, negated, real


def interleaved(first, second):
    marks = [(k / len(first), 0, k) for k in range(len(first))]
    marks += [((k + 0.5) / len(second), 1, k) for k in range(len(second))]
    for _, which, k in sorted(marks):
        (first, second)[which][k]()


def slot_stages(slot, alive, base_row, refs, work):
    corner, probe, amp, tables, wide, acc, probe_acc = refs
    rolled, arriving, field, stack, joined = work
    left_a, right_a, left_f, right_f = tables
    edge = probe.shape[1]
    col_tiles = wide.shape[2]
    parts = edge // LANES
    lane = lax.broadcasted_iota(jnp.int32, (CHUNK, LANES), 1)
    row = corner[slot, 0] - base_row
    col = corner[slot, 1]
    first = jnp.minimum(col // LANES, col_tiles - parts - 1)
    shift = col - first * LANES
    turn = jnp.where(shift >= LANES, 0, shift)
    back = jnp.where(turn == 0, 0, LANES - turn)
    own = lane >= shift
    near = lane < LANES - shift

    def patch(part, s, i, j):
        rows = pl.ds(row + i, CHUNK)
        main = wide[part, s, first + j, rows, :]
        if j > 0:
            return main
        return jnp.where(own, main, wide[part, s, first + parts, rows, :])

    def place(part, s, i, j, value):
        rows = pl.ds(row + i, CHUNK)
        if j > 0:
            acc[part, s, first + j, rows, :] += value
        else:
            acc[part, s, first, rows, :] += jnp.where(own, value, 0.0)
            acc[part, s, first + parts, rows, :] += jnp.where(own, 0.0, value)

    def put(i, j, re, im):
        cols = pl.ds(j * LANES, LANES)
        stack[pl.ds(i, CHUNK), cols] = re.astype(jnp.bfloat16)
        stack[pl.ds(edge + i, CHUNK), cols] = im.astype(jnp.bfloat16)

    def halves():
        return [(j, pl.ds(j * LANES, LANES)) for j in range(parts)]

    def enter(i):
        rows = pl.ds(i, CHUNK)
        turned = [
            [pltpu.roll(probe[part, rows, cols], turn, 1) for j, cols in halves()]
            for part in range(2)
        ]
        for j, cols in halves():
            u_re, u_im = [
                jnp.where(own, turned[part][j], turned[part][j - 1]) for part in range(2)
            ]
            rolled[0, rows, cols] = u_re
            rolled[1, rows, cols] = u_im
            o_re, o_im = patch(0, 0, i, j), patch(1, 0, i, j)
            put(i, j, u_re * o_re - u_im * o_im, u_re * o_im + u_im * o_re)

    def second_slice(i):
        rows = pl.ds(i, CHUNK)
        for j, cols in halves():
            u_re, u_im = arriving[0, rows, cols], arriving[1, rows, cols]
            o_re, o_im = patch(0, 1, i, j), patch(1, 1, i, j)
            put(i, j, u_re * o_re - u_im * o_im, u_re * o_im + u_im * o_re)

    def residual(i):
        rows = pl.ds(i, CHUNK)
        for j, cols in halves():
            far_re, far_im = field[0, rows, cols], field[1, rows, cols]
            measured = amp[slot, rows, cols].astype(jnp.float32) * alive
            ratio = measured * lax.rsqrt(far_re * far_re + far_im * far_im + AMP_EPS)
            put(i, j, (alive - ratio) * far_re, (ratio - alive) * far_im)

    def second_grad(i):
        rows = pl.ds(i, CHUNK)
        for j, cols in halves():
            u_re, u_im = arriving[0, rows, cols], arriving[1, rows, cols]
            w_re, w_im = field[0, rows, cols], field[1, rows, cols]
            place(0, 1, i, j, u_re * w_re - u_im * w_im)
            place(1, 1, i, j, u_re * w_im + u_im * w_re)
            o_re, o_im = patch(0, 1, i, j), patch(1, 1, i, j)
            put(i, j, o_re * w_re - o_im * w_im, o_re * w_im + o_im * w_re)

    def first_grad(i):
        rows = pl.ds(i, CHUNK)
        turned = [[None] * parts for _ in range(2)]
        for j, cols in halves():
            u_re, u_im = rolled[0, rows, cols], rolled[1, rows, cols]
            w_re, w_im = field[0, rows, cols], field[1, rows, cols]
            place(0, 0, i, j, u_re * w_re - u_im * w_im)
            place(1, 0, i, j, u_re * w_im + u_im * w_re)
            o_re, o_im = patch(0, 0, i, j), patch(1, 0, i, j)
            turned[0][j] = pltpu.roll(o_re * w_re - o_im * w_im, back, 1)
            turned[1][j] = pltpu.roll(o_re * w_im + o_im * w_re, back, 1)
        for part in range(2):
            for j, cols in halves():
                after = turned[part][(j + 1) % parts]
                probe_acc[part, rows, cols] += jnp.where(near, turned[part][j], after)

    def two_sided(left, right, out):
        def rows_of(part):
            span = pl.ds(part * edge, edge)
            joined[:, span] = jnp.dot(
                left[span, :], stack[...], preferred_element_type=jnp.float32
            ).astype(jnp.bfloat16)

        def cols_of(part):
            out[part] = jnp.dot(
                joined[...],
                right[:, pl.ds(part * edge, edge)],
                preferred_element_type=jnp.float32,
            )

        return [lambda p=p: rows_of(p) for p in range(2)] + [
            lambda p=p: cols_of(p) for p in range(2)
        ]

    def each(step):
        return [lambda i=i: step(i) for i in range(0, edge, CHUNK)]

    return [
        each(enter),
        two_sided(left_a, right_a, arriving),
        each(second_slice),
        two_sided(left_f, right_f, field),
        each(residual),
        two_sided(left_f, right_f, field),
        each(second_grad),
        two_sided(left_a, right_a, field),
        each(first_grad),
    ]


def listed(order, corner, lists, base_row, edge, tile_rows, second_call):
    mine, near, far, _ = lists
    slots = mine.shape[0] - 1
    own, near_own, far_own, far_near = (part[slots, 0] for part in lists)
    ahead = own + far_own - near_own - far_near
    give = jnp.minimum(jnp.maximum(ahead, 0) // 2, GIVEN)
    take = jnp.minimum(jnp.maximum(-ahead, 0) // 2, GIVEN)
    entries = [(mine[q, 0], mine[q, 1], q < own - give, True) for q in range(slots)]
    entries += [(far[q, 0], far[q, 1], q < far_own, q < slots // 2) for q in range(slots)]
    for k in range(GIVEN):
        q = jnp.maximum(near_own - GIVEN + k, 0)
        entries.append((near[q, 0], near[q, 1], k >= GIVEN - take, True))
    inner = []
    for q, (row, col, live, early) in enumerate(entries):
        corner[q, 0] = row
        corner[q, 1] = col
        fits = live & (row - base_row + edge <= tile_rows)
        inner.append(jnp.where(fits, 1, 0) if early else jnp.int32(0))
    early_total = jnp.minimum(sum(inner) // 2, EARLY_PAIRS) * 2
    taken = jnp.int32(0)
    rank = jnp.int32(0)
    order[0] = 0
    for q, (_, _, live, _) in enumerate(entries):
        first = jnp.where(rank < early_total, inner[q], 0)
        rank = rank + inner[q]
        chosen = jnp.where(live, 1 - first, 0) if second_call else first
        order[taken] = q
        taken = taken + chosen
    return taken


def run_pairs(order, total, base_row, refs, work):
    def visit(step, carry):
        a = order[2 * step]
        b_lives = 2 * step + 1 < total
        b = jnp.where(b_lives, order[2 * step + 1], a)
        ones = slot_stages(a, 1.0, base_row, refs, work[0])
        twos = slot_stages(b, jnp.where(b_lives, 1.0, 0.0), base_row, refs, work[1])
        for step_now in ones[0]:
            step_now()
        for k in range(1, len(ones)):
            if k % 2:
                interleaved(ones[k], twos[k - 1])
            else:
                interleaved(twos[k - 1], ones[k])
        for step_now in twos[-1]:
            step_now()
        return carry

    lax.fori_loop(0, (total + 1) // 2, visit, 0)


def widen(wide, source, start, part, s_from, s_to):
    rows = source.shape[-2]
    for t in range(wide.shape[2]):
        wide[part, s_to, t, pl.ds(start, rows), :] = source[
            part, s_from, :, pl.ds(t * LANES, LANES)
        ].astype(jnp.float32)


def fetch(copies, sems):
    started = {}
    for k, (group, source, target) in enumerate(copies):
        copy = pltpu.make_async_copy(source, target, sems.at[k])
        copy.start()
        started.setdefault(group, []).append(copy)

    def wait(group):
        for copy in started[group]:
            copy.wait()

    return wait


def amp_copies(own, far_a, far_b, given, amp):
    slots, ahead = own.shape[0], far_a.shape[0]
    copies = [("rest", own, amp.at[pl.ds(0, slots)]), ("rest", far_a, amp.at[pl.ds(slots, ahead)])]
    if far_b is not None:
        copies.append(("rest", far_b, amp.at[pl.ds(slots + ahead, slots - ahead)]))
    return copies + [("rest", given, amp.at[pl.ds(2 * slots, GIVEN)])]


def early_kernel(
    meta,
    mine,
    near,
    far,
    far_near,
    probe_any,
    spec_any,
    own_any,
    far_a_any,
    given_any,
    planes_any,
    acc,
    probe_acc,
    order,
    corner,
    sems,
    probe,
    spec,
    amp,
    planes,
    la,
    ra,
    lf,
    rf,
    wide,
    *work,
):
    wait = fetch(
        [
            ("spec", spec_any, spec),
            ("planes", planes_any, planes),
            ("rest", probe_any, probe),
        ]
        + amp_copies(own_any, far_a_any, None, given_any, amp),
        sems,
    )
    tables = (la, ra, lf, rf)
    edge = probe.shape[1]
    slices, tile_rows = spec.shape[1:3]
    for part in range(2):
        for s in range(slices):
            for t in range(wide.shape[2]):
                acc[part, s, t] = jnp.zeros(acc.shape[3:], jnp.float32)
    probe_acc[...] = jnp.zeros(probe_acc.shape, jnp.float32)
    total = listed(order, corner, (mine, near, far, far_near), meta[0], edge, tile_rows, False)
    wait("spec")
    for part in range(2):
        for s in range(slices):
            widen(wide, spec, 0, part, s, s)
    wait("planes")
    lay_tables(planes, tables)
    wait("rest")
    refs = (corner, probe, amp, tables, wide, acc, probe_acc)
    run_pairs(order, total, meta[0], refs, (work[:5], work[5:]))


def late_kernel(
    meta,
    mine,
    near,
    far,
    far_near,
    probe_any,
    spec_any,
    rim_own_any,
    rim_other_any,
    acc_any,
    probe_acc_any,
    own_any,
    far_a_any,
    far_b_any,
    given_any,
    planes_any,
    send_first,
    send_rows,
    keep_rim,
    keep_rows,
    keep_probe,
    order,
    corner,
    sems,
    probe,
    spec,
    amp,
    planes,
    la,
    ra,
    lf,
    rf,
    wide,
    rim_own,
    rim_other,
    acc,
    probe_acc,
    *work,
):
    slices, tile_rows, width = spec.shape[1:]
    edge = probe.shape[1]
    wait = fetch(
        [
            ("spec", spec_any, spec),
            ("planes", planes_any, planes),
            ("rim", rim_own_any, rim_own),
            ("rim", rim_other_any, rim_other),
            ("acc", acc_any, acc.at[:, :, :, pl.ds(0, tile_rows), :]),
            ("acc", probe_acc_any, probe_acc),
            ("rest", probe_any, probe),
        ]
        + amp_copies(own_any, far_a_any, far_b_any, given_any, amp),
        sems,
    )
    tables = (la, ra, lf, rf)
    half = meta[1]
    other = 1 - half
    col_tiles = width // LANES
    for part in range(2):
        for s in range(slices):
            for t in range(col_tiles):
                acc[part, s, t, pl.ds(tile_rows, edge), :] = jnp.zeros((edge, LANES), jnp.float32)
    total = listed(order, corner, (mine, near, far, far_near), meta[0], edge, tile_rows, True)
    wait("spec")
    for part in range(2):
        for s in range(slices):
            widen(wide, spec, 0, part, s, s)
    wait("planes")
    lay_tables(planes, tables)
    wait("rim")
    for part in range(2):
        widen(wide, rim_own, tile_rows, part, 0, half)
        widen(wide, rim_other, tile_rows, part, 0, other)
    wait("acc")
    wait("rest")
    refs = (corner, probe, amp, tables, wide, acc, probe_acc)
    run_pairs(order, total, meta[0], refs, (work[:5], work[5:]))

    below = pl.ds(tile_rows, edge)
    rows = pl.ds(0, tile_rows)
    for part in range(2):
        sign = 1.0 if part == 0 else -1.0
        for t in range(col_tiles):
            cols = pl.ds(t * LANES, LANES)
            send_first[pl.ds(part * edge, edge), cols] = (
                sign * acc[part, other, t, below, :]
            ).astype(jnp.bfloat16)
            keep_rim[part, :, cols] = sign * acc[part, half, t, below, :]
            send_rows[part, :, cols] = (sign * acc[part, other, t, rows, :]).astype(jnp.bfloat16)
            keep_rows[part, :, cols] = sign * acc[part, half, t, rows, :]
    deep = keep_probe.shape[0]
    flip = jnp.where(other == 1, -1.0, 1.0)
    for piece in range(width // edge):
        piece_rows, cols = pl.ds(piece * deep, deep), pl.ds(piece * edge, edge)
        send_first[pl.ds(2 * edge, deep), cols] = (
            flip * probe_acc[other, piece_rows, :]
        ).astype(jnp.bfloat16)
        keep_probe[:, cols] = -flip * probe_acc[half, piece_rows, :]


VMEM = pl.BlockSpec(memory_space=pltpu.VMEM)
SMEM = pl.BlockSpec(memory_space=pltpu.SMEM)
ANY = pl.BlockSpec(memory_space=pl.ANY)


def scratch(slots, slices, width, tile_rows, rows, edge, copies):
    entries = 2 * slots + GIVEN
    planes = pltpu.VMEM((2, edge, edge), jnp.float32)
    table = pltpu.VMEM((2 * edge, 2 * edge), jnp.bfloat16)
    stack = pltpu.VMEM((2 * edge, edge), jnp.bfloat16)
    joined = pltpu.VMEM((edge, 2 * edge), jnp.bfloat16)
    lead = [
        pltpu.SMEM((entries + 1,), jnp.int32),
        pltpu.SMEM((entries, 2), jnp.int32),
        pltpu.SemaphoreType.DMA((copies,)),
        planes,
        pltpu.VMEM((2, slices, tile_rows, width), jnp.bfloat16),
        pltpu.VMEM((entries, edge, edge), jnp.bfloat16),
        pltpu.VMEM((6, edge, edge), jnp.bfloat16),
        table,
        table,
        table,
        table,
        pltpu.VMEM((2, slices, width // LANES, rows, LANES), jnp.float32),
    ]
    return lead, [planes, planes, planes, stack, joined] * 2


def run_early(meta, lists, probe, spec, amps, planes):
    edge = probe.shape[1]
    _, slices, tile_rows, width = spec.shape
    operands = (probe, spec, *amps, planes)
    slots = amps[0].shape[0]
    lead, work = scratch(slots, slices, width, tile_rows, tile_rows, edge, len(operands))
    return pl.pallas_call(
        early_kernel,
        out_shape=(
            jax.ShapeDtypeStruct((2, slices, width // LANES, tile_rows, LANES), jnp.float32),
            jax.ShapeDtypeStruct((2, edge, edge), jnp.float32),
        ),
        in_specs=[SMEM] * 5 + [ANY] * len(operands),
        out_specs=(VMEM, VMEM),
        scratch_shapes=lead + work,
        compiler_params=pltpu.CompilerParams(vmem_limit_bytes=34 * 1024 * 1024),
        name="early_slots",
    )(meta, *lists, *operands)


def run_late(meta, lists, probe, spec, rims, accs, amps, planes):
    edge = probe.shape[1]
    _, slices, tile_rows, width = spec.shape
    total = tile_rows + edge
    deep = edge * edge // width
    operands = (probe, spec, *rims, *accs, *amps, planes)
    slots = amps[0].shape[0]
    lead, work = scratch(slots, slices, width, tile_rows, total, edge, len(operands))
    rim = pltpu.VMEM((2, 1, edge, width), jnp.bfloat16)
    return pl.pallas_call(
        late_kernel,
        out_shape=(
            jax.ShapeDtypeStruct((2 * edge + deep, width), jnp.bfloat16),
            jax.ShapeDtypeStruct((2, tile_rows, width), jnp.bfloat16),
            jax.ShapeDtypeStruct((2, edge, width), jnp.float32),
            jax.ShapeDtypeStruct((2, tile_rows, width), jnp.float32),
            jax.ShapeDtypeStruct((deep, width), jnp.float32),
        ),
        in_specs=[SMEM] * 5 + [ANY] * len(operands),
        out_specs=(VMEM,) * 5,
        scratch_shapes=lead
        + [
            rim,
            rim,
            pltpu.VMEM((2, slices, width // LANES, total, LANES), jnp.float32),
            pltpu.VMEM((2, edge, edge), jnp.float32),
        ]
        + work,
        compiler_params=pltpu.CompilerParams(vmem_limit_bytes=38 * 1024 * 1024),
        name="late_slots",
    )(meta, *lists, *operands)


def write_rows(meta, own, theirs, start, shape, base=None):
    slices, rows, width = shape[1], own.shape[1], own.shape[2]

    def kernel(meta, own, theirs, *rest):
        out, wide, sems = rest[-3:]
        half = meta[1]
        wide[half] = own[...].astype(jnp.float32)
        wide[1 - half] = theirs[...].astype(jnp.float32)
        copies = [
            pltpu.make_async_copy(
                wide.at[s, part], out.at[part, s, pl.ds(start, rows), :], sems.at[2 * s + part]
            )
            for s in range(slices)
            for part in range(2)
        ]
        for copy in copies:
            copy.start()
        for copy in copies:
            copy.wait()

    extra = [] if base is None else [base]
    return pl.pallas_call(
        kernel,
        out_shape=jax.ShapeDtypeStruct(shape, jnp.float32),
        in_specs=[SMEM, VMEM, VMEM] + [ANY] * len(extra),
        out_specs=ANY,
        input_output_aliases={} if base is None else {3: 0},
        scratch_shapes=[
            pltpu.VMEM((slices, 2, rows, width), jnp.float32),
            pltpu.SemaphoreType.DMA((2 * slices,)),
        ],
        compiler_params=pltpu.CompilerParams(vmem_limit_bytes=16 * 1024 * 1024),
        cost_estimate=pl.CostEstimate(
            flops=0, bytes_accessed=2 * slices * rows * width * 6, transcendentals=0
        ),
        name="write_rows",
    )(meta, own, theirs, *extra)


def traded(value, axis, distance):
    count = lax.axis_size(axis)
    return lax.ppermute(value, axis, [(i, i ^ distance) for i in range(count)])


def passed_along(value, axis, steps):
    count = lax.axis_size(axis)
    initial, last = (max(0, -steps), min(count, count - steps))
    return lax.ppermute(value, axis, [(source, source + steps) for source in range(initial, last)])


def narrow_sum(own, got):
    return (own.astype(jnp.float32) + got.astype(jnp.float32)).astype(jnp.bfloat16)


def unfolded(value, edge):
    return jnp.concatenate([value[:, k : k + edge] for k in range(0, value.shape[1], edge)], 0)


def split_probe(place, kept, got, first, group):
    deep, width = kept.shape
    rows = deep // group

    def kernel(place, kept, got, own, *rest):
        shares, total = rest[:-1], rest[-1]
        total[...] = kept[...] + got[pl.ds(first, deep), :].astype(jnp.float32)
        own[...] = total[pl.ds(pl.multiple_of(place[0] * rows, rows), rows), :]
        for d, share in enumerate(shares, 1):
            start = pl.multiple_of((place[0] ^ d) * rows, rows)
            share[...] = total[pl.ds(start, rows), :].astype(jnp.bfloat16)

    return pl.pallas_call(
        kernel,
        out_shape=(jax.ShapeDtypeStruct((rows, width), jnp.float32),)
        + (jax.ShapeDtypeStruct((rows, width), jnp.bfloat16),) * (group - 1),
        in_specs=[SMEM, VMEM, VMEM],
        out_specs=(VMEM,) * group,
        scratch_shapes=[pltpu.VMEM((deep, width), jnp.float32)],
        compiler_params=pltpu.CompilerParams(vmem_limit_bytes=8 * 1024 * 1024),
        name="split_probe",
    )(place, kept, got)


def join_probe(place, shares):
    rows, width = shares[0].shape

    def kernel(place, *rest):
        out = rest[-1]
        for d, share in enumerate(rest[:-1]):
            out[pl.ds(pl.multiple_of((place[0] ^ d) * rows, rows), rows), :] = share[...]

    return pl.pallas_call(
        kernel,
        out_shape=jax.ShapeDtypeStruct((rows * len(shares), width), jnp.bfloat16),
        in_specs=[SMEM] + [VMEM] * len(shares),
        out_specs=VMEM,
        compiler_params=pltpu.CompilerParams(vmem_limit_bytes=8 * 1024 * 1024),
        name="join_probe",
    )(place, *shares)


def body(probe_field, specimen, amplitude, scan_anchor, counts):
    edge = probe_field.shape[1]
    _, slices, tile_rows, width = specimen.shape
    slots = amplitude.shape[0]
    half = lax.axis_index("pos") % 2
    base_row = lax.axis_index("tile") * tile_rows
    meta = jnp.stack([base_row, half]).astype(jnp.int32)
    planes = fixed_tables(edge)
    rim_own = passed_along(
        lax.dynamic_slice(specimen, (0, half, 0, 0), (2, 1, edge, width)), "tile", -1
    )
    mine = jnp.concatenate([scan_anchor, jnp.broadcast_to(counts, (1, 2))], 0)
    near, far, far_near = (traded(mine, "pos", d) for d in (1, 2, 3))
    given = traded(
        lax.dynamic_slice(amplitude, (counts[0] - GIVEN, 0, 0), (GIVEN, edge, edge)), "pos", 1
    )
    far_a = traded(amplitude[: slots // 2], "pos", 2)
    rest, near, far, far_near = lax.optimization_barrier(
        (amplitude[slots // 2 :], near, far, far_near)
    )
    far_b = traded(rest, "pos", 2)
    lists = (mine, near, far, far_near)
    acc, probe_acc = run_early(
        meta, lists, probe_field, specimen, (amplitude, far_a, given), planes
    )
    rim_own, probe_acc = lax.optimization_barrier((rim_own, probe_acc))
    rim_other = traded(rim_own, "pos", 1)
    sent_first, sent_rows, kept_rim, kept_rows, kept_probe = run_late(
        meta,
        lists,
        probe_field,
        specimen,
        (rim_own, rim_other),
        (acc, probe_acc),
        (amplitude, far_a, far_b, given),
        planes,
    )
    got_first = traded(sent_first, "pos", 1)
    got_rows = traded(sent_rows, "pos", 1)
    below = kept_rim + got_first[: 2 * edge].reshape(kept_rim.shape).astype(jnp.float32)
    below = passed_along(below.astype(jnp.bfloat16), "tile", 1)
    tiles = lax.axis_size("tile")
    group = min(tiles // 2, SHARDS)
    place = (lax.axis_index("tile") // 2 % group).astype(jnp.int32).reshape(1)
    share, *others = split_probe(place, kept_probe, got_first, 2 * edge, group)
    for d, other in enumerate(others, 1):
        share = share + traded(other, "tile", 2 * d).astype(jnp.float32)
    share = share.astype(jnp.bfloat16)
    distance = 2 * group
    while distance < tiles:
        share = narrow_sum(share, traded(share, "tile", distance))
        distance *= 2
    share = narrow_sum(share, traded(share, "tile", 1))
    rows = kept_rows + got_rows.astype(jnp.float32)
    lower = rows[:, edge:].astype(jnp.bfloat16)
    tile_grad = write_rows(meta, lower, traded(lower, "pos", 1), edge, specimen.shape)
    upper = (rows[:, :edge] + below.astype(jnp.float32)).astype(jnp.bfloat16)
    tile_grad = write_rows(meta, upper, traded(upper, "pos", 1), 0, specimen.shape, tile_grad)
    probe_part = join_probe(
        place, [share] + [traded(share, "tile", 2 * d) for d in range(1, group)]
    )
    probe_theirs, tile_grad = lax.optimization_barrier((traded(probe_part, "pos", 1), tile_grad))
    probe_own, probe_theirs = [unfolded(value, edge) for value in (probe_part, probe_theirs)]
    probe_total = jnp.where(
        half == 0, jnp.stack([probe_own, probe_theirs]), jnp.stack([probe_theirs, probe_own])
    ).astype(jnp.float32)
    return (tile_grad, probe_total)


def solution(mesh):
    return jax.shard_map(
        body,
        mesh=mesh,
        in_specs=(
            P(),
            P(None, None, "tile", None),
            P(("tile", "pos"), None, None),
            P(("tile", "pos"), None),
            P(("tile", "pos")),
        ),
        out_specs=(P(None, None, "tile", None), P()),
        check_vma=False,
    )
```

```python
import math

import jax
import jax.numpy as jnp
import ml_dtypes
import numpy as np
from jax import lax
from jax.experimental import pallas as pl
from jax.experimental.pallas import tpu as pltpu
from jax.sharding import PartitionSpec as P

PROP_COEF = 0.5
AMP_EPS = 0.05
LANES = 128
CHUNK = 32
EARLY_PAIRS = 3
GIVEN = 2


def fixed_tables(edge):
    index = np.arange(edge)
    angles = (np.outer(index, index) % edge) * (2.0 * math.pi / edge)
    cosine = (np.cos(angles) / math.sqrt(edge)).astype(ml_dtypes.bfloat16).astype(np.float64)
    sine = (np.sin(angles) / math.sqrt(edge)).astype(ml_dtypes.bfloat16).astype(np.float64)
    forward = cosine - 1j * sine
    centred = np.where(index < edge // 2, index, index - edge)
    ramp = np.exp(-1j * (PROP_COEF * math.pi / edge) * centred * centred)
    spread = (np.conj(forward) * ramp[None, :]) @ forward
    planes = [
        plane for matrix in (spread, forward) for plane in (matrix.real, matrix.imag, -matrix.imag)
    ]
    return jnp.asarray(np.stack(planes).astype(ml_dtypes.bfloat16))


def lay_tables(planes, tables):
    edge = planes.shape[1]
    lo, hi = pl.ds(0, edge), pl.ds(edge, edge)
    for k in range(2):
        real, imag, negated = (planes[3 * k + i] for i in range(3))
        left, right = tables[2 * k : 2 * k + 2]
        left[lo, lo], left[lo, hi], left[hi, lo], left[hi, hi] = real, negated, imag, real
        right[lo, lo], right[lo, hi], right[hi, lo], right[hi, hi] = real, imag, negated, real


def interleaved(first, second):
    marks = [(k / len(first), 0, k) for k in range(len(first))]
    marks += [((k + 0.5) / len(second), 1, k) for k in range(len(second))]
    for _, which, k in sorted(marks):
        (first, second)[which][k]()


def slot_stages(slot, alive, base_row, refs, work):
    corner, probe, amp, tables, wide, acc, probe_acc = refs
    rolled, arriving, field, stack, joined = work
    left_a, right_a, left_f, right_f = tables
    edge = probe.shape[1]
    col_tiles = wide.shape[2]
    parts = edge // LANES
    lane = lax.broadcasted_iota(jnp.int32, (CHUNK, LANES), 1)
    row = corner[slot, 0] - base_row
    col = corner[slot, 1]
    first = jnp.minimum(col // LANES, col_tiles - parts - 1)
    shift = col - first * LANES
    turn = jnp.where(shift >= LANES, 0, shift)
    back = jnp.where(turn == 0, 0, LANES - turn)
    own = lane >= shift
    near = lane < LANES - shift

    def patch(part, s, i, j):
        rows = pl.ds(row + i, CHUNK)
        main = wide[part, s, first + j, rows, :]
        if j > 0:
            return main
        return jnp.where(own, main, wide[part, s, first + parts, rows, :])

    def place(part, s, i, j, value):
        rows = pl.ds(row + i, CHUNK)
        if j > 0:
            acc[part, s, first + j, rows, :] += value
        else:
            acc[part, s, first, rows, :] += jnp.where(own, value, 0.0)
            acc[part, s, first + parts, rows, :] += jnp.where(own, 0.0, value)

    def put(i, j, re, im):
        cols = pl.ds(j * LANES, LANES)
        stack[pl.ds(i, CHUNK), cols] = re.astype(jnp.bfloat16)
        stack[pl.ds(edge + i, CHUNK), cols] = im.astype(jnp.bfloat16)

    def halves():
        return [(j, pl.ds(j * LANES, LANES)) for j in range(parts)]

    def enter(i):
        rows = pl.ds(i, CHUNK)
        turned = [
            [pltpu.roll(probe[part, rows, cols], turn, 1) for j, cols in halves()]
            for part in range(2)
        ]
        for j, cols in halves():
            u_re, u_im = [
                jnp.where(own, turned[part][j], turned[part][j - 1]) for part in range(2)
            ]
            rolled[0, rows, cols] = u_re
            rolled[1, rows, cols] = u_im
            o_re, o_im = patch(0, 0, i, j), patch(1, 0, i, j)
            put(i, j, u_re * o_re - u_im * o_im, u_re * o_im + u_im * o_re)

    def second_slice(i):
        rows = pl.ds(i, CHUNK)
        for j, cols in halves():
            u_re, u_im = arriving[0, rows, cols], arriving[1, rows, cols]
            o_re, o_im = patch(0, 1, i, j), patch(1, 1, i, j)
            put(i, j, u_re * o_re - u_im * o_im, u_re * o_im + u_im * o_re)

    def residual(i):
        rows = pl.ds(i, CHUNK)
        for j, cols in halves():
            far_re, far_im = field[0, rows, cols], field[1, rows, cols]
            measured = amp[slot, rows, cols].astype(jnp.float32) * alive
            ratio = measured * lax.rsqrt(far_re * far_re + far_im * far_im + AMP_EPS)
            put(i, j, (alive - ratio) * far_re, (ratio - alive) * far_im)

    def second_grad(i):
        rows = pl.ds(i, CHUNK)
        for j, cols in halves():
            u_re, u_im = arriving[0, rows, cols], arriving[1, rows, cols]
            w_re, w_im = field[0, rows, cols], field[1, rows, cols]
            place(0, 1, i, j, u_re * w_re - u_im * w_im)
            place(1, 1, i, j, u_re * w_im + u_im * w_re)
            o_re, o_im = patch(0, 1, i, j), patch(1, 1, i, j)
            put(i, j, o_re * w_re - o_im * w_im, o_re * w_im + o_im * w_re)

    def first_grad(i):
        rows = pl.ds(i, CHUNK)
        turned = [[None] * parts for _ in range(2)]
        for j, cols in halves():
            u_re, u_im = rolled[0, rows, cols], rolled[1, rows, cols]
            w_re, w_im = field[0, rows, cols], field[1, rows, cols]
            place(0, 0, i, j, u_re * w_re - u_im * w_im)
            place(1, 0, i, j, u_re * w_im + u_im * w_re)
            o_re, o_im = patch(0, 0, i, j), patch(1, 0, i, j)
            turned[0][j] = pltpu.roll(o_re * w_re - o_im * w_im, back, 1)
            turned[1][j] = pltpu.roll(o_re * w_im + o_im * w_re, back, 1)
        for part in range(2):
            for j, cols in halves():
                after = turned[part][(j + 1) % parts]
                probe_acc[part, rows, cols] += jnp.where(near, turned[part][j], after)

    def two_sided(left, right, out):
        def rows_of(part):
            span = pl.ds(part * edge, edge)
            joined[:, span] = jnp.dot(
                left[span, :], stack[...], preferred_element_type=jnp.float32
            ).astype(jnp.bfloat16)

        def cols_of(part):
            out[part] = jnp.dot(
                joined[...],
                right[:, pl.ds(part * edge, edge)],
                preferred_element_type=jnp.float32,
            )

        return [lambda p=p: rows_of(p) for p in range(2)] + [
            lambda p=p: cols_of(p) for p in range(2)
        ]

    def each(step):
        return [lambda i=i: step(i) for i in range(0, edge, CHUNK)]

    return [
        each(enter),
        two_sided(left_a, right_a, arriving),
        each(second_slice),
        two_sided(left_f, right_f, field),
        each(residual),
        two_sided(left_f, right_f, field),
        each(second_grad),
        two_sided(left_a, right_a, field),
        each(first_grad),
    ]


def listed(order, corner, lists, base_row, edge, tile_rows, second_call):
    mine, near, far, _ = lists
    slots = mine.shape[0] - 1
    own, near_own, far_own, far_near = (part[slots, 0] for part in lists)
    ahead = own + far_own - near_own - far_near
    give = jnp.minimum(jnp.maximum(ahead, 0) // 2, GIVEN)
    take = jnp.minimum(jnp.maximum(-ahead, 0) // 2, GIVEN)
    entries = [(mine[q, 0], mine[q, 1], q < own - give, True) for q in range(slots)]
    entries += [(far[q, 0], far[q, 1], q < far_own, q < slots // 2) for q in range(slots)]
    for k in range(GIVEN):
        q = jnp.maximum(near_own - GIVEN + k, 0)
        entries.append((near[q, 0], near[q, 1], k >= GIVEN - take, True))
    inner = []
    for q, (row, col, live, early) in enumerate(entries):
        corner[q, 0] = row
        corner[q, 1] = col
        fits = live & (row - base_row + edge <= tile_rows)
        inner.append(jnp.where(fits, 1, 0) if early else jnp.int32(0))
    early_total = jnp.minimum(sum(inner) // 2, EARLY_PAIRS) * 2
    taken = jnp.int32(0)
    rank = jnp.int32(0)
    order[0] = 0
    for q, (_, _, live, _) in enumerate(entries):
        first = jnp.where(rank < early_total, inner[q], 0)
        rank = rank + inner[q]
        chosen = jnp.where(live, 1 - first, 0) if second_call else first
        order[taken] = q
        taken = taken + chosen
    return taken


def run_pairs(order, total, base_row, refs, work):
    def visit(step, carry):
        a = order[2 * step]
        b_lives = 2 * step + 1 < total
        b = jnp.where(b_lives, order[2 * step + 1], a)
        ones = slot_stages(a, 1.0, base_row, refs, work[0])
        twos = slot_stages(b, jnp.where(b_lives, 1.0, 0.0), base_row, refs, work[1])
        for step_now in ones[0]:
            step_now()
        for k in range(1, len(ones)):
            if k % 2:
                interleaved(ones[k], twos[k - 1])
            else:
                interleaved(twos[k - 1], ones[k])
        for step_now in twos[-1]:
            step_now()
        return carry

    lax.fori_loop(0, (total + 1) // 2, visit, 0)


def widen(wide, source, start, part, s_from, s_to):
    rows = source.shape[-2]
    for t in range(wide.shape[2]):
        wide[part, s_to, t, pl.ds(start, rows), :] = source[
            part, s_from, :, pl.ds(t * LANES, LANES)
        ].astype(jnp.float32)


def fetch(copies, sems):
    started = {}
    for k, (group, source, target) in enumerate(copies):
        copy = pltpu.make_async_copy(source, target, sems.at[k])
        copy.start()
        started.setdefault(group, []).append(copy)

    def wait(group):
        for copy in started[group]:
            copy.wait()

    return wait


def amp_copies(own, far_a, far_b, given, amp):
    slots, ahead = own.shape[0], far_a.shape[0]
    copies = [("rest", own, amp.at[pl.ds(0, slots)]), ("rest", far_a, amp.at[pl.ds(slots, ahead)])]
    if far_b is not None:
        copies.append(("rest", far_b, amp.at[pl.ds(slots + ahead, slots - ahead)]))
    return copies + [("rest", given, amp.at[pl.ds(2 * slots, GIVEN)])]


def early_kernel(
    meta,
    mine,
    near,
    far,
    far_near,
    probe_any,
    spec_any,
    own_any,
    far_a_any,
    given_any,
    planes_any,
    acc,
    probe_acc,
    order,
    corner,
    sems,
    probe,
    spec,
    amp,
    planes,
    la,
    ra,
    lf,
    rf,
    wide,
    *work,
):
    wait = fetch(
        [
            ("spec", spec_any, spec),
            ("planes", planes_any, planes),
            ("rest", probe_any, probe),
        ]
        + amp_copies(own_any, far_a_any, None, given_any, amp),
        sems,
    )
    tables = (la, ra, lf, rf)
    edge = probe.shape[1]
    slices, tile_rows = spec.shape[1:3]
    for part in range(2):
        for s in range(slices):
            for t in range(wide.shape[2]):
                acc[part, s, t] = jnp.zeros(acc.shape[3:], jnp.float32)
    probe_acc[...] = jnp.zeros(probe_acc.shape, jnp.float32)
    total = listed(order, corner, (mine, near, far, far_near), meta[0], edge, tile_rows, False)
    wait("spec")
    for part in range(2):
        for s in range(slices):
            widen(wide, spec, 0, part, s, s)
    wait("planes")
    lay_tables(planes, tables)
    wait("rest")
    refs = (corner, probe, amp, tables, wide, acc, probe_acc)
    run_pairs(order, total, meta[0], refs, (work[:5], work[5:]))


def late_kernel(
    meta,
    mine,
    near,
    far,
    far_near,
    probe_any,
    spec_any,
    rim_own_any,
    rim_other_any,
    acc_any,
    probe_acc_any,
    own_any,
    far_a_any,
    far_b_any,
    given_any,
    planes_any,
    send_first,
    send_rows,
    keep_rim,
    keep_rows,
    keep_probe,
    order,
    corner,
    sems,
    probe,
    spec,
    amp,
    planes,
    la,
    ra,
    lf,
    rf,
    wide,
    rim_own,
    rim_other,
    acc,
    probe_acc,
    *work,
):
    slices, tile_rows, width = spec.shape[1:]
    edge = probe.shape[1]
    wait = fetch(
        [
            ("spec", spec_any, spec),
            ("planes", planes_any, planes),
            ("rim", rim_own_any, rim_own),
            ("rim", rim_other_any, rim_other),
            ("acc", acc_any, acc.at[:, :, :, pl.ds(0, tile_rows), :]),
            ("acc", probe_acc_any, probe_acc),
            ("rest", probe_any, probe),
        ]
        + amp_copies(own_any, far_a_any, far_b_any, given_any, amp),
        sems,
    )
    tables = (la, ra, lf, rf)
    half = meta[1]
    other = 1 - half
    col_tiles = width // LANES
    for part in range(2):
        for s in range(slices):
            for t in range(col_tiles):
                acc[part, s, t, pl.ds(tile_rows, edge), :] = jnp.zeros((edge, LANES), jnp.float32)
    total = listed(order, corner, (mine, near, far, far_near), meta[0], edge, tile_rows, True)
    wait("spec")
    for part in range(2):
        for s in range(slices):
            widen(wide, spec, 0, part, s, s)
    wait("planes")
    lay_tables(planes, tables)
    wait("rim")
    for part in range(2):
        widen(wide, rim_own, tile_rows, part, 0, half)
        widen(wide, rim_other, tile_rows, part, 0, other)
    wait("acc")
    wait("rest")
    refs = (corner, probe, amp, tables, wide, acc, probe_acc)
    run_pairs(order, total, meta[0], refs, (work[:5], work[5:]))

    below = pl.ds(tile_rows, edge)
    rows = pl.ds(0, tile_rows)
    for part in range(2):
        sign = 1.0 if part == 0 else -1.0
        for t in range(col_tiles):
            cols = pl.ds(t * LANES, LANES)
            send_first[pl.ds(part * edge, edge), cols] = (
                sign * acc[part, other, t, below, :]
            ).astype(jnp.bfloat16)
            keep_rim[part, :, cols] = sign * acc[part, half, t, below, :]
            send_rows[part, :, cols] = (sign * acc[part, other, t, rows, :]).astype(jnp.bfloat16)
            keep_rows[part, :, cols] = sign * acc[part, half, t, rows, :]
    deep = keep_probe.shape[0]
    flip = jnp.where(other == 1, -1.0, 1.0)
    for piece in range(width // edge):
        piece_rows, cols = pl.ds(piece * deep, deep), pl.ds(piece * edge, edge)
        send_first[pl.ds(2 * edge, deep), cols] = (
            flip * probe_acc[other, piece_rows, :]
        ).astype(jnp.bfloat16)
        keep_probe[:, cols] = -flip * probe_acc[half, piece_rows, :]


VMEM = pl.BlockSpec(memory_space=pltpu.VMEM)
SMEM = pl.BlockSpec(memory_space=pltpu.SMEM)
ANY = pl.BlockSpec(memory_space=pl.ANY)


def scratch(slots, slices, width, tile_rows, rows, edge, copies):
    entries = 2 * slots + GIVEN
    planes = pltpu.VMEM((2, edge, edge), jnp.float32)
    table = pltpu.VMEM((2 * edge, 2 * edge), jnp.bfloat16)
    stack = pltpu.VMEM((2 * edge, edge), jnp.bfloat16)
    joined = pltpu.VMEM((edge, 2 * edge), jnp.bfloat16)
    lead = [
        pltpu.SMEM((entries + 1,), jnp.int32),
        pltpu.SMEM((entries, 2), jnp.int32),
        pltpu.SemaphoreType.DMA((copies,)),
        planes,
        pltpu.VMEM((2, slices, tile_rows, width), jnp.bfloat16),
        pltpu.VMEM((entries, edge, edge), jnp.bfloat16),
        pltpu.VMEM((6, edge, edge), jnp.bfloat16),
        table,
        table,
        table,
        table,
        pltpu.VMEM((2, slices, width // LANES, rows, LANES), jnp.float32),
    ]
    return lead, [planes, planes, planes, stack, joined] * 2


def run_early(meta, lists, probe, spec, amps, planes):
    edge = probe.shape[1]
    _, slices, tile_rows, width = spec.shape
    operands = (probe, spec, *amps, planes)
    slots = amps[0].shape[0]
    lead, work = scratch(slots, slices, width, tile_rows, tile_rows, edge, len(operands))
    return pl.pallas_call(
        early_kernel,
        out_shape=(
            jax.ShapeDtypeStruct((2, slices, width // LANES, tile_rows, LANES), jnp.float32),
            jax.ShapeDtypeStruct((2, edge, edge), jnp.float32),
        ),
        in_specs=[SMEM] * 5 + [ANY] * len(operands),
        out_specs=(VMEM, VMEM),
        scratch_shapes=lead + work,
        compiler_params=pltpu.CompilerParams(vmem_limit_bytes=24 * 1024 * 1024),
        name="early_slots",
    )(meta, *lists, *operands)


def run_late(meta, lists, probe, spec, rims, accs, amps, planes):
    edge = probe.shape[1]
    _, slices, tile_rows, width = spec.shape
    total = tile_rows + edge
    deep = edge * edge // width
    operands = (probe, spec, *rims, *accs, *amps, planes)
    slots = amps[0].shape[0]
    lead, work = scratch(slots, slices, width, tile_rows, total, edge, len(operands))
    rim = pltpu.VMEM((2, 1, edge, width), jnp.bfloat16)
    return pl.pallas_call(
        late_kernel,
        out_shape=(
            jax.ShapeDtypeStruct((2 * edge + deep, width), jnp.bfloat16),
            jax.ShapeDtypeStruct((2, tile_rows, width), jnp.bfloat16),
            jax.ShapeDtypeStruct((2, edge, width), jnp.float32),
            jax.ShapeDtypeStruct((2, tile_rows, width), jnp.float32),
            jax.ShapeDtypeStruct((deep, width), jnp.float32),
        ),
        in_specs=[SMEM] * 5 + [ANY] * len(operands),
        out_specs=(VMEM,) * 5,
        scratch_shapes=lead
        + [
            rim,
            rim,
            pltpu.VMEM((2, slices, width // LANES, total, LANES), jnp.float32),
            pltpu.VMEM((2, edge, edge), jnp.float32),
        ]
        + work,
        compiler_params=pltpu.CompilerParams(vmem_limit_bytes=32 * 1024 * 1024),
        name="late_slots",
    )(meta, *lists, *operands)


def write_rows(meta, own, theirs, start, shape, base=None):
    slices, rows, width = shape[1], own.shape[1], own.shape[2]

    def kernel(meta, own, theirs, *rest):
        out, wide, sems = rest[-3:]
        half = meta[1]
        wide[half] = own[...].astype(jnp.float32)
        wide[1 - half] = theirs[...].astype(jnp.float32)
        copies = [
            pltpu.make_async_copy(
                wide.at[s, part], out.at[part, s, pl.ds(start, rows), :], sems.at[2 * s + part]
            )
            for s in range(slices)
            for part in range(2)
        ]
        for copy in copies:
            copy.start()
        for copy in copies:
            copy.wait()

    extra = [] if base is None else [base]
    return pl.pallas_call(
        kernel,
        out_shape=jax.ShapeDtypeStruct(shape, jnp.float32),
        in_specs=[SMEM, VMEM, VMEM] + [ANY] * len(extra),
        out_specs=ANY,
        input_output_aliases={} if base is None else {3: 0},
        scratch_shapes=[
            pltpu.VMEM((slices, 2, rows, width), jnp.float32),
            pltpu.SemaphoreType.DMA((2 * slices,)),
        ],
        compiler_params=pltpu.CompilerParams(vmem_limit_bytes=16 * 1024 * 1024),
        cost_estimate=pl.CostEstimate(
            flops=0, bytes_accessed=2 * slices * rows * width * 6, transcendentals=0
        ),
        name="write_rows",
    )(meta, own, theirs, *extra)


def traded(value, axis, distance):
    count = lax.axis_size(axis)
    return lax.ppermute(value, axis, [(i, i ^ distance) for i in range(count)])


def passed_along(value, axis, steps):
    count = lax.axis_size(axis)
    initial, last = (max(0, -steps), min(count, count - steps))
    return lax.ppermute(value, axis, [(source, source + steps) for source in range(initial, last)])


def narrow_sum(own, got):
    return (own.astype(jnp.float32) + got.astype(jnp.float32)).astype(jnp.bfloat16)


def unfolded(value, edge):
    return jnp.concatenate([value[:, k : k + edge] for k in range(0, value.shape[1], edge)], 0)


def cut_amplitudes(lists, amplitude):
    slots, edge = amplitude.shape[:2]
    ahead = slots // 2

    def kernel(mine, near, far, far_near, amp, first, second, last, sems):
        live = pl.ds(jnp.maximum(mine[slots, 0] - GIVEN, 0), GIVEN)
        copies = [
            pltpu.make_async_copy(amp.at[pl.ds(0, ahead)], first, sems.at[0]),
            pltpu.make_async_copy(amp.at[live], last, sems.at[1]),
            pltpu.make_async_copy(amp.at[pl.ds(ahead, slots - ahead)], second, sems.at[2]),
        ]
        for copy in copies:
            copy.start()
        for copy in copies:
            copy.wait()

    return pl.pallas_call(
        kernel,
        out_shape=tuple(
            jax.ShapeDtypeStruct((n, edge, edge), amplitude.dtype)
            for n in (ahead, slots - ahead, GIVEN)
        ),
        in_specs=[SMEM] * 4 + [ANY],
        out_specs=(ANY,) * 3,
        scratch_shapes=[pltpu.SemaphoreType.DMA((3,))],
        compiler_params=pltpu.CompilerParams(vmem_limit_bytes=8 * 1024 * 1024),
        name="cut_amplitudes",
    )(*lists, amplitude)


def body(probe_field, specimen, amplitude, scan_anchor, counts):
    edge = probe_field.shape[1]
    _, slices, tile_rows, width = specimen.shape
    slots = amplitude.shape[0]
    half = lax.axis_index("pos") % 2
    base_row = lax.axis_index("tile") * tile_rows
    meta = jnp.stack([base_row, half]).astype(jnp.int32)
    planes = fixed_tables(edge)
    rim_own = passed_along(
        lax.dynamic_slice(specimen, (0, half, 0, 0), (2, 1, edge, width)), "tile", -1
    )
    mine = jnp.concatenate([scan_anchor, jnp.broadcast_to(counts, (1, 2))], 0)
    near, far, far_near = (traded(mine, "pos", d) for d in (1, 2, 3))
    amp_a, amp_b, amp_last = cut_amplitudes((mine, near, far, far_near), amplitude)
    far_a = traded(amp_a, "pos", 2)
    far_b = traded(amp_b, "pos", 2)
    given = traded(amp_last, "pos", 1)
    lists = (mine, near, far, far_near)
    acc, probe_acc = run_early(
        meta, lists, probe_field, specimen, (amplitude, far_a, given), planes
    )
    rim_own, probe_acc = lax.optimization_barrier((rim_own, probe_acc))
    rim_other = traded(rim_own, "pos", 1)
    sent_first, sent_rows, kept_rim, kept_rows, kept_probe = run_late(
        meta,
        lists,
        probe_field,
        specimen,
        (rim_own, rim_other),
        (acc, probe_acc),
        (amplitude, far_a, far_b, given),
        planes,
    )
    got_first = traded(sent_first, "pos", 1)
    got_rows = traded(sent_rows, "pos", 1)
    below = kept_rim + got_first[: 2 * edge].reshape(kept_rim.shape).astype(jnp.float32)
    below = passed_along(below.astype(jnp.bfloat16), "tile", 1)
    probe_part = (kept_probe + got_first[2 * edge :].astype(jnp.float32)).astype(jnp.bfloat16)
    rows = kept_rows + got_rows.astype(jnp.float32)
    lower = rows[:, edge:].astype(jnp.bfloat16)
    tile_grad = write_rows(meta, lower, traded(lower, "pos", 1), edge, specimen.shape)
    distance = lax.axis_size("tile")
    while distance > 2:
        distance //= 2
        probe_part = narrow_sum(probe_part, traded(probe_part, "tile", distance))
    below, tile_grad, probe_part = lax.optimization_barrier((below, tile_grad, probe_part))
    upper = (rows[:, :edge] + below.astype(jnp.float32)).astype(jnp.bfloat16)
    tile_grad = write_rows(meta, upper, traded(upper, "pos", 1), 0, specimen.shape, tile_grad)
    probe_part = narrow_sum(probe_part, traded(probe_part, "tile", 1))
    probe_theirs, tile_grad = lax.optimization_barrier((traded(probe_part, "pos", 1), tile_grad))
    probe_own, probe_theirs = [unfolded(value, edge) for value in (probe_part, probe_theirs)]
    probe_total = jnp.where(
        half == 0, jnp.stack([probe_own, probe_theirs]), jnp.stack([probe_theirs, probe_own])
    ).astype(jnp.float32)
    return (tile_grad, probe_total)


def solution(mesh):
    return jax.shard_map(
        body,
        mesh=mesh,
        in_specs=(
            P(),
            P(None, None, "tile", None),
            P(("tile", "pos"), None, None),
            P(("tile", "pos"), None),
            P(("tile", "pos")),
        ),
        out_specs=(P(None, None, "tile", None), P()),
        check_vma=False,
    )
```

```python
import math

import jax
import jax.numpy as jnp
import ml_dtypes
import numpy as np
from jax import lax
from jax.experimental import pallas as pl
from jax.experimental.pallas import tpu as pltpu
from jax.sharding import PartitionSpec as P

PROP_COEF = 0.5
AMP_EPS = 0.05
LANES = 128
CHUNK = 32
EARLY_PAIRS = 3


def fixed_tables(edge):
    index = np.arange(edge)
    angles = (np.outer(index, index) % edge) * (2.0 * math.pi / edge)
    cosine = (np.cos(angles) / math.sqrt(edge)).astype(ml_dtypes.bfloat16).astype(np.float64)
    sine = (np.sin(angles) / math.sqrt(edge)).astype(ml_dtypes.bfloat16).astype(np.float64)
    forward = cosine - 1j * sine
    centred = np.where(index < edge // 2, index, index - edge)
    ramp = np.exp(-1j * (PROP_COEF * math.pi / edge) * centred * centred)
    spread = (np.conj(forward) * ramp[None, :]) @ forward
    planes = [
        plane for matrix in (spread, forward) for plane in (matrix.real, matrix.imag, -matrix.imag)
    ]
    return jnp.asarray(np.stack(planes).astype(ml_dtypes.bfloat16))


def lay_tables(planes, tables):
    edge = planes.shape[1]
    lo, hi = pl.ds(0, edge), pl.ds(edge, edge)
    for k in range(2):
        real, imag, negated = (planes[3 * k + i] for i in range(3))
        left, right = tables[2 * k : 2 * k + 2]
        left[lo, lo], left[lo, hi], left[hi, lo], left[hi, hi] = real, negated, imag, real
        right[lo, lo], right[lo, hi], right[hi, lo], right[hi, hi] = real, imag, negated, real


def interleaved(first, second):
    marks = [(k / len(first), 0, k) for k in range(len(first))]
    marks += [((k + 0.5) / len(second), 1, k) for k in range(len(second))]
    for _, which, k in sorted(marks):
        (first, second)[which][k]()


def slot_stages(slot, alive, base_row, refs, work):
    corner, probe, amp, tables, wide, acc, probe_acc = refs
    rolled, arriving, field, stack, joined = work
    left_a, right_a, left_f, right_f = tables
    edge = probe.shape[1]
    col_tiles = wide.shape[2]
    parts = edge // LANES
    lane = lax.broadcasted_iota(jnp.int32, (CHUNK, LANES), 1)
    row = corner[slot, 0] - base_row
    col = corner[slot, 1]
    first = jnp.minimum(col // LANES, col_tiles - parts - 1)
    shift = col - first * LANES
    turn = jnp.where(shift >= LANES, 0, shift)
    back = jnp.where(turn == 0, 0, LANES - turn)
    own = lane >= shift
    near = lane < LANES - shift

    def patch(part, s, i, j):
        rows = pl.ds(row + i, CHUNK)
        main = wide[part, s, first + j, rows, :]
        if j > 0:
            return main
        return jnp.where(own, main, wide[part, s, first + parts, rows, :])

    def place(part, s, i, j, value):
        rows = pl.ds(row + i, CHUNK)
        if j > 0:
            acc[part, s, first + j, rows, :] += value
        else:
            acc[part, s, first, rows, :] += jnp.where(own, value, 0.0)
            acc[part, s, first + parts, rows, :] += jnp.where(own, 0.0, value)

    def put(i, j, re, im):
        cols = pl.ds(j * LANES, LANES)
        stack[pl.ds(i, CHUNK), cols] = re.astype(jnp.bfloat16)
        stack[pl.ds(edge + i, CHUNK), cols] = im.astype(jnp.bfloat16)

    def halves():
        return [(j, pl.ds(j * LANES, LANES)) for j in range(parts)]

    def enter(i):
        rows = pl.ds(i, CHUNK)
        turned = [
            [pltpu.roll(probe[part, rows, cols], turn, 1) for j, cols in halves()]
            for part in range(2)
        ]
        for j, cols in halves():
            u_re, u_im = [
                jnp.where(own, turned[part][j], turned[part][j - 1]) for part in range(2)
            ]
            rolled[0, rows, cols] = u_re
            rolled[1, rows, cols] = u_im
            o_re, o_im = patch(0, 0, i, j), patch(1, 0, i, j)
            put(i, j, u_re * o_re - u_im * o_im, u_re * o_im + u_im * o_re)

    def second_slice(i):
        rows = pl.ds(i, CHUNK)
        for j, cols in halves():
            u_re, u_im = arriving[0, rows, cols], arriving[1, rows, cols]
            o_re, o_im = patch(0, 1, i, j), patch(1, 1, i, j)
            put(i, j, u_re * o_re - u_im * o_im, u_re * o_im + u_im * o_re)

    def residual(i):
        rows = pl.ds(i, CHUNK)
        for j, cols in halves():
            far_re, far_im = field[0, rows, cols], field[1, rows, cols]
            measured = amp[slot, rows, cols].astype(jnp.float32) * alive
            ratio = measured * lax.rsqrt(far_re * far_re + far_im * far_im + AMP_EPS)
            put(i, j, (alive - ratio) * far_re, (ratio - alive) * far_im)

    def second_grad(i):
        rows = pl.ds(i, CHUNK)
        for j, cols in halves():
            u_re, u_im = arriving[0, rows, cols], arriving[1, rows, cols]
            w_re, w_im = field[0, rows, cols], field[1, rows, cols]
            place(0, 1, i, j, u_re * w_re - u_im * w_im)
            place(1, 1, i, j, u_re * w_im + u_im * w_re)
            o_re, o_im = patch(0, 1, i, j), patch(1, 1, i, j)
            put(i, j, o_re * w_re - o_im * w_im, o_re * w_im + o_im * w_re)

    def first_grad(i):
        rows = pl.ds(i, CHUNK)
        turned = [[None] * parts for _ in range(2)]
        for j, cols in halves():
            u_re, u_im = rolled[0, rows, cols], rolled[1, rows, cols]
            w_re, w_im = field[0, rows, cols], field[1, rows, cols]
            place(0, 0, i, j, u_re * w_re - u_im * w_im)
            place(1, 0, i, j, u_re * w_im + u_im * w_re)
            o_re, o_im = patch(0, 0, i, j), patch(1, 0, i, j)
            turned[0][j] = pltpu.roll(o_re * w_re - o_im * w_im, back, 1)
            turned[1][j] = pltpu.roll(o_re * w_im + o_im * w_re, back, 1)
        for part in range(2):
            for j, cols in halves():
                after = turned[part][(j + 1) % parts]
                probe_acc[part, rows, cols] += jnp.where(near, turned[part][j], after)

    def two_sided(left, right, out):
        def rows_of(part):
            span = pl.ds(part * edge, edge)
            joined[:, span] = jnp.dot(
                left[span, :], stack[...], preferred_element_type=jnp.float32
            ).astype(jnp.bfloat16)

        def cols_of(part):
            out[part] = jnp.dot(
                joined[...],
                right[:, pl.ds(part * edge, edge)],
                preferred_element_type=jnp.float32,
            )

        return [lambda p=p: rows_of(p) for p in range(2)] + [
            lambda p=p: cols_of(p) for p in range(2)
        ]

    def each(step):
        return [lambda i=i: step(i) for i in range(0, edge, CHUNK)]

    return [
        each(enter),
        two_sided(left_a, right_a, arriving),
        each(second_slice),
        two_sided(left_f, right_f, field),
        each(residual),
        two_sided(left_f, right_f, field),
        each(second_grad),
        two_sided(left_a, right_a, field),
        each(first_grad),
    ]


def early_marks(rows, live, base_row, edge, tile_rows):
    inner = [
        jnp.where((q < live) & (row - base_row + edge <= tile_rows), 1, 0)
        for q, row in enumerate(rows)
    ]
    total = jnp.minimum(sum(inner) // 2, EARLY_PAIRS) * 2
    marks = []
    rank = jnp.int32(0)
    for one in inner:
        marks.append(jnp.where(rank < total, one, 0))
        rank = rank + one
    return marks


def put_in_order(order, marks):
    taken = jnp.int32(0)
    order[0] = 0
    for q, mark in enumerate(marks):
        order[taken] = q
        taken = taken + mark
    return taken


def list_early(order, corner, mine, base_row, edge, tile_rows):
    slots = mine.shape[0] - 1
    for q in range(slots):
        corner[q, 0] = mine[q, 0]
        corner[q, 1] = mine[q, 1]
    rows = [mine[q, 0] for q in range(slots)]
    return put_in_order(order, early_marks(rows, mine[slots, 0], base_row, edge, tile_rows))


def list_late(order, corner, lists, base_row, edge, tile_rows):
    mine, near, far, far_near = lists
    slots = mine.shape[0] - 1

    def left(part):
        live = part[slots, 0]
        marks = early_marks(
            [part[q, 0] for q in range(slots)], live, base_row, edge, tile_rows
        )
        return [jnp.where(q < live, 1 - mark, 0) for q, mark in enumerate(marks)]

    own, other = left(mine), left(near)
    ahead = sum(own) + far[slots, 0] - sum(other) - far_near[slots, 0]
    give = jnp.minimum(jnp.maximum(ahead, 0) // 2, sum(own))
    take = jnp.minimum(jnp.maximum(-ahead, 0) // 2, sum(other))
    kept, got = sum(own) - give, sum(other) - take
    marks = []
    rank = jnp.int32(0)
    for one in own:
        marks.append(jnp.where(rank < kept, one, 0))
        rank = rank + one
    marks += [jnp.where(q < far[slots, 0], 1, 0) for q in range(slots)]
    rank = jnp.int32(0)
    for one in other:
        marks.append(jnp.where(rank >= got, one, 0))
        rank = rank + one
    for k, part in enumerate((mine, far, near)):
        for q in range(slots):
            corner[k * slots + q, 0] = part[q, 0]
            corner[k * slots + q, 1] = part[q, 1]
    return put_in_order(order, marks)


def run_pairs(order, total, base_row, refs, work):
    def visit(step, carry):
        a = order[2 * step]
        b_lives = 2 * step + 1 < total
        b = jnp.where(b_lives, order[2 * step + 1], a)
        ones = slot_stages(a, 1.0, base_row, refs, work[0])
        twos = slot_stages(b, jnp.where(b_lives, 1.0, 0.0), base_row, refs, work[1])
        for step_now in ones[0]:
            step_now()
        for k in range(1, len(ones)):
            if k % 2:
                interleaved(ones[k], twos[k - 1])
            else:
                interleaved(twos[k - 1], ones[k])
        for step_now in twos[-1]:
            step_now()
        return carry

    lax.fori_loop(0, (total + 1) // 2, visit, 0)


def widen(wide, source, start, part, s_from, s_to):
    rows = source.shape[-2]
    for t in range(wide.shape[2]):
        wide[part, s_to, t, pl.ds(start, rows), :] = source[
            part, s_from, :, pl.ds(t * LANES, LANES)
        ].astype(jnp.float32)


def fetch(copies, sems):
    started = {}
    for k, (group, source, target) in enumerate(copies):
        copy = pltpu.make_async_copy(source, target, sems.at[k])
        copy.start()
        started.setdefault(group, []).append(copy)

    def wait(group):
        for copy in started[group]:
            copy.wait()

    return wait


def early_kernel(
    meta,
    mine,
    probe_any,
    spec_any,
    amp_any,
    planes_any,
    acc,
    probe_acc,
    order,
    corner,
    sems,
    probe,
    spec,
    amp,
    planes,
    la,
    ra,
    lf,
    rf,
    wide,
    *work,
):
    wait = fetch(
        [
            ("spec", spec_any, spec),
            ("planes", planes_any, planes),
            ("rest", probe_any, probe),
            ("rest", amp_any, amp),
        ],
        sems,
    )
    tables = (la, ra, lf, rf)
    edge = probe.shape[1]
    slices, tile_rows = spec.shape[1:3]
    for part in range(2):
        for s in range(slices):
            for t in range(wide.shape[2]):
                acc[part, s, t] = jnp.zeros(acc.shape[3:], jnp.float32)
    probe_acc[...] = jnp.zeros(probe_acc.shape, jnp.float32)
    total = list_early(order, corner, mine, meta[0], edge, tile_rows)
    wait("spec")
    for part in range(2):
        for s in range(slices):
            widen(wide, spec, 0, part, s, s)
    wait("planes")
    lay_tables(planes, tables)
    wait("rest")
    refs = (corner, probe, amp, tables, wide, acc, probe_acc)
    run_pairs(order, total, meta[0], refs, (work[:5], work[5:]))


def late_kernel(
    meta,
    mine,
    near,
    far,
    far_near,
    probe_any,
    spec_any,
    rim_own_any,
    rim_other_any,
    acc_any,
    probe_acc_any,
    own_any,
    far_amp_any,
    near_amp_any,
    planes_any,
    send_first,
    send_rows,
    keep_rim,
    keep_rows,
    keep_probe,
    order,
    corner,
    sems,
    probe,
    spec,
    amp,
    planes,
    la,
    ra,
    lf,
    rf,
    wide,
    rim_own,
    rim_other,
    acc,
    probe_acc,
    *work,
):
    slices, tile_rows, width = spec.shape[1:]
    edge = probe.shape[1]
    slots = mine.shape[0] - 1
    wait = fetch(
        [
            ("spec", spec_any, spec),
            ("planes", planes_any, planes),
            ("rim", rim_own_any, rim_own),
            ("rim", rim_other_any, rim_other),
            ("acc", acc_any, acc.at[:, :, :, pl.ds(0, tile_rows), :]),
            ("acc", probe_acc_any, probe_acc),
            ("rest", probe_any, probe),
            ("rest", own_any, amp.at[pl.ds(0, slots)]),
            ("rest", far_amp_any, amp.at[pl.ds(slots, slots)]),
            ("rest", near_amp_any, amp.at[pl.ds(2 * slots, slots)]),
        ],
        sems,
    )
    tables = (la, ra, lf, rf)
    half = meta[1]
    side = meta[2]
    other = 1 - half
    col_tiles = width // LANES
    for part in range(2):
        for s in range(slices):
            for t in range(col_tiles):
                acc[part, s, t, pl.ds(tile_rows, edge), :] = jnp.zeros((edge, LANES), jnp.float32)
    total = list_late(order, corner, (mine, near, far, far_near), meta[0], edge, tile_rows)
    wait("spec")
    for part in range(2):
        for s in range(slices):
            widen(wide, spec, 0, part, s, s)
    wait("planes")
    lay_tables(planes, tables)
    wait("rim")
    for part in range(2):
        widen(wide, rim_own, tile_rows, part, 0, half)
        widen(wide, rim_other, tile_rows, part, 0, other)
    wait("acc")
    wait("rest")
    refs = (corner, probe, amp, tables, wide, acc, probe_acc)
    run_pairs(order, total, meta[0], refs, (work[:5], work[5:]))

    below = pl.ds(tile_rows, edge)
    rows = pl.ds(0, tile_rows)
    turned = jnp.where(side == 1, -1.0, 1.0)
    for t in range(col_tiles):
        cols = pl.ds(t * LANES, LANES)
        send_first[pl.ds(0, edge), cols] = (turned * acc[side, other, t, below, :]).astype(
            jnp.bfloat16
        )
        keep_rim[:, cols] = turned * acc[side, half, t, below, :]
        for part in range(2):
            sign = 1.0 if part == 0 else -1.0
            send_rows[part, :, cols] = (sign * acc[part, other, t, rows, :]).astype(jnp.bfloat16)
            keep_rows[part, :, cols] = sign * acc[part, half, t, rows, :]
    deep = keep_probe.shape[0]
    flip = jnp.where(other == 1, -1.0, 1.0)
    for piece in range(width // edge):
        piece_rows, cols = pl.ds(piece * deep, deep), pl.ds(piece * edge, edge)
        send_first[pl.ds(edge, deep), cols] = (flip * probe_acc[other, piece_rows, :]).astype(
            jnp.bfloat16
        )
        keep_probe[:, cols] = -flip * probe_acc[half, piece_rows, :]


VMEM = pl.BlockSpec(memory_space=pltpu.VMEM)
SMEM = pl.BlockSpec(memory_space=pltpu.SMEM)
ANY = pl.BlockSpec(memory_space=pl.ANY)


def scratch(entries, slices, width, tile_rows, rows, edge, copies):
    planes = pltpu.VMEM((2, edge, edge), jnp.float32)
    table = pltpu.VMEM((2 * edge, 2 * edge), jnp.bfloat16)
    stack = pltpu.VMEM((2 * edge, edge), jnp.bfloat16)
    joined = pltpu.VMEM((edge, 2 * edge), jnp.bfloat16)
    lead = [
        pltpu.SMEM((entries + 1,), jnp.int32),
        pltpu.SMEM((entries, 2), jnp.int32),
        pltpu.SemaphoreType.DMA((copies,)),
        planes,
        pltpu.VMEM((2, slices, tile_rows, width), jnp.bfloat16),
        pltpu.VMEM((entries, edge, edge), jnp.bfloat16),
        pltpu.VMEM((6, edge, edge), jnp.bfloat16),
        table,
        table,
        table,
        table,
        pltpu.VMEM((2, slices, width // LANES, rows, LANES), jnp.float32),
    ]
    return lead, [planes, planes, planes, stack, joined] * 2


def run_early(meta, mine, probe, spec, amp, planes):
    edge = probe.shape[1]
    _, slices, tile_rows, width = spec.shape
    lead, work = scratch(amp.shape[0], slices, width, tile_rows, tile_rows, edge, 4)
    return pl.pallas_call(
        early_kernel,
        out_shape=(
            jax.ShapeDtypeStruct((2, slices, width // LANES, tile_rows, LANES), jnp.float32),
            jax.ShapeDtypeStruct((2, edge, edge), jnp.float32),
        ),
        in_specs=[SMEM] * 2 + [ANY] * 4,
        out_specs=(VMEM, VMEM),
        scratch_shapes=lead + work,
        compiler_params=pltpu.CompilerParams(vmem_limit_bytes=24 * 1024 * 1024),
        name="early_slots",
    )(meta, mine, probe, spec, amp, planes)


def run_late(meta, lists, probe, spec, rims, accs, amps, planes):
    edge = probe.shape[1]
    _, slices, tile_rows, width = spec.shape
    total = tile_rows + edge
    deep = edge * edge // width
    operands = (probe, spec, *rims, *accs, *amps, planes)
    entries = len(amps) * amps[0].shape[0]
    lead, work = scratch(entries, slices, width, tile_rows, total, edge, len(operands))
    rim = pltpu.VMEM((2, 1, edge, width), jnp.bfloat16)
    return pl.pallas_call(
        late_kernel,
        out_shape=(
            jax.ShapeDtypeStruct((edge + deep, width), jnp.bfloat16),
            jax.ShapeDtypeStruct((2, tile_rows, width), jnp.bfloat16),
            jax.ShapeDtypeStruct((edge, width), jnp.float32),
            jax.ShapeDtypeStruct((2, tile_rows, width), jnp.float32),
            jax.ShapeDtypeStruct((deep, width), jnp.float32),
        ),
        in_specs=[SMEM] * 5 + [ANY] * len(operands),
        out_specs=(VMEM,) * 5,
        scratch_shapes=lead
        + [
            rim,
            rim,
            pltpu.VMEM((2, slices, width // LANES, total, LANES), jnp.float32),
            pltpu.VMEM((2, edge, edge), jnp.float32),
        ]
        + work,
        compiler_params=pltpu.CompilerParams(vmem_limit_bytes=32 * 1024 * 1024),
        name="late_slots",
    )(meta, *lists, *operands)


def write_rows(meta, own, theirs, start, shape, base=None):
    slices, rows, width = shape[1], own.shape[1], own.shape[2]

    def kernel(meta, own, theirs, *rest):
        out, wide, sems = rest[-3:]
        half = meta[1]
        wide[half] = own[...].astype(jnp.float32)
        wide[1 - half] = theirs[...].astype(jnp.float32)
        copies = [
            pltpu.make_async_copy(
                wide.at[s, part], out.at[part, s, pl.ds(start, rows), :], sems.at[2 * s + part]
            )
            for s in range(slices)
            for part in range(2)
        ]
        for copy in copies:
            copy.start()
        for copy in copies:
            copy.wait()

    extra = [] if base is None else [base]
    return pl.pallas_call(
        kernel,
        out_shape=jax.ShapeDtypeStruct(shape, jnp.float32),
        in_specs=[SMEM, VMEM, VMEM] + [ANY] * len(extra),
        out_specs=ANY,
        input_output_aliases={} if base is None else {3: 0},
        scratch_shapes=[
            pltpu.VMEM((slices, 2, rows, width), jnp.float32),
            pltpu.SemaphoreType.DMA((2 * slices,)),
        ],
        compiler_params=pltpu.CompilerParams(vmem_limit_bytes=16 * 1024 * 1024),
        cost_estimate=pl.CostEstimate(
            flops=0, bytes_accessed=2 * slices * rows * width * 6, transcendentals=0
        ),
        name="write_rows",
    )(meta, own, theirs, *extra)


def traded(value, axis, distance):
    count = lax.axis_size(axis)
    return lax.ppermute(value, axis, [(i, i ^ distance) for i in range(count)])


def passed_along(value, axis, steps):
    count = lax.axis_size(axis)
    initial, last = (max(0, -steps), min(count, count - steps))
    return lax.ppermute(value, axis, [(source, source + steps) for source in range(initial, last)])


def narrow_sum(own, got):
    return (own.astype(jnp.float32) + got.astype(jnp.float32)).astype(jnp.bfloat16)


def unfolded(value, edge):
    return jnp.concatenate([value[:, k : k + edge] for k in range(0, value.shape[1], edge)], 0)


def body(probe_field, specimen, amplitude, scan_anchor, counts):
    edge = probe_field.shape[1]
    _, slices, tile_rows, width = specimen.shape
    half = lax.axis_index("pos") % 2
    side = lax.axis_index("pos") // 2 % 2
    base_row = lax.axis_index("tile") * tile_rows
    meta = jnp.stack([base_row, half, side]).astype(jnp.int32)
    planes = fixed_tables(edge)
    rim_own = passed_along(
        lax.dynamic_slice(specimen, (0, half, 0, 0), (2, 1, edge, width)), "tile", -1
    )
    mine = jnp.concatenate([scan_anchor, jnp.broadcast_to(counts, (1, 2))], 0)
    near, far, far_near = (traded(mine, "pos", d) for d in (1, 2, 3))
    far_amp = traded(amplitude, "pos", 2)
    near_amp = traded(amplitude, "pos", 1)
    acc, probe_acc = run_early(meta, mine, probe_field, specimen, amplitude, planes)
    rim_own, probe_acc = lax.optimization_barrier((rim_own, probe_acc))
    rim_other = traded(rim_own, "pos", 1)
    sent_first, sent_rows, kept_rim, kept_rows, kept_probe = run_late(
        meta,
        (mine, near, far, far_near),
        probe_field,
        specimen,
        (rim_own, rim_other),
        (acc, probe_acc),
        (amplitude, far_amp, near_amp),
        planes,
    )
    got_first = traded(sent_first, "pos", 1)
    got_rows = traded(sent_rows, "pos", 1)
    below = (kept_rim + got_first[:edge].astype(jnp.float32)).astype(jnp.bfloat16)
    below = passed_along(below, "tile", 1)
    below_other = traded(below, "pos", 2)
    probe_part = (kept_probe + got_first[edge:].astype(jnp.float32)).astype(jnp.bfloat16)
    distance = lax.axis_size("tile")
    while distance > 1:
        distance //= 2
        probe_part = narrow_sum(probe_part, traded(probe_part, "tile", distance))
    rows = kept_rows + got_rows.astype(jnp.float32)
    lower = rows[:, edge:].astype(jnp.bfloat16)
    tile_grad = write_rows(meta, lower, traded(lower, "pos", 1), edge, specimen.shape)
    below, below_other, tile_grad = lax.optimization_barrier((below, below_other, tile_grad))
    below = jnp.where(
        side == 0, jnp.stack([below, below_other]), jnp.stack([below_other, below])
    )
    upper = (rows[:, :edge] + below.astype(jnp.float32)).astype(jnp.bfloat16)
    tile_grad = write_rows(meta, upper, traded(upper, "pos", 1), 0, specimen.shape, tile_grad)
    probe_theirs, tile_grad = lax.optimization_barrier((traded(probe_part, "pos", 1), tile_grad))
    probe_own, probe_theirs = [unfolded(value, edge) for value in (probe_part, probe_theirs)]
    probe_total = jnp.where(
        half == 0, jnp.stack([probe_own, probe_theirs]), jnp.stack([probe_theirs, probe_own])
    ).astype(jnp.float32)
    return (tile_grad, probe_total)


def solution(mesh):
    return jax.shard_map(
        body,
        mesh=mesh,
        in_specs=(
            P(),
            P(None, None, "tile", None),
            P(("tile", "pos"), None, None),
            P(("tile", "pos"), None),
            P(("tile", "pos")),
        ),
        out_specs=(P(None, None, "tile", None), P()),
        check_vma=False,
    )
```

```python
import math

import jax
import jax.numpy as jnp
import ml_dtypes
import numpy as np
from jax import lax
from jax.experimental import pallas as pl
from jax.experimental.pallas import tpu as pltpu
from jax.sharding import PartitionSpec as P

PROP_COEF = 0.5
AMP_EPS = 0.05
LANES = 128
CHUNK = 32
EARLY = 4
MIDDLE = 4


def fixed_tables(edge):
    index = np.arange(edge)
    angles = (np.outer(index, index) % edge) * (2.0 * math.pi / edge)
    cosine = (np.cos(angles) / math.sqrt(edge)).astype(ml_dtypes.bfloat16).astype(np.float64)
    sine = (np.sin(angles) / math.sqrt(edge)).astype(ml_dtypes.bfloat16).astype(np.float64)
    forward = cosine - 1j * sine
    centred = np.where(index < edge // 2, index, index - edge)
    ramp = np.exp(-1j * (PROP_COEF * math.pi / edge) * centred * centred)
    spread = (np.conj(forward) * ramp[None, :]) @ forward
    planes = [
        plane for matrix in (spread, forward) for plane in (matrix.real, matrix.imag, -matrix.imag)
    ]
    return jnp.asarray(np.stack(planes).astype(ml_dtypes.bfloat16))


def lay_tables(planes, tables):
    edge = planes.shape[1]
    lo, hi = pl.ds(0, edge), pl.ds(edge, edge)
    for k in range(2):
        real, imag, negated = (planes[3 * k + i] for i in range(3))
        left, right = tables[2 * k : 2 * k + 2]
        left[lo, lo], left[lo, hi], left[hi, lo], left[hi, hi] = real, negated, imag, real
        right[lo, lo], right[lo, hi], right[hi, lo], right[hi, hi] = real, imag, negated, real


def interleaved(first, second):
    marks = [(k / len(first), 0, k) for k in range(len(first))]
    marks += [((k + 0.5) / len(second), 1, k) for k in range(len(second))]
    for _, which, k in sorted(marks):
        (first, second)[which][k]()


def slot_stages(slot, alive, base_row, refs, work):
    corner, probe, amp, tables, wide, acc, probe_acc = refs
    rolled, arriving, field, stack, joined = work
    left_a, right_a, left_f, right_f = tables
    edge = probe.shape[1]
    col_tiles = wide.shape[2]
    parts = edge // LANES
    lane = lax.broadcasted_iota(jnp.int32, (CHUNK, LANES), 1)
    row = corner[slot, 0] - base_row
    col = corner[slot, 1]
    first = jnp.minimum(col // LANES, col_tiles - parts - 1)
    shift = col - first * LANES
    turn = jnp.where(shift >= LANES, 0, shift)
    back = jnp.where(turn == 0, 0, LANES - turn)
    own = lane >= shift
    near = lane < LANES - shift

    def patch(part, s, i, j):
        rows = pl.ds(row + i, CHUNK)
        main = wide[part, s, first + j, rows, :]
        if j > 0:
            return main
        return jnp.where(own, main, wide[part, s, first + parts, rows, :])

    def place(part, s, i, j, value):
        rows = pl.ds(row + i, CHUNK)
        if j > 0:
            acc[part, s, first + j, rows, :] += value
        else:
            acc[part, s, first, rows, :] += jnp.where(own, value, 0.0)
            acc[part, s, first + parts, rows, :] += jnp.where(own, 0.0, value)

    def put(i, j, re, im):
        cols = pl.ds(j * LANES, LANES)
        stack[pl.ds(i, CHUNK), cols] = re.astype(jnp.bfloat16)
        stack[pl.ds(edge + i, CHUNK), cols] = im.astype(jnp.bfloat16)

    def halves():
        return [(j, pl.ds(j * LANES, LANES)) for j in range(parts)]

    def enter(i):
        rows = pl.ds(i, CHUNK)
        turned = [
            [pltpu.roll(probe[part, rows, cols], turn, 1) for j, cols in halves()]
            for part in range(2)
        ]
        for j, cols in halves():
            u_re, u_im = [
                jnp.where(own, turned[part][j], turned[part][j - 1]) for part in range(2)
            ]
            rolled[0, rows, cols] = u_re
            rolled[1, rows, cols] = u_im
            o_re, o_im = patch(0, 0, i, j), patch(1, 0, i, j)
            put(i, j, u_re * o_re - u_im * o_im, u_re * o_im + u_im * o_re)

    def second_slice(i):
        rows = pl.ds(i, CHUNK)
        for j, cols in halves():
            u_re, u_im = arriving[0, rows, cols], arriving[1, rows, cols]
            o_re, o_im = patch(0, 1, i, j), patch(1, 1, i, j)
            put(i, j, u_re * o_re - u_im * o_im, u_re * o_im + u_im * o_re)

    def residual(i):
        rows = pl.ds(i, CHUNK)
        for j, cols in halves():
            far_re, far_im = field[0, rows, cols], field[1, rows, cols]
            measured = amp[slot, rows, cols].astype(jnp.float32) * alive
            ratio = measured * lax.rsqrt(far_re * far_re + far_im * far_im + AMP_EPS)
            put(i, j, (alive - ratio) * far_re, (ratio - alive) * far_im)

    def second_grad(i):
        rows = pl.ds(i, CHUNK)
        for j, cols in halves():
            u_re, u_im = arriving[0, rows, cols], arriving[1, rows, cols]
            w_re, w_im = field[0, rows, cols], field[1, rows, cols]
            place(0, 1, i, j, u_re * w_re - u_im * w_im)
            place(1, 1, i, j, u_re * w_im + u_im * w_re)
            o_re, o_im = patch(0, 1, i, j), patch(1, 1, i, j)
            put(i, j, o_re * w_re - o_im * w_im, o_re * w_im + o_im * w_re)

    def first_grad(i):
        rows = pl.ds(i, CHUNK)
        turned = [[None] * parts for _ in range(2)]
        for j, cols in halves():
            u_re, u_im = rolled[0, rows, cols], rolled[1, rows, cols]
            w_re, w_im = field[0, rows, cols], field[1, rows, cols]
            place(0, 0, i, j, u_re * w_re - u_im * w_im)
            place(1, 0, i, j, u_re * w_im + u_im * w_re)
            o_re, o_im = patch(0, 0, i, j), patch(1, 0, i, j)
            turned[0][j] = pltpu.roll(o_re * w_re - o_im * w_im, back, 1)
            turned[1][j] = pltpu.roll(o_re * w_im + o_im * w_re, back, 1)
        for part in range(2):
            for j, cols in halves():
                after = turned[part][(j + 1) % parts]
                probe_acc[part, rows, cols] += jnp.where(near, turned[part][j], after)

    def two_sided(left, right, out):
        def rows_of(part):
            span = pl.ds(part * edge, edge)
            joined[:, span] = jnp.dot(
                left[span, :], stack[...], preferred_element_type=jnp.float32
            ).astype(jnp.bfloat16)

        def cols_of(part):
            out[part] = jnp.dot(
                joined[...],
                right[:, pl.ds(part * edge, edge)],
                preferred_element_type=jnp.float32,
            )

        return [lambda p=p: rows_of(p) for p in range(2)] + [
            lambda p=p: cols_of(p) for p in range(2)
        ]

    def each(step):
        return [lambda i=i: step(i) for i in range(0, edge, CHUNK)]

    return [
        each(enter),
        two_sided(left_a, right_a, arriving),
        each(second_slice),
        two_sided(left_f, right_f, field),
        each(residual),
        two_sided(left_f, right_f, field),
        each(second_grad),
        two_sided(left_a, right_a, field),
        each(first_grad),
    ]


def own_marks(part, base_row, edge, tile_rows):
    slots = part.shape[0] - 1
    first, second, left = [], [], []
    ranks = [jnp.int32(0), jnp.int32(0)]
    for q in range(slots):
        live = jnp.where(q < part[slots, 0], 1, 0)
        inner = jnp.where(part[q, 0] - base_row + edge <= tile_rows, live, 0)
        first.append(jnp.where(ranks[0] < EARLY, inner, 0))
        ranks[0] = ranks[0] + inner
        rest = live - first[q]
        second.append(jnp.where(ranks[1] < MIDDLE, rest, 0))
        ranks[1] = ranks[1] + rest
        left.append(rest - second[q])
    return first, second, left


def put_in_order(order, marks):
    taken = jnp.int32(0)
    order[0] = 0
    for q, mark in enumerate(marks):
        order[taken] = q
        taken = taken + mark
    return taken


def fill_corners(corner, part):
    for q in range(part.shape[0] - 1):
        corner[q, 0] = part[q, 0]
        corner[q, 1] = part[q, 1]


def list_late(order, corner, mine, across, crossed, base_row, edge, tile_rows):
    slots = mine.shape[0] - 1
    fill_corners(corner, mine)
    marks = own_marks(mine, base_row, edge, tile_rows)[2]
    for first, part in enumerate((across, crossed)):
        for q in range(first, slots, 2):
            corner[len(marks), 0] = part[q, 0]
            corner[len(marks), 1] = part[q, 1]
            marks.append(jnp.where(q < part[slots, 0], 1, 0))
    return put_in_order(order, marks)


def run_pairs(order, total, base_row, refs, work):
    def visit(step, carry):
        a = order[2 * step]
        b_lives = 2 * step + 1 < total
        b = jnp.where(b_lives, order[2 * step + 1], a)
        ones = slot_stages(a, 1.0, base_row, refs, work[0])
        twos = slot_stages(b, jnp.where(b_lives, 1.0, 0.0), base_row, refs, work[1])
        for step_now in ones[0]:
            step_now()
        for k in range(1, len(ones)):
            if k % 2:
                interleaved(ones[k], twos[k - 1])
            else:
                interleaved(twos[k - 1], ones[k])
        for step_now in twos[-1]:
            step_now()
        return carry

    lax.fori_loop(0, (total + 1) // 2, visit, 0)


def widen(wide, source, start, part, s_from, s_to):
    rows = source.shape[-2]
    for t in range(wide.shape[2]):
        wide[part, s_to, t, pl.ds(start, rows), :] = source[
            part, s_from, :, pl.ds(t * LANES, LANES)
        ].astype(jnp.float32)


def fetch(copies, sems):
    started = {}
    for k, (group, source, target) in enumerate(copies):
        copy = pltpu.make_async_copy(source, target, sems.at[k])
        copy.start()
        started.setdefault(group, []).append(copy)

    def wait(group):
        for copy in started[group]:
            copy.wait()

    return wait


def zero_rows(acc, start, rows):
    for part in range(2):
        for s in range(acc.shape[1]):
            for t in range(acc.shape[2]):
                acc[part, s, t, pl.ds(start, rows), :] = jnp.zeros((rows, LANES), jnp.float32)


def lay_patches(wide, wait, spec, rims, half):
    slices, tile_rows = spec.shape[1:3]
    wait("spec")
    for part in range(2):
        for s in range(slices):
            widen(wide, spec, 0, part, s, s)
    if rims:
        wait("rim")
        for part in range(2):
            widen(wide, rims[0], tile_rows, part, 0, half)
            widen(wide, rims[1], tile_rows, part, 0, 1 - half)


def early_kernel(
    meta,
    mine,
    probe_any,
    spec_any,
    amp_any,
    planes_any,
    acc,
    probe_acc,
    order,
    corner,
    sems,
    probe,
    spec,
    amp,
    planes,
    la,
    ra,
    lf,
    rf,
    wide,
    *work,
):
    wait = fetch(
        [
            ("spec", spec_any, spec),
            ("planes", planes_any, planes),
            ("rest", probe_any, probe),
            ("rest", amp_any, amp),
        ],
        sems,
    )
    tables = (la, ra, lf, rf)
    edge, tile_rows = probe.shape[1], spec.shape[2]
    zero_rows(acc, 0, tile_rows)
    probe_acc[...] = jnp.zeros(probe_acc.shape, jnp.float32)
    fill_corners(corner, mine)
    total = put_in_order(order, own_marks(mine, meta[0], edge, tile_rows)[0])
    lay_patches(wide, wait, spec, (), meta[1])
    wait("planes")
    lay_tables(planes, tables)
    wait("rest")
    refs = (corner, probe, amp, tables, wide, acc, probe_acc)
    run_pairs(order, total, meta[0], refs, (work[:5], work[5:]))


def middle_kernel(
    meta,
    mine,
    probe_any,
    spec_any,
    rim_own_any,
    rim_other_any,
    acc_any,
    probe_acc_any,
    amp_any,
    planes_any,
    acc,
    probe_acc,
    order,
    corner,
    sems,
    probe,
    spec,
    amp,
    planes,
    la,
    ra,
    lf,
    rf,
    wide,
    rim_own,
    rim_other,
    *work,
):
    edge, tile_rows = probe.shape[1], spec.shape[2]
    wait = fetch(
        [
            ("spec", spec_any, spec),
            ("planes", planes_any, planes),
            ("rim", rim_own_any, rim_own),
            ("rim", rim_other_any, rim_other),
            ("acc", acc_any, acc.at[:, :, :, pl.ds(0, tile_rows), :]),
            ("acc", probe_acc_any, probe_acc),
            ("rest", probe_any, probe),
            ("rest", amp_any, amp),
        ],
        sems,
    )
    tables = (la, ra, lf, rf)
    zero_rows(acc, tile_rows, edge)
    fill_corners(corner, mine)
    total = put_in_order(order, own_marks(mine, meta[0], edge, tile_rows)[1])
    lay_patches(wide, wait, spec, (rim_own, rim_other), meta[1])
    wait("planes")
    lay_tables(planes, tables)
    wait("acc")
    wait("rest")
    refs = (corner, probe, amp, tables, wide, acc, probe_acc)
    run_pairs(order, total, meta[0], refs, (work[:5], work[5:]))


def late_kernel(
    meta,
    mine,
    across,
    crossed,
    probe_any,
    spec_any,
    rim_own_any,
    rim_other_any,
    acc_any,
    probe_acc_any,
    amp_any,
    across_amp_any,
    crossed_amp_any,
    planes_any,
    send_first,
    send_rows,
    keep_rim,
    keep_rows,
    keep_probe,
    order,
    corner,
    sems,
    probe,
    spec,
    amp,
    planes,
    la,
    ra,
    lf,
    rf,
    wide,
    rim_own,
    rim_other,
    acc,
    probe_acc,
    *work,
):
    tile_rows, width = spec.shape[2:]
    edge = probe.shape[1]
    slots = mine.shape[0] - 1
    evens = across_amp_any.shape[0]
    wait = fetch(
        [
            ("spec", spec_any, spec),
            ("planes", planes_any, planes),
            ("rim", rim_own_any, rim_own),
            ("rim", rim_other_any, rim_other),
            ("acc", acc_any, acc),
            ("acc", probe_acc_any, probe_acc),
            ("rest", probe_any, probe),
            ("rest", amp_any, amp.at[pl.ds(0, slots)]),
            ("rest", across_amp_any, amp.at[pl.ds(slots, evens)]),
            ("rest", crossed_amp_any, amp.at[pl.ds(slots + evens, slots - evens)]),
        ],
        sems,
    )
    tables = (la, ra, lf, rf)
    half = meta[1]
    side = meta[2]
    other = 1 - half
    col_tiles = width // LANES
    total = list_late(order, corner, mine, across, crossed, meta[0], edge, tile_rows)
    lay_patches(wide, wait, spec, (rim_own, rim_other), half)
    wait("planes")
    lay_tables(planes, tables)
    wait("acc")
    wait("rest")
    refs = (corner, probe, amp, tables, wide, acc, probe_acc)
    run_pairs(order, total, meta[0], refs, (work[:5], work[5:]))

    below = pl.ds(tile_rows, edge)
    rows = pl.ds(0, tile_rows)
    turned = jnp.where(side == 1, -1.0, 1.0)
    for t in range(col_tiles):
        cols = pl.ds(t * LANES, LANES)
        send_first[pl.ds(0, edge), cols] = (turned * acc[side, other, t, below, :]).astype(
            jnp.bfloat16
        )
        keep_rim[:, cols] = turned * acc[side, half, t, below, :]
        for part in range(2):
            sign = 1.0 if part == 0 else -1.0
            send_rows[part, :, cols] = (sign * acc[part, other, t, rows, :]).astype(jnp.bfloat16)
            keep_rows[part, :, cols] = sign * acc[part, half, t, rows, :]
    deep = keep_probe.shape[0]
    flip = jnp.where(other == 1, -1.0, 1.0)
    for piece in range(width // edge):
        piece_rows, cols = pl.ds(piece * deep, deep), pl.ds(piece * edge, edge)
        send_first[pl.ds(edge, deep), cols] = (flip * probe_acc[other, piece_rows, :]).astype(
            jnp.bfloat16
        )
        keep_probe[:, cols] = -flip * probe_acc[half, piece_rows, :]


VMEM = pl.BlockSpec(memory_space=pltpu.VMEM)
SMEM = pl.BlockSpec(memory_space=pltpu.SMEM)
ANY = pl.BlockSpec(memory_space=pl.ANY)


def scratch(entries, slices, width, tile_rows, rows, edge, copies):
    planes = pltpu.VMEM((2, edge, edge), jnp.float32)
    table = pltpu.VMEM((2 * edge, 2 * edge), jnp.bfloat16)
    stack = pltpu.VMEM((2 * edge, edge), jnp.bfloat16)
    joined = pltpu.VMEM((edge, 2 * edge), jnp.bfloat16)
    lead = [
        pltpu.SMEM((entries + 1,), jnp.int32),
        pltpu.SMEM((entries, 2), jnp.int32),
        pltpu.SemaphoreType.DMA((copies,)),
        planes,
        pltpu.VMEM((2, slices, tile_rows, width), jnp.bfloat16),
        pltpu.VMEM((entries, edge, edge), jnp.bfloat16),
        pltpu.VMEM((6, edge, edge), jnp.bfloat16),
        table,
        table,
        table,
        table,
        pltpu.VMEM((2, slices, width // LANES, rows, LANES), jnp.float32),
    ]
    return lead, [planes, planes, planes, stack, joined] * 2


def run_early(meta, mine, probe, spec, amp, planes):
    edge = probe.shape[1]
    _, slices, tile_rows, width = spec.shape
    lead, work = scratch(amp.shape[0], slices, width, tile_rows, tile_rows, edge, 4)
    return pl.pallas_call(
        early_kernel,
        out_shape=(
            jax.ShapeDtypeStruct((2, slices, width // LANES, tile_rows, LANES), jnp.float32),
            jax.ShapeDtypeStruct((2, edge, edge), jnp.float32),
        ),
        in_specs=[SMEM] * 2 + [ANY] * 4,
        out_specs=(VMEM, VMEM),
        scratch_shapes=lead + work,
        compiler_params=pltpu.CompilerParams(vmem_limit_bytes=24 * 1024 * 1024),
        name="early_slots",
    )(meta, mine, probe, spec, amp, planes)


def run_middle(meta, mine, probe, spec, rims, accs, amp, planes):
    edge = probe.shape[1]
    _, slices, tile_rows, width = spec.shape
    total = tile_rows + edge
    operands = (probe, spec, *rims, *accs, amp, planes)
    lead, work = scratch(amp.shape[0], slices, width, tile_rows, total, edge, len(operands))
    rim = pltpu.VMEM((2, 1, edge, width), jnp.bfloat16)
    return pl.pallas_call(
        middle_kernel,
        out_shape=(
            jax.ShapeDtypeStruct((2, slices, width // LANES, total, LANES), jnp.float32),
            jax.ShapeDtypeStruct((2, edge, edge), jnp.float32),
        ),
        in_specs=[SMEM] * 2 + [ANY] * len(operands),
        out_specs=(VMEM, VMEM),
        scratch_shapes=lead + [rim, rim] + work,
        compiler_params=pltpu.CompilerParams(vmem_limit_bytes=30 * 1024 * 1024),
        name="middle_slots",
    )(meta, mine, *operands)


def run_late(meta, lists, probe, spec, rims, accs, amps, planes):
    edge = probe.shape[1]
    _, slices, tile_rows, width = spec.shape
    total = tile_rows + edge
    deep = edge * edge // width
    operands = (probe, spec, *rims, *accs, *amps, planes)
    entries = sum(amp.shape[0] for amp in amps)
    lead, work = scratch(entries, slices, width, tile_rows, total, edge, len(operands))
    rim = pltpu.VMEM((2, 1, edge, width), jnp.bfloat16)
    return pl.pallas_call(
        late_kernel,
        out_shape=(
            jax.ShapeDtypeStruct((edge + deep, width), jnp.bfloat16),
            jax.ShapeDtypeStruct((2, tile_rows, width), jnp.bfloat16),
            jax.ShapeDtypeStruct((edge, width), jnp.float32),
            jax.ShapeDtypeStruct((2, tile_rows, width), jnp.float32),
            jax.ShapeDtypeStruct((deep, width), jnp.float32),
        ),
        in_specs=[SMEM] * 4 + [ANY] * len(operands),
        out_specs=(VMEM,) * 5,
        scratch_shapes=lead
        + [
            rim,
            rim,
            pltpu.VMEM((2, slices, width // LANES, total, LANES), jnp.float32),
            pltpu.VMEM((2, edge, edge), jnp.float32),
        ]
        + work,
        compiler_params=pltpu.CompilerParams(vmem_limit_bytes=32 * 1024 * 1024),
        name="late_slots",
    )(meta, *lists, *operands)


def cut_amplitudes(amplitude, first):
    slots, edge = amplitude.shape[:2]
    count = len(range(first, slots, 2))

    def kernel(amp, out, sems):
        copies = [
            pltpu.make_async_copy(amp.at[first + 2 * k], out.at[k], sems.at[k])
            for k in range(count)
        ]
        for copy in copies:
            copy.start()
        for copy in copies:
            copy.wait()

    return pl.pallas_call(
        kernel,
        out_shape=jax.ShapeDtypeStruct((count, edge, edge), amplitude.dtype),
        in_specs=[ANY],
        out_specs=VMEM,
        scratch_shapes=[pltpu.SemaphoreType.DMA((count,))],
        compiler_params=pltpu.CompilerParams(vmem_limit_bytes=8 * 1024 * 1024),
        name="cut_amplitudes",
    )(amplitude)


def write_rows(meta, own, theirs, start, shape, base=None):
    slices, rows, width = shape[1], own.shape[1], own.shape[2]

    def kernel(meta, own, theirs, *rest):
        out, wide, sems = rest[-3:]
        half = meta[1]
        copies = []
        for s, source in ((half, own), (1 - half, theirs)):
            for part in range(2):
                wide[s, part] = source[part].astype(jnp.float32)
                copy = pltpu.make_async_copy(
                    wide.at[s, part],
                    out.at[part, s, pl.ds(start, rows), :],
                    sems.at[len(copies)],
                )
                copy.start()
                copies.append(copy)
        for copy in copies:
            copy.wait()

    extra = [] if base is None else [base]
    return pl.pallas_call(
        kernel,
        out_shape=jax.ShapeDtypeStruct(shape, jnp.float32),
        in_specs=[SMEM, VMEM, VMEM] + [ANY] * len(extra),
        out_specs=ANY,
        input_output_aliases={} if base is None else {3: 0},
        scratch_shapes=[
            pltpu.VMEM((slices, 2, rows, width), jnp.float32),
            pltpu.SemaphoreType.DMA((2 * slices,)),
        ],
        compiler_params=pltpu.CompilerParams(vmem_limit_bytes=16 * 1024 * 1024),
        cost_estimate=pl.CostEstimate(
            flops=0, bytes_accessed=2 * slices * rows * width * 6, transcendentals=0
        ),
        name="write_rows",
    )(meta, own, theirs, *extra)


def traded(value, axis, distance):
    count = lax.axis_size(axis)
    return lax.ppermute(value, axis, [(i, i ^ distance) for i in range(count)])


def passed_along(value, axis, steps):
    count = lax.axis_size(axis)
    initial, last = (max(0, -steps), min(count, count - steps))
    return lax.ppermute(value, axis, [(source, source + steps) for source in range(initial, last)])


def narrow_sum(own, got):
    return (own.astype(jnp.float32) + got.astype(jnp.float32)).astype(jnp.bfloat16)


def unfolded(value, edge):
    return jnp.concatenate([value[:, k : k + edge] for k in range(0, value.shape[1], edge)], 0)


def body(probe_field, specimen, amplitude, scan_anchor, counts):
    edge = probe_field.shape[1]
    _, slices, tile_rows, width = specimen.shape
    half = lax.axis_index("pos") % 2
    side = lax.axis_index("pos") // 2 % 2
    base_row = lax.axis_index("tile") * tile_rows
    meta = jnp.stack([base_row, half, side]).astype(jnp.int32)
    planes = fixed_tables(edge)
    rim_own = passed_along(
        lax.dynamic_slice(specimen, (0, half, 0, 0), (2, 1, edge, width)), "tile", -1
    )
    across_amp = traded(cut_amplitudes(amplitude, 0), "pos", 2)
    odd = cut_amplitudes(amplitude, 1)
    mine = jnp.concatenate([scan_anchor, jnp.broadcast_to(counts, (1, 2))], 0)
    across, crossed = (traded(mine, "pos", d) for d in (2, 3))
    accs = run_early(meta, mine, probe_field, specimen, amplitude, planes)
    rim_own, across_amp, odd, accs = lax.optimization_barrier((rim_own, across_amp, odd, accs))
    crossed_amp = traded(odd, "pos", 3)
    rims = (rim_own, traded(rim_own, "pos", 1))
    accs = run_middle(meta, mine, probe_field, specimen, rims, accs, amplitude, planes)
    sent_first, sent_rows, kept_rim, kept_rows, kept_probe = run_late(
        meta,
        (mine, across, crossed),
        probe_field,
        specimen,
        rims,
        accs,
        (amplitude, across_amp, crossed_amp),
        planes,
    )
    got_first = traded(sent_first, "pos", 1)
    got_first, sent_rows = lax.optimization_barrier((got_first, sent_rows))
    got_rows = traded(sent_rows, "pos", 1)
    below = (kept_rim + got_first[:edge].astype(jnp.float32)).astype(jnp.bfloat16)
    below = passed_along(below, "tile", 1)
    below_other = traded(below, "pos", 2)
    probe_part = (kept_probe + got_first[edge:].astype(jnp.float32)).astype(jnp.bfloat16)
    distance = lax.axis_size("tile")
    while distance > 1:
        distance //= 2
        probe_part = narrow_sum(probe_part, traded(probe_part, "tile", distance))
    rows = kept_rows + got_rows.astype(jnp.float32)
    lower = rows[:, edge:].astype(jnp.bfloat16)
    tile_grad = write_rows(meta, lower, traded(lower, "pos", 1), edge, specimen.shape)
    below, below_other, tile_grad = lax.optimization_barrier((below, below_other, tile_grad))
    below = jnp.where(
        side == 0, jnp.stack([below, below_other]), jnp.stack([below_other, below])
    )
    upper = (rows[:, :edge] + below.astype(jnp.float32)).astype(jnp.bfloat16)
    tile_grad = write_rows(meta, upper, traded(upper, "pos", 1), 0, specimen.shape, tile_grad)
    probe_theirs, tile_grad = lax.optimization_barrier((traded(probe_part, "pos", 1), tile_grad))
    probe_own, probe_theirs = [unfolded(value, edge) for value in (probe_part, probe_theirs)]
    probe_total = jnp.where(
        half == 0, jnp.stack([probe_own, probe_theirs]), jnp.stack([probe_theirs, probe_own])
    ).astype(jnp.float32)
    return (tile_grad, probe_total)


def solution(mesh):
    return jax.shard_map(
        body,
        mesh=mesh,
        in_specs=(
            P(),
            P(None, None, "tile", None),
            P(("tile", "pos"), None, None),
            P(("tile", "pos"), None),
            P(("tile", "pos")),
        ),
        out_specs=(P(None, None, "tile", None), P()),
        check_vma=False,
    )
```

```python
import math

import jax
import jax.numpy as jnp
import ml_dtypes
import numpy as np
from jax import lax
from jax.experimental import pallas as pl
from jax.experimental.pallas import tpu as pltpu
from jax.sharding import PartitionSpec as P

PROP_COEF = 0.5
AMP_EPS = 0.05
LANES = 128
CHUNK = 32
EARLY = 4
MIDDLE = 4


def fixed_tables(edge):
    index = np.arange(edge)
    angles = (np.outer(index, index) % edge) * (2.0 * math.pi / edge)
    cosine = (np.cos(angles) / math.sqrt(edge)).astype(ml_dtypes.bfloat16).astype(np.float64)
    sine = (np.sin(angles) / math.sqrt(edge)).astype(ml_dtypes.bfloat16).astype(np.float64)
    forward = cosine - 1j * sine
    centred = np.where(index < edge // 2, index, index - edge)
    ramp = np.exp(-1j * (PROP_COEF * math.pi / edge) * centred * centred)
    spread = (np.conj(forward) * ramp[None, :]) @ forward
    planes = [
        plane for matrix in (spread, forward) for plane in (matrix.real, matrix.imag, -matrix.imag)
    ]
    return jnp.asarray(np.stack(planes).astype(ml_dtypes.bfloat16))


def lay_tables(planes, tables):
    edge = planes.shape[1]
    lo, hi = pl.ds(0, edge), pl.ds(edge, edge)
    for k in range(2):
        real, imag, negated = (planes[3 * k + i] for i in range(3))
        left, right = tables[2 * k : 2 * k + 2]
        left[lo, lo], left[lo, hi], left[hi, lo], left[hi, hi] = real, negated, imag, real
        right[lo, lo], right[lo, hi], right[hi, lo], right[hi, hi] = real, imag, negated, real


def interleaved(first, second):
    marks = [(k / len(first), 0, k) for k in range(len(first))]
    marks += [((k + 0.5) / len(second), 1, k) for k in range(len(second))]
    for _, which, k in sorted(marks):
        (first, second)[which][k]()


def slot_stages(slot, alive, base_row, refs, work):
    corner, probe, amp, tables, wide, acc, probe_acc = refs
    rolled, arriving, field, stack, joined = work
    left_a, right_a, left_f, right_f = tables
    edge = probe.shape[1]
    col_tiles = wide.shape[2]
    parts = edge // LANES
    lane = lax.broadcasted_iota(jnp.int32, (CHUNK, LANES), 1)
    row = corner[slot, 0] - base_row
    col = corner[slot, 1]
    first = jnp.minimum(col // LANES, col_tiles - parts - 1)
    shift = col - first * LANES
    turn = jnp.where(shift >= LANES, 0, shift)
    back = jnp.where(turn == 0, 0, LANES - turn)
    own = lane >= shift
    near = lane < LANES - shift

    def patch(part, s, i, j):
        rows = pl.ds(row + i, CHUNK)
        main = wide[part, s, first + j, rows, :]
        if j > 0:
            return main
        return jnp.where(own, main, wide[part, s, first + parts, rows, :])

    def place(part, s, i, j, value):
        rows = pl.ds(row + i, CHUNK)
        if j > 0:
            acc[part, s, first + j, rows, :] += value
        else:
            acc[part, s, first, rows, :] += jnp.where(own, value, 0.0)
            acc[part, s, first + parts, rows, :] += jnp.where(own, 0.0, value)

    def put(i, j, re, im):
        cols = pl.ds(j * LANES, LANES)
        stack[pl.ds(i, CHUNK), cols] = re.astype(jnp.bfloat16)
        stack[pl.ds(edge + i, CHUNK), cols] = im.astype(jnp.bfloat16)

    def halves():
        return [(j, pl.ds(j * LANES, LANES)) for j in range(parts)]

    def enter(i):
        rows = pl.ds(i, CHUNK)
        turned = [
            [pltpu.roll(probe[part, rows, cols], turn, 1) for j, cols in halves()]
            for part in range(2)
        ]
        for j, cols in halves():
            u_re, u_im = [
                jnp.where(own, turned[part][j], turned[part][j - 1]) for part in range(2)
            ]
            rolled[0, rows, cols] = u_re
            rolled[1, rows, cols] = u_im
            o_re, o_im = patch(0, 0, i, j), patch(1, 0, i, j)
            put(i, j, u_re * o_re - u_im * o_im, u_re * o_im + u_im * o_re)

    def second_slice(i):
        rows = pl.ds(i, CHUNK)
        for j, cols in halves():
            u_re, u_im = arriving[0, rows, cols], arriving[1, rows, cols]
            o_re, o_im = patch(0, 1, i, j), patch(1, 1, i, j)
            put(i, j, u_re * o_re - u_im * o_im, u_re * o_im + u_im * o_re)

    def residual(i):
        rows = pl.ds(i, CHUNK)
        for j, cols in halves():
            far_re, far_im = field[0, rows, cols], field[1, rows, cols]
            measured = amp[slot, rows, cols].astype(jnp.float32) * alive
            ratio = measured * lax.rsqrt(far_re * far_re + far_im * far_im + AMP_EPS)
            put(i, j, (alive - ratio) * far_re, (ratio - alive) * far_im)

    def second_grad(i):
        rows = pl.ds(i, CHUNK)
        for j, cols in halves():
            u_re, u_im = arriving[0, rows, cols], arriving[1, rows, cols]
            w_re, w_im = field[0, rows, cols], field[1, rows, cols]
            place(0, 1, i, j, u_re * w_re - u_im * w_im)
            place(1, 1, i, j, u_re * w_im + u_im * w_re)
            o_re, o_im = patch(0, 1, i, j), patch(1, 1, i, j)
            put(i, j, o_re * w_re - o_im * w_im, o_re * w_im + o_im * w_re)

    def first_grad(i):
        rows = pl.ds(i, CHUNK)
        turned = [[None] * parts for _ in range(2)]
        for j, cols in halves():
            u_re, u_im = rolled[0, rows, cols], rolled[1, rows, cols]
            w_re, w_im = field[0, rows, cols], field[1, rows, cols]
            place(0, 0, i, j, u_re * w_re - u_im * w_im)
            place(1, 0, i, j, u_re * w_im + u_im * w_re)
            o_re, o_im = patch(0, 0, i, j), patch(1, 0, i, j)
            turned[0][j] = pltpu.roll(o_re * w_re - o_im * w_im, back, 1)
            turned[1][j] = pltpu.roll(o_re * w_im + o_im * w_re, back, 1)
        for part in range(2):
            for j, cols in halves():
                after = turned[part][(j + 1) % parts]
                probe_acc[part, rows, cols] += jnp.where(near, turned[part][j], after)

    def two_sided(left, right, out):
        def rows_of(part):
            span = pl.ds(part * edge, edge)
            joined[:, span] = jnp.dot(
                left[span, :], stack[...], preferred_element_type=jnp.float32
            ).astype(jnp.bfloat16)

        def cols_of(part):
            out[part] = jnp.dot(
                joined[...],
                right[:, pl.ds(part * edge, edge)],
                preferred_element_type=jnp.float32,
            )

        return [lambda p=p: rows_of(p) for p in range(2)] + [
            lambda p=p: cols_of(p) for p in range(2)
        ]

    def each(step):
        return [lambda i=i: step(i) for i in range(0, edge, CHUNK)]

    return [
        each(enter),
        two_sided(left_a, right_a, arriving),
        each(second_slice),
        two_sided(left_f, right_f, field),
        each(residual),
        two_sided(left_f, right_f, field),
        each(second_grad),
        two_sided(left_a, right_a, field),
        each(first_grad),
    ]


def own_marks(part, base_row, edge, tile_rows):
    slots = part.shape[0] - 1
    first, second, left = [], [], []
    ranks = [jnp.int32(0), jnp.int32(0)]
    for q in range(slots):
        live = jnp.where(q < part[slots, 0], 1, 0)
        inner = jnp.where(part[q, 0] - base_row + edge <= tile_rows, live, 0)
        first.append(jnp.where(ranks[0] < EARLY, inner, 0))
        ranks[0] = ranks[0] + inner
        rest = live - first[q]
        second.append(jnp.where(ranks[1] < MIDDLE, rest, 0))
        ranks[1] = ranks[1] + rest
        left.append(rest - second[q])
    return first, second, left


def put_in_order(order, marks):
    taken = jnp.int32(0)
    order[0] = 0
    for q, mark in enumerate(marks):
        order[taken] = q
        taken = taken + mark
    return taken


def fill_corners(corner, part):
    for q in range(part.shape[0] - 1):
        corner[q, 0] = part[q, 0]
        corner[q, 1] = part[q, 1]


def list_late(order, corner, mine, across, base_row, edge, tile_rows):
    slots = mine.shape[0] - 1
    fill_corners(corner, mine)
    marks = own_marks(mine, base_row, edge, tile_rows)[2]
    for q in range(slots):
        corner[slots + q, 0] = across[q, 0]
        corner[slots + q, 1] = across[q, 1]
        marks.append(jnp.where(q < across[slots, 0], 1, 0))
    return put_in_order(order, marks)


def run_pairs(order, total, base_row, refs, work):
    def visit(step, carry):
        a = order[2 * step]
        b_lives = 2 * step + 1 < total
        b = jnp.where(b_lives, order[2 * step + 1], a)
        ones = slot_stages(a, 1.0, base_row, refs, work[0])
        twos = slot_stages(b, jnp.where(b_lives, 1.0, 0.0), base_row, refs, work[1])
        for step_now in ones[0]:
            step_now()
        for k in range(1, len(ones)):
            if k % 2:
                interleaved(ones[k], twos[k - 1])
            else:
                interleaved(twos[k - 1], ones[k])
        for step_now in twos[-1]:
            step_now()
        return carry

    lax.fori_loop(0, (total + 1) // 2, visit, 0)


def widen(wide, source, start, part, s_from, s_to):
    rows = source.shape[-2]
    for t in range(wide.shape[2]):
        wide[part, s_to, t, pl.ds(start, rows), :] = source[
            part, s_from, :, pl.ds(t * LANES, LANES)
        ].astype(jnp.float32)


def fetch(copies, sems):
    started = {}
    for k, (group, source, target) in enumerate(copies):
        copy = pltpu.make_async_copy(source, target, sems.at[k])
        copy.start()
        started.setdefault(group, []).append(copy)

    def wait(group):
        for copy in started[group]:
            copy.wait()

    return wait


def zero_rows(acc, start, rows):
    for part in range(2):
        for s in range(acc.shape[1]):
            for t in range(acc.shape[2]):
                acc[part, s, t, pl.ds(start, rows), :] = jnp.zeros((rows, LANES), jnp.float32)


def lay_patches(wide, wait, spec, rims, half):
    slices, tile_rows = spec.shape[1:3]
    wait("spec")
    for part in range(2):
        for s in range(slices):
            widen(wide, spec, 0, part, s, s)
    if rims:
        wait("rim")
        for part in range(2):
            widen(wide, rims[0], tile_rows, part, 0, half)
            widen(wide, rims[1], tile_rows, part, 0, 1 - half)


def early_kernel(
    meta,
    mine,
    probe_any,
    spec_any,
    amp_any,
    planes_any,
    acc,
    probe_acc,
    order,
    corner,
    sems,
    probe,
    spec,
    amp,
    planes,
    la,
    ra,
    lf,
    rf,
    wide,
    *work,
):
    wait = fetch(
        [
            ("spec", spec_any, spec),
            ("planes", planes_any, planes),
            ("rest", probe_any, probe),
            ("rest", amp_any, amp),
        ],
        sems,
    )
    tables = (la, ra, lf, rf)
    edge, tile_rows = probe.shape[1], spec.shape[2]
    zero_rows(acc, 0, tile_rows)
    probe_acc[...] = jnp.zeros(probe_acc.shape, jnp.float32)
    fill_corners(corner, mine)
    total = put_in_order(order, own_marks(mine, meta[0], edge, tile_rows)[0])
    lay_patches(wide, wait, spec, (), meta[1])
    wait("planes")
    lay_tables(planes, tables)
    wait("rest")
    refs = (corner, probe, amp, tables, wide, acc, probe_acc)
    run_pairs(order, total, meta[0], refs, (work[:5], work[5:]))


def middle_kernel(
    meta,
    mine,
    probe_any,
    spec_any,
    rim_own_any,
    rim_other_any,
    acc_any,
    probe_acc_any,
    amp_any,
    planes_any,
    acc,
    probe_acc,
    order,
    corner,
    sems,
    probe,
    spec,
    amp,
    planes,
    la,
    ra,
    lf,
    rf,
    wide,
    rim_own,
    rim_other,
    *work,
):
    edge, tile_rows = probe.shape[1], spec.shape[2]
    wait = fetch(
        [
            ("spec", spec_any, spec),
            ("planes", planes_any, planes),
            ("rim", rim_own_any, rim_own),
            ("rim", rim_other_any, rim_other),
            ("acc", acc_any, acc.at[:, :, :, pl.ds(0, tile_rows), :]),
            ("acc", probe_acc_any, probe_acc),
            ("rest", probe_any, probe),
            ("rest", amp_any, amp),
        ],
        sems,
    )
    tables = (la, ra, lf, rf)
    zero_rows(acc, tile_rows, edge)
    fill_corners(corner, mine)
    total = put_in_order(order, own_marks(mine, meta[0], edge, tile_rows)[1])
    lay_patches(wide, wait, spec, (rim_own, rim_other), meta[1])
    wait("planes")
    lay_tables(planes, tables)
    wait("acc")
    wait("rest")
    refs = (corner, probe, amp, tables, wide, acc, probe_acc)
    run_pairs(order, total, meta[0], refs, (work[:5], work[5:]))


def late_kernel(
    meta,
    mine,
    across,
    probe_any,
    spec_any,
    rim_own_any,
    rim_other_any,
    acc_any,
    probe_acc_any,
    amp_any,
    across_amp_any,
    planes_any,
    send_first,
    send_rows,
    keep_rim,
    keep_low,
    keep_top,
    keep_probe,
    order,
    corner,
    sems,
    probe,
    spec,
    amp,
    planes,
    la,
    ra,
    lf,
    rf,
    wide,
    rim_own,
    rim_other,
    acc,
    probe_acc,
    *work,
):
    tile_rows, width = spec.shape[2:]
    edge = probe.shape[1]
    slots = mine.shape[0] - 1
    wait = fetch(
        [
            ("spec", spec_any, spec),
            ("planes", planes_any, planes),
            ("rim", rim_own_any, rim_own),
            ("rim", rim_other_any, rim_other),
            ("acc", acc_any, acc),
            ("acc", probe_acc_any, probe_acc),
            ("rest", probe_any, probe),
            ("rest", amp_any, amp.at[pl.ds(0, slots)]),
            ("rest", across_amp_any, amp.at[pl.ds(slots, slots)]),
        ],
        sems,
    )
    tables = (la, ra, lf, rf)
    half = meta[1]
    other = 1 - half
    col_tiles = width // LANES
    total = list_late(order, corner, mine, across, meta[0], edge, tile_rows)
    lay_patches(wide, wait, spec, (rim_own, rim_other), half)
    wait("planes")
    lay_tables(planes, tables)
    wait("acc")
    wait("rest")
    refs = (corner, probe, amp, tables, wide, acc, probe_acc)
    run_pairs(order, total, meta[0], refs, (work[:5], work[5:]))

    below = pl.ds(tile_rows, edge)
    low = pl.ds(edge, tile_rows - edge)
    top = pl.ds(0, edge)
    rows = pl.ds(0, tile_rows)
    for part in range(2):
        sign = 1.0 if part == 0 else -1.0
        for t in range(col_tiles):
            cols = pl.ds(t * LANES, LANES)
            send_first[pl.ds(part * edge, edge), cols] = (
                sign * acc[part, other, t, below, :]
            ).astype(jnp.bfloat16)
            send_rows[part, :, cols] = (sign * acc[part, other, t, rows, :]).astype(jnp.bfloat16)
            keep_rim[part, :, cols] = sign * acc[part, half, t, below, :]
            keep_low[part, :, cols] = sign * acc[part, half, t, low, :]
            keep_top[part, :, cols] = sign * acc[part, half, t, top, :]
    deep = keep_probe.shape[0]
    flip = jnp.where(other == 1, -1.0, 1.0)
    for piece in range(width // edge):
        piece_rows, cols = pl.ds(piece * deep, deep), pl.ds(piece * edge, edge)
        send_first[pl.ds(2 * edge, deep), cols] = (flip * probe_acc[other, piece_rows, :]).astype(
            jnp.bfloat16
        )
        keep_probe[:, cols] = -flip * probe_acc[half, piece_rows, :]


VMEM = pl.BlockSpec(memory_space=pltpu.VMEM)
SMEM = pl.BlockSpec(memory_space=pltpu.SMEM)
ANY = pl.BlockSpec(memory_space=pl.ANY)


def scratch(entries, slices, width, tile_rows, rows, edge, copies):
    planes = pltpu.VMEM((2, edge, edge), jnp.float32)
    table = pltpu.VMEM((2 * edge, 2 * edge), jnp.bfloat16)
    stack = pltpu.VMEM((2 * edge, edge), jnp.bfloat16)
    joined = pltpu.VMEM((edge, 2 * edge), jnp.bfloat16)
    lead = [
        pltpu.SMEM((entries + 1,), jnp.int32),
        pltpu.SMEM((entries, 2), jnp.int32),
        pltpu.SemaphoreType.DMA((copies,)),
        planes,
        pltpu.VMEM((2, slices, tile_rows, width), jnp.bfloat16),
        pltpu.VMEM((entries, edge, edge), jnp.bfloat16),
        pltpu.VMEM((6, edge, edge), jnp.bfloat16),
        table,
        table,
        table,
        table,
        pltpu.VMEM((2, slices, width // LANES, rows, LANES), jnp.float32),
    ]
    return lead, [planes, planes, planes, stack, joined] * 2


def run_early(meta, mine, probe, spec, amp, planes):
    edge = probe.shape[1]
    _, slices, tile_rows, width = spec.shape
    lead, work = scratch(amp.shape[0], slices, width, tile_rows, tile_rows, edge, 4)
    return pl.pallas_call(
        early_kernel,
        out_shape=(
            jax.ShapeDtypeStruct((2, slices, width // LANES, tile_rows, LANES), jnp.float32),
            jax.ShapeDtypeStruct((2, edge, edge), jnp.float32),
        ),
        in_specs=[SMEM] * 2 + [ANY] * 4,
        out_specs=(VMEM, VMEM),
        scratch_shapes=lead + work,
        compiler_params=pltpu.CompilerParams(vmem_limit_bytes=24 * 1024 * 1024),
        name="early_slots",
    )(meta, mine, probe, spec, amp, planes)


def run_middle(meta, mine, probe, spec, rims, accs, amp, planes):
    edge = probe.shape[1]
    _, slices, tile_rows, width = spec.shape
    total = tile_rows + edge
    operands = (probe, spec, *rims, *accs, amp, planes)
    lead, work = scratch(amp.shape[0], slices, width, tile_rows, total, edge, len(operands))
    rim = pltpu.VMEM((2, 1, edge, width), jnp.bfloat16)
    return pl.pallas_call(
        middle_kernel,
        out_shape=(
            jax.ShapeDtypeStruct((2, slices, width // LANES, total, LANES), jnp.float32),
            jax.ShapeDtypeStruct((2, edge, edge), jnp.float32),
        ),
        in_specs=[SMEM] * 2 + [ANY] * len(operands),
        out_specs=(VMEM, VMEM),
        scratch_shapes=lead + [rim, rim] + work,
        compiler_params=pltpu.CompilerParams(vmem_limit_bytes=30 * 1024 * 1024),
        name="middle_slots",
    )(meta, mine, *operands)


def run_late(meta, lists, probe, spec, rims, accs, amps, planes):
    edge = probe.shape[1]
    _, slices, tile_rows, width = spec.shape
    total = tile_rows + edge
    deep = edge * edge // width
    operands = (probe, spec, *rims, *accs, *amps, planes)
    entries = sum(amp.shape[0] for amp in amps)
    lead, work = scratch(entries, slices, width, tile_rows, total, edge, len(operands))
    rim = pltpu.VMEM((2, 1, edge, width), jnp.bfloat16)
    return pl.pallas_call(
        late_kernel,
        out_shape=(
            jax.ShapeDtypeStruct((2 * edge + deep, width), jnp.bfloat16),
            jax.ShapeDtypeStruct((2, tile_rows, width), jnp.bfloat16),
            jax.ShapeDtypeStruct((2, edge, width), jnp.float32),
            jax.ShapeDtypeStruct((2, tile_rows - edge, width), jnp.float32),
            jax.ShapeDtypeStruct((2, edge, width), jnp.float32),
            jax.ShapeDtypeStruct((deep, width), jnp.float32),
        ),
        in_specs=[SMEM] * 3 + [ANY] * len(operands),
        out_specs=(VMEM,) * 6,
        scratch_shapes=lead
        + [
            rim,
            rim,
            pltpu.VMEM((2, slices, width // LANES, total, LANES), jnp.float32),
            pltpu.VMEM((2, edge, edge), jnp.float32),
        ]
        + work,
        compiler_params=pltpu.CompilerParams(vmem_limit_bytes=32 * 1024 * 1024),
        name="late_slots",
    )(meta, *lists, *operands)


def write_rows(meta, own, theirs, start, shape, base=None):
    slices, rows, width = shape[1], own.shape[1], own.shape[2]

    def kernel(meta, own, theirs, *rest):
        out, wide, sems = rest[-3:]
        half = meta[1]
        copies = []
        for s, source in ((half, own), (1 - half, theirs)):
            for part in range(2):
                wide[s, part] = source[part].astype(jnp.float32)
                copy = pltpu.make_async_copy(
                    wide.at[s, part],
                    out.at[part, s, pl.ds(start, rows), :],
                    sems.at[len(copies)],
                )
                copy.start()
                copies.append(copy)
        for copy in copies:
            copy.wait()

    extra = [] if base is None else [base]
    return pl.pallas_call(
        kernel,
        out_shape=jax.ShapeDtypeStruct(shape, jnp.float32),
        in_specs=[SMEM, VMEM, VMEM] + [ANY] * len(extra),
        out_specs=ANY,
        input_output_aliases={} if base is None else {3: 0},
        scratch_shapes=[
            pltpu.VMEM((slices, 2, rows, width), jnp.float32),
            pltpu.SemaphoreType.DMA((2 * slices,)),
        ],
        compiler_params=pltpu.CompilerParams(vmem_limit_bytes=16 * 1024 * 1024),
        cost_estimate=pl.CostEstimate(
            flops=0, bytes_accessed=2 * slices * rows * width * 6, transcendentals=0
        ),
        name="write_rows",
    )(meta, own, theirs, *extra)


def traded(value, axis, distance):
    count = lax.axis_size(axis)
    return lax.ppermute(value, axis, [(i, i ^ distance) for i in range(count)])


def passed_along(value, axis, steps):
    count = lax.axis_size(axis)
    initial, last = (max(0, -steps), min(count, count - steps))
    return lax.ppermute(value, axis, [(source, source + steps) for source in range(initial, last)])


def narrow_sum(own, got):
    return (own.astype(jnp.float32) + got.astype(jnp.float32)).astype(jnp.bfloat16)


def unfolded(value, edge):
    return jnp.concatenate([value[:, k : k + edge] for k in range(0, value.shape[1], edge)], 0)


def body(probe_field, specimen, amplitude, scan_anchor, counts):
    edge = probe_field.shape[1]
    _, slices, tile_rows, width = specimen.shape
    half = lax.axis_index("pos") % 2
    base_row = lax.axis_index("tile") * tile_rows
    meta = jnp.stack([base_row, half]).astype(jnp.int32)
    planes = fixed_tables(edge)
    rim_own = passed_along(
        lax.dynamic_slice(specimen, (0, half, 0, 0), (2, 1, edge, width)), "tile", -1
    )
    across_amp = traded(amplitude, "pos", 2)
    mine = jnp.concatenate([scan_anchor, jnp.broadcast_to(counts, (1, 2))], 0)
    across = traded(mine, "pos", 2)
    accs = run_early(meta, mine, probe_field, specimen, amplitude, planes)
    rim_own, accs = lax.optimization_barrier((rim_own, accs))
    rims = (rim_own, traded(rim_own, "pos", 1))
    accs = run_middle(meta, mine, probe_field, specimen, rims, accs, amplitude, planes)
    sent_first, sent_rows, kept_rim, kept_low, kept_top, kept_probe = run_late(
        meta,
        (mine, across),
        probe_field,
        specimen,
        rims,
        accs,
        (amplitude, across_amp),
        planes,
    )
    got_first = traded(sent_first, "pos", 1)
    got_first, sent_rows = lax.optimization_barrier((got_first, sent_rows))
    got_rows = traded(sent_rows, "pos", 1)
    below = kept_rim + got_first[: 2 * edge].reshape(kept_rim.shape).astype(jnp.float32)
    below = passed_along(below.astype(jnp.bfloat16), "tile", 1)
    probe_part = (kept_probe + got_first[2 * edge :].astype(jnp.float32)).astype(jnp.bfloat16)
    distance = lax.axis_size("tile")
    while distance > 1:
        distance //= 2
        probe_part = narrow_sum(probe_part, traded(probe_part, "tile", distance))
    lower = (kept_low + got_rows[:, edge:].astype(jnp.float32)).astype(jnp.bfloat16)
    tile_grad = write_rows(meta, lower, traded(lower, "pos", 1), edge, specimen.shape)
    top = kept_top + got_rows[:, :edge].astype(jnp.float32)
    below, top, tile_grad = lax.optimization_barrier((below, top, tile_grad))
    upper = (top + below.astype(jnp.float32)).astype(jnp.bfloat16)
    tile_grad = write_rows(meta, upper, traded(upper, "pos", 1), 0, specimen.shape, tile_grad)
    probe_theirs, tile_grad = lax.optimization_barrier((traded(probe_part, "pos", 1), tile_grad))
    probe_own, probe_theirs = [unfolded(value, edge) for value in (probe_part, probe_theirs)]
    probe_total = jnp.where(
        half == 0, jnp.stack([probe_own, probe_theirs]), jnp.stack([probe_theirs, probe_own])
    ).astype(jnp.float32)
    return (tile_grad, probe_total)


def solution(mesh):
    return jax.shard_map(
        body,
        mesh=mesh,
        in_specs=(
            P(),
            P(None, None, "tile", None),
            P(("tile", "pos"), None, None),
            P(("tile", "pos"), None),
            P(("tile", "pos")),
        ),
        out_specs=(P(None, None, "tile", None), P()),
        check_vma=False,
    )
```

```python
import math

import jax
import jax.numpy as jnp
import ml_dtypes
import numpy as np
from jax import lax
from jax.experimental import pallas as pl
from jax.experimental.pallas import tpu as pltpu
from jax.sharding import PartitionSpec as P

PROP_COEF = 0.5
AMP_EPS = 0.05
LANES = 128
CHUNK = 32
EARLY = 4
MIDDLE = 4


def fixed_tables(edge):
    index = np.arange(edge)
    angles = (np.outer(index, index) % edge) * (2.0 * math.pi / edge)
    cosine = (np.cos(angles) / math.sqrt(edge)).astype(ml_dtypes.bfloat16).astype(np.float64)
    sine = (np.sin(angles) / math.sqrt(edge)).astype(ml_dtypes.bfloat16).astype(np.float64)
    forward = cosine - 1j * sine
    centred = np.where(index < edge // 2, index, index - edge)
    ramp = np.exp(-1j * (PROP_COEF * math.pi / edge) * centred * centred)
    spread = (np.conj(forward) * ramp[None, :]) @ forward
    planes = [
        plane for matrix in (spread, forward) for plane in (matrix.real, matrix.imag, -matrix.imag)
    ]
    return jnp.asarray(np.stack(planes).astype(ml_dtypes.bfloat16))


def lay_tables(planes, tables):
    edge = planes.shape[1]
    lo, hi = pl.ds(0, edge), pl.ds(edge, edge)
    for k in range(2):
        real, imag, negated = (planes[3 * k + i] for i in range(3))
        left, right = tables[2 * k : 2 * k + 2]
        left[lo, lo], left[lo, hi], left[hi, lo], left[hi, hi] = real, negated, imag, real
        right[lo, lo], right[lo, hi], right[hi, lo], right[hi, hi] = real, imag, negated, real


def interleaved(first, second):
    marks = [(k / len(first), 0, k) for k in range(len(first))]
    marks += [((k + 0.5) / len(second), 1, k) for k in range(len(second))]
    for _, which, k in sorted(marks):
        (first, second)[which][k]()


def slot_stages(slot, alive, base_row, refs, work):
    corner, probe, amp, tables, wide, acc, probe_acc = refs
    rolled, arriving, field, stack, joined = work
    left_a, right_a, left_f, right_f = tables
    edge = probe.shape[1]
    col_tiles = wide.shape[2]
    parts = edge // LANES
    lane = lax.broadcasted_iota(jnp.int32, (CHUNK, LANES), 1)
    row = corner[slot, 0] - base_row
    col = corner[slot, 1]
    first = jnp.minimum(col // LANES, col_tiles - parts - 1)
    shift = col - first * LANES
    turn = jnp.where(shift >= LANES, 0, shift)
    back = jnp.where(turn == 0, 0, LANES - turn)
    own = lane >= shift
    near = lane < LANES - shift

    def patch(part, s, i, j):
        rows = pl.ds(row + i, CHUNK)
        main = wide[part, s, first + j, rows, :]
        if j > 0:
            return main
        return jnp.where(own, main, wide[part, s, first + parts, rows, :])

    def place(part, s, i, j, value):
        rows = pl.ds(row + i, CHUNK)
        if j > 0:
            acc[part, s, first + j, rows, :] += value
        else:
            acc[part, s, first, rows, :] += jnp.where(own, value, 0.0)
            acc[part, s, first + parts, rows, :] += jnp.where(own, 0.0, value)

    def put(i, j, re, im):
        cols = pl.ds(j * LANES, LANES)
        stack[pl.ds(i, CHUNK), cols] = re.astype(jnp.bfloat16)
        stack[pl.ds(edge + i, CHUNK), cols] = im.astype(jnp.bfloat16)

    def halves():
        return [(j, pl.ds(j * LANES, LANES)) for j in range(parts)]

    def enter(i):
        rows = pl.ds(i, CHUNK)
        turned = [
            [pltpu.roll(probe[part, rows, cols], turn, 1) for j, cols in halves()]
            for part in range(2)
        ]
        for j, cols in halves():
            u_re, u_im = [
                jnp.where(own, turned[part][j], turned[part][j - 1]) for part in range(2)
            ]
            rolled[0, rows, cols] = u_re
            rolled[1, rows, cols] = u_im
            o_re, o_im = patch(0, 0, i, j), patch(1, 0, i, j)
            put(i, j, u_re * o_re - u_im * o_im, u_re * o_im + u_im * o_re)

    def second_slice(i):
        rows = pl.ds(i, CHUNK)
        for j, cols in halves():
            u_re, u_im = arriving[0, rows, cols], arriving[1, rows, cols]
            o_re, o_im = patch(0, 1, i, j), patch(1, 1, i, j)
            put(i, j, u_re * o_re - u_im * o_im, u_re * o_im + u_im * o_re)

    def residual(i):
        rows = pl.ds(i, CHUNK)
        for j, cols in halves():
            far_re, far_im = field[0, rows, cols], field[1, rows, cols]
            measured = amp[slot, rows, cols].astype(jnp.float32) * alive
            ratio = measured * lax.rsqrt(far_re * far_re + far_im * far_im + AMP_EPS)
            put(i, j, (alive - ratio) * far_re, (ratio - alive) * far_im)

    def second_grad(i):
        rows = pl.ds(i, CHUNK)
        for j, cols in halves():
            u_re, u_im = arriving[0, rows, cols], arriving[1, rows, cols]
            w_re, w_im = field[0, rows, cols], field[1, rows, cols]
            place(0, 1, i, j, u_re * w_re - u_im * w_im)
            place(1, 1, i, j, u_re * w_im + u_im * w_re)
            o_re, o_im = patch(0, 1, i, j), patch(1, 1, i, j)
            put(i, j, o_re * w_re - o_im * w_im, o_re * w_im + o_im * w_re)

    def first_grad(i):
        rows = pl.ds(i, CHUNK)
        turned = [[None] * parts for _ in range(2)]
        for j, cols in halves():
            u_re, u_im = rolled[0, rows, cols], rolled[1, rows, cols]
            w_re, w_im = field[0, rows, cols], field[1, rows, cols]
            place(0, 0, i, j, u_re * w_re - u_im * w_im)
            place(1, 0, i, j, u_re * w_im + u_im * w_re)
            o_re, o_im = patch(0, 0, i, j), patch(1, 0, i, j)
            turned[0][j] = pltpu.roll(o_re * w_re - o_im * w_im, back, 1)
            turned[1][j] = pltpu.roll(o_re * w_im + o_im * w_re, back, 1)
        for part in range(2):
            for j, cols in halves():
                after = turned[part][(j + 1) % parts]
                probe_acc[part, rows, cols] += jnp.where(near, turned[part][j], after)

    def two_sided(left, right, out):
        def rows_of(part):
            span = pl.ds(part * edge, edge)
            joined[:, span] = jnp.dot(
                left[span, :], stack[...], preferred_element_type=jnp.float32
            ).astype(jnp.bfloat16)

        def cols_of(part):
            out[part] = jnp.dot(
                joined[...],
                right[:, pl.ds(part * edge, edge)],
                preferred_element_type=jnp.float32,
            )

        return [lambda p=p: rows_of(p) for p in range(2)] + [
            lambda p=p: cols_of(p) for p in range(2)
        ]

    def each(step):
        return [lambda i=i: step(i) for i in range(0, edge, CHUNK)]

    return [
        each(enter),
        two_sided(left_a, right_a, arriving),
        each(second_slice),
        two_sided(left_f, right_f, field),
        each(residual),
        two_sided(left_f, right_f, field),
        each(second_grad),
        two_sided(left_a, right_a, field),
        each(first_grad),
    ]


def own_marks(part, base_row, edge, tile_rows):
    slots = part.shape[0] - 1
    first, second, left = [], [], []
    ranks = [jnp.int32(0), jnp.int32(0)]
    for q in range(slots):
        live = jnp.where(q < part[slots, 0], 1, 0)
        inner = jnp.where(part[q, 0] - base_row + edge <= tile_rows, live, 0)
        first.append(jnp.where(ranks[0] < EARLY, inner, 0))
        ranks[0] = ranks[0] + inner
        rest = live - first[q]
        second.append(jnp.where(ranks[1] < MIDDLE, rest, 0))
        ranks[1] = ranks[1] + rest
        left.append(rest - second[q])
    return first, second, left


def put_in_order(order, marks):
    taken = jnp.int32(0)
    order[0] = 0
    for q, mark in enumerate(marks):
        order[taken] = q
        taken = taken + mark
    return taken


def fill_corners(corner, part):
    for q in range(part.shape[0] - 1):
        corner[q, 0] = part[q, 0]
        corner[q, 1] = part[q, 1]


def list_late(order, corner, mine, across, base_row, edge, tile_rows):
    slots = mine.shape[0] - 1
    fill_corners(corner, mine)
    marks = own_marks(mine, base_row, edge, tile_rows)[2]
    for q in range(slots):
        corner[slots + q, 0] = across[q, 0]
        corner[slots + q, 1] = across[q, 1]
        marks.append(jnp.where(q < across[slots, 0], 1, 0))
    return put_in_order(order, marks)


def run_pairs(order, total, base_row, refs, work):
    def visit(step, carry):
        a = order[2 * step]
        b_lives = 2 * step + 1 < total
        b = jnp.where(b_lives, order[2 * step + 1], a)
        ones = slot_stages(a, 1.0, base_row, refs, work[0])
        twos = slot_stages(b, jnp.where(b_lives, 1.0, 0.0), base_row, refs, work[1])
        for step_now in ones[0]:
            step_now()
        for k in range(1, len(ones)):
            if k % 2:
                interleaved(ones[k], twos[k - 1])
            else:
                interleaved(twos[k - 1], ones[k])
        for step_now in twos[-1]:
            step_now()
        return carry

    lax.fori_loop(0, (total + 1) // 2, visit, 0)


def widen(wide, source, start, part, s_from, s_to):
    rows = source.shape[-2]
    for t in range(wide.shape[2]):
        wide[part, s_to, t, pl.ds(start, rows), :] = source[
            part, s_from, :, pl.ds(t * LANES, LANES)
        ].astype(jnp.float32)


def fetch(copies, sems):
    started = {}
    for k, (group, source, target) in enumerate(copies):
        copy = pltpu.make_async_copy(source, target, sems.at[k])
        copy.start()
        started.setdefault(group, []).append(copy)

    def wait(group):
        for copy in started[group]:
            copy.wait()

    return wait


def zero_rows(acc, start, rows):
    for part in range(2):
        for s in range(acc.shape[1]):
            for t in range(acc.shape[2]):
                acc[part, s, t, pl.ds(start, rows), :] = jnp.zeros((rows, LANES), jnp.float32)


def lay_patches(wide, wait, spec, rims, half):
    slices, tile_rows = spec.shape[1:3]
    wait("spec")
    for part in range(2):
        for s in range(slices):
            widen(wide, spec, 0, part, s, s)
    if rims:
        wait("rim")
        for part in range(2):
            widen(wide, rims[0], tile_rows, part, 0, half)
            widen(wide, rims[1], tile_rows, part, 0, 1 - half)


def early_kernel(
    meta,
    mine,
    probe_any,
    spec_any,
    amp_any,
    planes_any,
    acc,
    probe_acc,
    order,
    corner,
    sems,
    probe,
    spec,
    amp,
    planes,
    la,
    ra,
    lf,
    rf,
    wide,
    *work,
):
    wait = fetch(
        [
            ("spec", spec_any, spec),
            ("planes", planes_any, planes),
            ("rest", probe_any, probe),
            ("rest", amp_any, amp),
        ],
        sems,
    )
    tables = (la, ra, lf, rf)
    edge, tile_rows = probe.shape[1], spec.shape[2]
    zero_rows(acc, 0, tile_rows)
    probe_acc[...] = jnp.zeros(probe_acc.shape, jnp.float32)
    fill_corners(corner, mine)
    total = put_in_order(order, own_marks(mine, meta[0], edge, tile_rows)[0])
    lay_patches(wide, wait, spec, (), meta[1])
    wait("planes")
    lay_tables(planes, tables)
    wait("rest")
    refs = (corner, probe, amp, tables, wide, acc, probe_acc)
    run_pairs(order, total, meta[0], refs, (work[:5], work[5:]))


def middle_kernel(
    meta,
    mine,
    probe_any,
    spec_any,
    rim_own_any,
    rim_other_any,
    acc_any,
    probe_acc_any,
    amp_any,
    planes_any,
    acc,
    probe_acc,
    order,
    corner,
    sems,
    probe,
    spec,
    amp,
    planes,
    la,
    ra,
    lf,
    rf,
    wide,
    rim_own,
    rim_other,
    *work,
):
    edge, tile_rows = probe.shape[1], spec.shape[2]
    wait = fetch(
        [
            ("spec", spec_any, spec),
            ("planes", planes_any, planes),
            ("rim", rim_own_any, rim_own),
            ("rim", rim_other_any, rim_other),
            ("acc", acc_any, acc.at[:, :, :, pl.ds(0, tile_rows), :]),
            ("acc", probe_acc_any, probe_acc),
            ("rest", probe_any, probe),
            ("rest", amp_any, amp),
        ],
        sems,
    )
    tables = (la, ra, lf, rf)
    zero_rows(acc, tile_rows, edge)
    fill_corners(corner, mine)
    total = put_in_order(order, own_marks(mine, meta[0], edge, tile_rows)[1])
    lay_patches(wide, wait, spec, (rim_own, rim_other), meta[1])
    wait("planes")
    lay_tables(planes, tables)
    wait("acc")
    wait("rest")
    refs = (corner, probe, amp, tables, wide, acc, probe_acc)
    run_pairs(order, total, meta[0], refs, (work[:5], work[5:]))


def late_kernel(
    meta,
    mine,
    across,
    probe_any,
    spec_any,
    rim_own_any,
    rim_other_any,
    acc_any,
    probe_acc_any,
    amp_any,
    across_amp_any,
    planes_any,
    send_first,
    send_rows,
    keep_rim,
    keep_low,
    keep_top,
    keep_probe,
    order,
    corner,
    sems,
    probe,
    spec,
    amp,
    planes,
    la,
    ra,
    lf,
    rf,
    wide,
    rim_own,
    rim_other,
    acc,
    probe_acc,
    *work,
):
    tile_rows, width = spec.shape[2:]
    edge = probe.shape[1]
    slots = mine.shape[0] - 1
    wait = fetch(
        [
            ("spec", spec_any, spec),
            ("planes", planes_any, planes),
            ("rim", rim_own_any, rim_own),
            ("rim", rim_other_any, rim_other),
            ("acc", acc_any, acc),
            ("acc", probe_acc_any, probe_acc),
            ("rest", probe_any, probe),
            ("rest", amp_any, amp.at[pl.ds(0, slots)]),
            ("rest", across_amp_any, amp.at[pl.ds(slots, slots)]),
        ],
        sems,
    )
    tables = (la, ra, lf, rf)
    half = meta[1]
    other = 1 - half
    col_tiles = width // LANES
    total = list_late(order, corner, mine, across, meta[0], edge, tile_rows)
    lay_patches(wide, wait, spec, (rim_own, rim_other), half)
    wait("planes")
    lay_tables(planes, tables)
    wait("acc")
    wait("rest")
    refs = (corner, probe, amp, tables, wide, acc, probe_acc)
    run_pairs(order, total, meta[0], refs, (work[:5], work[5:]))

    below = pl.ds(tile_rows, edge)
    low = pl.ds(edge, tile_rows - edge)
    top = pl.ds(0, edge)
    rows = pl.ds(0, tile_rows)
    for part in range(2):
        sign = 1.0 if part == 0 else -1.0
        for t in range(col_tiles):
            cols = pl.ds(t * LANES, LANES)
            send_first[pl.ds(part * edge, edge), cols] = (
                sign * acc[part, other, t, below, :]
            ).astype(jnp.bfloat16)
            send_rows[part, :, cols] = (sign * acc[part, other, t, rows, :]).astype(jnp.bfloat16)
            keep_rim[part, :, cols] = sign * acc[part, half, t, below, :]
            keep_low[part, :, cols] = sign * acc[part, half, t, low, :]
            keep_top[part, :, cols] = sign * acc[part, half, t, top, :]
    deep = keep_probe.shape[0]
    flip = jnp.where(other == 1, -1.0, 1.0)
    for piece in range(width // edge):
        piece_rows, cols = pl.ds(piece * deep, deep), pl.ds(piece * edge, edge)
        send_first[pl.ds(2 * edge, deep), cols] = (flip * probe_acc[other, piece_rows, :]).astype(
            jnp.bfloat16
        )
        keep_probe[:, cols] = -flip * probe_acc[half, piece_rows, :]


VMEM = pl.BlockSpec(memory_space=pltpu.VMEM)
SMEM = pl.BlockSpec(memory_space=pltpu.SMEM)
ANY = pl.BlockSpec(memory_space=pl.ANY)


def scratch(entries, slices, width, tile_rows, rows, edge, copies):
    planes = pltpu.VMEM((2, edge, edge), jnp.float32)
    table = pltpu.VMEM((2 * edge, 2 * edge), jnp.bfloat16)
    stack = pltpu.VMEM((2 * edge, edge), jnp.bfloat16)
    joined = pltpu.VMEM((edge, 2 * edge), jnp.bfloat16)
    lead = [
        pltpu.SMEM((entries + 1,), jnp.int32),
        pltpu.SMEM((entries, 2), jnp.int32),
        pltpu.SemaphoreType.DMA((copies,)),
        planes,
        pltpu.VMEM((2, slices, tile_rows, width), jnp.bfloat16),
        pltpu.VMEM((entries, edge, edge), jnp.bfloat16),
        pltpu.VMEM((6, edge, edge), jnp.bfloat16),
        table,
        table,
        table,
        table,
        pltpu.VMEM((2, slices, width // LANES, rows, LANES), jnp.float32),
    ]
    return lead, [planes, planes, planes, stack, joined] * 2


def run_early(meta, mine, probe, spec, amp, planes):
    edge = probe.shape[1]
    _, slices, tile_rows, width = spec.shape
    lead, work = scratch(amp.shape[0], slices, width, tile_rows, tile_rows, edge, 4)
    return pl.pallas_call(
        early_kernel,
        out_shape=(
            jax.ShapeDtypeStruct((2, slices, width // LANES, tile_rows, LANES), jnp.float32),
            jax.ShapeDtypeStruct((2, edge, edge), jnp.float32),
        ),
        in_specs=[SMEM] * 2 + [ANY] * 4,
        out_specs=(VMEM, VMEM),
        scratch_shapes=lead + work,
        compiler_params=pltpu.CompilerParams(vmem_limit_bytes=24 * 1024 * 1024),
        name="early_slots",
    )(meta, mine, probe, spec, amp, planes)


def run_middle(meta, mine, probe, spec, rims, accs, amp, planes):
    edge = probe.shape[1]
    _, slices, tile_rows, width = spec.shape
    total = tile_rows + edge
    operands = (probe, spec, *rims, *accs, amp, planes)
    lead, work = scratch(amp.shape[0], slices, width, tile_rows, total, edge, len(operands))
    rim = pltpu.VMEM((2, 1, edge, width), jnp.bfloat16)
    return pl.pallas_call(
        middle_kernel,
        out_shape=(
            jax.ShapeDtypeStruct((2, slices, width // LANES, total, LANES), jnp.float32),
            jax.ShapeDtypeStruct((2, edge, edge), jnp.float32),
        ),
        in_specs=[SMEM] * 2 + [ANY] * len(operands),
        out_specs=(VMEM, VMEM),
        scratch_shapes=lead + [rim, rim] + work,
        compiler_params=pltpu.CompilerParams(vmem_limit_bytes=30 * 1024 * 1024),
        name="middle_slots",
    )(meta, mine, *operands)


def run_late(meta, lists, probe, spec, rims, accs, amps, planes):
    edge = probe.shape[1]
    _, slices, tile_rows, width = spec.shape
    total = tile_rows + edge
    deep = edge * edge // width
    operands = (probe, spec, *rims, *accs, *amps, planes)
    entries = sum(amp.shape[0] for amp in amps)
    lead, work = scratch(entries, slices, width, tile_rows, total, edge, len(operands))
    rim = pltpu.VMEM((2, 1, edge, width), jnp.bfloat16)
    return pl.pallas_call(
        late_kernel,
        out_shape=(
            jax.ShapeDtypeStruct((2 * edge + deep, width), jnp.bfloat16),
            jax.ShapeDtypeStruct((2, tile_rows, width), jnp.bfloat16),
            jax.ShapeDtypeStruct((2, edge, width), jnp.float32),
            jax.ShapeDtypeStruct((2, tile_rows - edge, width), jnp.float32),
            jax.ShapeDtypeStruct((2, edge, width), jnp.float32),
            jax.ShapeDtypeStruct((deep, width), jnp.float32),
        ),
        in_specs=[SMEM] * 3 + [ANY] * len(operands),
        out_specs=(VMEM,) * 6,
        scratch_shapes=lead
        + [
            rim,
            rim,
            pltpu.VMEM((2, slices, width // LANES, total, LANES), jnp.float32),
            pltpu.VMEM((2, edge, edge), jnp.float32),
        ]
        + work,
        compiler_params=pltpu.CompilerParams(vmem_limit_bytes=32 * 1024 * 1024),
        name="late_slots",
    )(meta, *lists, *operands)


def write_rows(meta, own, theirs, start, shape, base=None):
    slices, rows, width = shape[1], own.shape[1], own.shape[2]

    def kernel(meta, own, theirs, *rest):
        out, wide, sems = rest[-3:]
        half = meta[1]
        copies = []
        for s, source in ((half, own), (1 - half, theirs)):
            for part in range(2):
                wide[s, part] = source[part].astype(jnp.float32)
                copy = pltpu.make_async_copy(
                    wide.at[s, part],
                    out.at[part, s, pl.ds(start, rows), :],
                    sems.at[len(copies)],
                )
                copy.start()
                copies.append(copy)
        for copy in copies:
            copy.wait()

    extra = [] if base is None else [base]
    return pl.pallas_call(
        kernel,
        out_shape=jax.ShapeDtypeStruct(shape, jnp.float32),
        in_specs=[SMEM, VMEM, VMEM] + [ANY] * len(extra),
        out_specs=ANY,
        input_output_aliases={} if base is None else {3: 0},
        scratch_shapes=[
            pltpu.VMEM((slices, 2, rows, width), jnp.float32),
            pltpu.SemaphoreType.DMA((2 * slices,)),
        ],
        compiler_params=pltpu.CompilerParams(vmem_limit_bytes=16 * 1024 * 1024),
        cost_estimate=pl.CostEstimate(
            flops=0, bytes_accessed=2 * slices * rows * width * 6, transcendentals=0
        ),
        name="write_rows",
    )(meta, own, theirs, *extra)


def sum_rows(kept, got):
    def kernel(kept, got, out):
        out[...] = kept[...] + got[:, pl.ds(0, kept.shape[1]), :].astype(jnp.float32)

    return pl.pallas_call(
        kernel,
        out_shape=jax.ShapeDtypeStruct(kept.shape, jnp.float32),
        in_specs=[VMEM, VMEM],
        out_specs=VMEM,
        compiler_params=pltpu.CompilerParams(vmem_limit_bytes=8 * 1024 * 1024),
        name="sum_rows",
    )(kept, got)


def traded(value, axis, distance):
    count = lax.axis_size(axis)
    return lax.ppermute(value, axis, [(i, i ^ distance) for i in range(count)])


def passed_along(value, axis, steps):
    count = lax.axis_size(axis)
    initial, last = (max(0, -steps), min(count, count - steps))
    return lax.ppermute(value, axis, [(source, source + steps) for source in range(initial, last)])


def narrow_sum(own, got):
    return (own.astype(jnp.float32) + got.astype(jnp.float32)).astype(jnp.bfloat16)


def unfolded(value, edge):
    return jnp.concatenate([value[:, k : k + edge] for k in range(0, value.shape[1], edge)], 0)


def body(probe_field, specimen, amplitude, scan_anchor, counts):
    edge = probe_field.shape[1]
    _, slices, tile_rows, width = specimen.shape
    half = lax.axis_index("pos") % 2
    base_row = lax.axis_index("tile") * tile_rows
    meta = jnp.stack([base_row, half]).astype(jnp.int32)
    planes = fixed_tables(edge)
    rim_own = passed_along(
        lax.dynamic_slice(specimen, (0, half, 0, 0), (2, 1, edge, width)), "tile", -1
    )
    across_amp = traded(amplitude, "pos", 2)
    mine = jnp.concatenate([scan_anchor, jnp.broadcast_to(counts, (1, 2))], 0)
    across = traded(mine, "pos", 2)
    accs = run_early(meta, mine, probe_field, specimen, amplitude, planes)
    rim_own, accs = lax.optimization_barrier((rim_own, accs))
    rims = (rim_own, traded(rim_own, "pos", 1))
    accs = run_middle(meta, mine, probe_field, specimen, rims, accs, amplitude, planes)
    sent_first, sent_rows, kept_rim, kept_low, kept_top, kept_probe = run_late(
        meta,
        (mine, across),
        probe_field,
        specimen,
        rims,
        accs,
        (amplitude, across_amp),
        planes,
    )
    got_first = traded(sent_first, "pos", 1)
    got_first, sent_rows = lax.optimization_barrier((got_first, sent_rows))
    got_rows = traded(sent_rows, "pos", 1)
    below = kept_rim + got_first[: 2 * edge].reshape(kept_rim.shape).astype(jnp.float32)
    below = passed_along(below.astype(jnp.bfloat16), "tile", 1)
    probe_part = (kept_probe + got_first[2 * edge :].astype(jnp.float32)).astype(jnp.bfloat16)
    got_probe = jnp.zeros_like(probe_part)
    distance = lax.axis_size("tile")
    while distance > 4:
        distance //= 2
        probe_part = narrow_sum(probe_part, got_probe)
        got_probe = traded(probe_part, "tile", distance)
    lower = (kept_low + got_rows[:, edge:].astype(jnp.float32)).astype(jnp.bfloat16)
    tile_grad = write_rows(meta, lower, traded(lower, "pos", 1), edge, specimen.shape)
    top = sum_rows(kept_top, got_rows)
    got_probe, top, tile_grad = lax.optimization_barrier((got_probe, top, tile_grad))
    probe_part = narrow_sum(probe_part, got_probe)
    below, top, probe_part = lax.optimization_barrier((below, top, probe_part))
    upper = (top + below.astype(jnp.float32)).astype(jnp.bfloat16)
    upper_theirs = traded(upper, "pos", 1)
    near = [traded(probe_part, "tile", d).astype(jnp.float32) for d in range(1, distance)]
    probe_part = (probe_part.astype(jnp.float32) + sum(near)).astype(jnp.bfloat16)
    tile_grad = write_rows(meta, upper, upper_theirs, 0, specimen.shape, tile_grad)
    probe_theirs, tile_grad = lax.optimization_barrier((traded(probe_part, "pos", 1), tile_grad))
    probe_own, probe_theirs = [unfolded(value, edge) for value in (probe_part, probe_theirs)]
    probe_total = jnp.where(
        half == 0, jnp.stack([probe_own, probe_theirs]), jnp.stack([probe_theirs, probe_own])
    ).astype(jnp.float32)
    return (tile_grad, probe_total)


def solution(mesh):
    return jax.shard_map(
        body,
        mesh=mesh,
        in_specs=(
            P(),
            P(None, None, "tile", None),
            P(("tile", "pos"), None, None),
            P(("tile", "pos"), None),
            P(("tile", "pos")),
        ),
        out_specs=(P(None, None, "tile", None), P()),
        check_vma=False,
    )
```

```python
import math

import jax
import jax.numpy as jnp
import ml_dtypes
import numpy as np
from jax import lax
from jax.experimental import pallas as pl
from jax.experimental.pallas import tpu as pltpu
from jax.sharding import PartitionSpec as P

PROP_COEF = 0.5
AMP_EPS = 0.05
LANES = 128
CHUNK = 32
EARLY = 4
MIDDLE = 4


def fixed_tables(edge):
    index = np.arange(edge)
    angles = (np.outer(index, index) % edge) * (2.0 * math.pi / edge)
    cosine = (np.cos(angles) / math.sqrt(edge)).astype(ml_dtypes.bfloat16).astype(np.float64)
    sine = (np.sin(angles) / math.sqrt(edge)).astype(ml_dtypes.bfloat16).astype(np.float64)
    forward = cosine - 1j * sine
    centred = np.where(index < edge // 2, index, index - edge)
    ramp = np.exp(-1j * (PROP_COEF * math.pi / edge) * centred * centred)
    spread = (np.conj(forward) * ramp[None, :]) @ forward
    planes = [
        plane for matrix in (spread, forward) for plane in (matrix.real, matrix.imag, -matrix.imag)
    ]
    return jnp.asarray(np.stack(planes).astype(ml_dtypes.bfloat16))


def lay_tables(planes, tables):
    edge = planes.shape[1]
    lo, hi = pl.ds(0, edge), pl.ds(edge, edge)
    for k in range(2):
        real, imag, negated = (planes[3 * k + i] for i in range(3))
        left, right = tables[2 * k : 2 * k + 2]
        left[lo, lo], left[lo, hi], left[hi, lo], left[hi, hi] = real, negated, imag, real
        right[lo, lo], right[lo, hi], right[hi, lo], right[hi, hi] = real, imag, negated, real


def interleaved(first, second):
    marks = [(k / len(first), 0, k) for k in range(len(first))]
    marks += [((k + 0.5) / len(second), 1, k) for k in range(len(second))]
    for _, which, k in sorted(marks):
        (first, second)[which][k]()


def slot_stages(slot, alive, base_row, refs, work):
    corner, probe, amp, tables, wide, acc, probe_acc = refs
    rolled, arriving, field, stack, joined = work
    left_a, right_a, left_f, right_f = tables
    edge = probe.shape[1]
    col_tiles = wide.shape[2]
    parts = edge // LANES
    lane = lax.broadcasted_iota(jnp.int32, (CHUNK, LANES), 1)
    row = corner[slot, 0] - base_row
    col = corner[slot, 1]
    first = jnp.minimum(col // LANES, col_tiles - parts - 1)
    shift = col - first * LANES
    turn = jnp.where(shift >= LANES, 0, shift)
    back = jnp.where(turn == 0, 0, LANES - turn)
    own = lane >= shift
    near = lane < LANES - shift

    def patch(part, s, i, j):
        rows = pl.ds(row + i, CHUNK)
        main = wide[part, s, first + j, rows, :]
        if j > 0:
            return main
        return jnp.where(own, main, wide[part, s, first + parts, rows, :])

    def place(part, s, i, j, value):
        rows = pl.ds(row + i, CHUNK)
        if j > 0:
            acc[part, s, first + j, rows, :] += value
        else:
            acc[part, s, first, rows, :] += jnp.where(own, value, 0.0)
            acc[part, s, first + parts, rows, :] += jnp.where(own, 0.0, value)

    def put(i, j, re, im):
        cols = pl.ds(j * LANES, LANES)
        stack[pl.ds(i, CHUNK), cols] = re.astype(jnp.bfloat16)
        stack[pl.ds(edge + i, CHUNK), cols] = im.astype(jnp.bfloat16)

    def halves():
        return [(j, pl.ds(j * LANES, LANES)) for j in range(parts)]

    def enter(i):
        rows = pl.ds(i, CHUNK)
        turned = [
            [pltpu.roll(probe[part, rows, cols], turn, 1) for j, cols in halves()]
            for part in range(2)
        ]
        for j, cols in halves():
            u_re, u_im = [
                jnp.where(own, turned[part][j], turned[part][j - 1]) for part in range(2)
            ]
            rolled[0, rows, cols] = u_re
            rolled[1, rows, cols] = u_im
            o_re, o_im = patch(0, 0, i, j), patch(1, 0, i, j)
            put(i, j, u_re * o_re - u_im * o_im, u_re * o_im + u_im * o_re)

    def second_slice(i):
        rows = pl.ds(i, CHUNK)
        for j, cols in halves():
            u_re, u_im = arriving[0, rows, cols], arriving[1, rows, cols]
            o_re, o_im = patch(0, 1, i, j), patch(1, 1, i, j)
            put(i, j, u_re * o_re - u_im * o_im, u_re * o_im + u_im * o_re)

    def residual(i):
        rows = pl.ds(i, CHUNK)
        for j, cols in halves():
            far_re, far_im = field[0, rows, cols], field[1, rows, cols]
            measured = amp[slot, rows, cols].astype(jnp.float32) * alive
            ratio = measured * lax.rsqrt(far_re * far_re + far_im * far_im + AMP_EPS)
            put(i, j, (alive - ratio) * far_re, (ratio - alive) * far_im)

    def second_grad(i):
        rows = pl.ds(i, CHUNK)
        for j, cols in halves():
            u_re, u_im = arriving[0, rows, cols], arriving[1, rows, cols]
            w_re, w_im = field[0, rows, cols], field[1, rows, cols]
            place(0, 1, i, j, u_re * w_re - u_im * w_im)
            place(1, 1, i, j, u_re * w_im + u_im * w_re)
            o_re, o_im = patch(0, 1, i, j), patch(1, 1, i, j)
            put(i, j, o_re * w_re - o_im * w_im, o_re * w_im + o_im * w_re)

    def first_grad(i):
        rows = pl.ds(i, CHUNK)
        turned = [[None] * parts for _ in range(2)]
        for j, cols in halves():
            u_re, u_im = rolled[0, rows, cols], rolled[1, rows, cols]
            w_re, w_im = field[0, rows, cols], field[1, rows, cols]
            place(0, 0, i, j, u_re * w_re - u_im * w_im)
            place(1, 0, i, j, u_re * w_im + u_im * w_re)
            o_re, o_im = patch(0, 0, i, j), patch(1, 0, i, j)
            turned[0][j] = pltpu.roll(o_re * w_re - o_im * w_im, back, 1)
            turned[1][j] = pltpu.roll(o_re * w_im + o_im * w_re, back, 1)
        for part in range(2):
            for j, cols in halves():
                after = turned[part][(j + 1) % parts]
                probe_acc[part, rows, cols] += jnp.where(near, turned[part][j], after)

    def two_sided(left, right, out):
        def rows_of(part):
            span = pl.ds(part * edge, edge)
            joined[:, span] = jnp.dot(
                left[span, :], stack[...], preferred_element_type=jnp.float32
            ).astype(jnp.bfloat16)

        def cols_of(part):
            out[part] = jnp.dot(
                joined[...],
                right[:, pl.ds(part * edge, edge)],
                preferred_element_type=jnp.float32,
            )

        return [lambda p=p: rows_of(p) for p in range(2)] + [
            lambda p=p: cols_of(p) for p in range(2)
        ]

    def each(step):
        return [lambda i=i: step(i) for i in range(0, edge, CHUNK)]

    return [
        each(enter),
        two_sided(left_a, right_a, arriving),
        each(second_slice),
        two_sided(left_f, right_f, field),
        each(residual),
        two_sided(left_f, right_f, field),
        each(second_grad),
        two_sided(left_a, right_a, field),
        each(first_grad),
    ]


def own_marks(part, base_row, edge, tile_rows):
    slots = part.shape[0] - 1
    first, second, left = [], [], []
    ranks = [jnp.int32(0), jnp.int32(0)]
    for q in range(slots):
        live = jnp.where(q < part[slots, 0], 1, 0)
        inner = jnp.where(part[q, 0] - base_row + edge <= tile_rows, live, 0)
        first.append(jnp.where(ranks[0] < EARLY, inner, 0))
        ranks[0] = ranks[0] + inner
        rest = live - first[q]
        second.append(jnp.where(ranks[1] < MIDDLE, rest, 0))
        ranks[1] = ranks[1] + rest
        left.append(rest - second[q])
    return first, second, left


def put_in_order(order, marks):
    taken = jnp.int32(0)
    order[0] = 0
    for q, mark in enumerate(marks):
        order[taken] = q
        taken = taken + mark
    return taken


def fill_corners(corner, part):
    for q in range(part.shape[0] - 1):
        corner[q, 0] = part[q, 0]
        corner[q, 1] = part[q, 1]


def list_late(order, corner, mine, across, base_row, edge, tile_rows):
    slots = mine.shape[0] - 1
    fill_corners(corner, mine)
    marks = own_marks(mine, base_row, edge, tile_rows)[2]
    for q in range(slots):
        corner[slots + q, 0] = across[q, 0]
        corner[slots + q, 1] = across[q, 1]
        marks.append(jnp.where(q < across[slots, 0], 1, 0))
    return put_in_order(order, marks)


def run_pairs(order, total, base_row, refs, work):
    def visit(step, carry):
        a = order[2 * step]
        b_lives = 2 * step + 1 < total
        b = jnp.where(b_lives, order[2 * step + 1], a)
        ones = slot_stages(a, 1.0, base_row, refs, work[0])
        twos = slot_stages(b, jnp.where(b_lives, 1.0, 0.0), base_row, refs, work[1])
        for step_now in ones[0]:
            step_now()
        for k in range(1, len(ones)):
            if k % 2:
                interleaved(ones[k], twos[k - 1])
            else:
                interleaved(twos[k - 1], ones[k])
        for step_now in twos[-1]:
            step_now()
        return carry

    lax.fori_loop(0, (total + 1) // 2, visit, 0)


def widen(wide, source, start, part, s_from, s_to):
    rows = source.shape[-2]
    for t in range(wide.shape[2]):
        wide[part, s_to, t, pl.ds(start, rows), :] = source[
            part, s_from, :, pl.ds(t * LANES, LANES)
        ].astype(jnp.float32)


def fetch(copies, sems):
    started = {}
    for k, (group, source, target) in enumerate(copies):
        copy = pltpu.make_async_copy(source, target, sems.at[k])
        copy.start()
        started.setdefault(group, []).append(copy)

    def wait(group):
        for copy in started[group]:
            copy.wait()

    return wait


def zero_rows(acc, start, rows):
    for part in range(2):
        for s in range(acc.shape[1]):
            for t in range(acc.shape[2]):
                acc[part, s, t, pl.ds(start, rows), :] = jnp.zeros((rows, LANES), jnp.float32)


def lay_patches(wide, wait, spec, rims, half):
    slices, tile_rows = spec.shape[1:3]
    wait("spec")
    for part in range(2):
        for s in range(slices):
            widen(wide, spec, 0, part, s, s)
    if rims:
        wait("rim")
        for part in range(2):
            widen(wide, rims[0], tile_rows, part, 0, half)
            widen(wide, rims[1], tile_rows, part, 0, 1 - half)


def early_kernel(
    meta,
    mine,
    probe_any,
    spec_any,
    amp_any,
    planes_any,
    acc,
    probe_acc,
    order,
    corner,
    sems,
    probe,
    spec,
    amp,
    planes,
    la,
    ra,
    lf,
    rf,
    wide,
    *work,
):
    wait = fetch(
        [
            ("spec", spec_any, spec),
            ("planes", planes_any, planes),
            ("rest", probe_any, probe),
            ("rest", amp_any, amp),
        ],
        sems,
    )
    tables = (la, ra, lf, rf)
    edge, tile_rows = probe.shape[1], spec.shape[2]
    zero_rows(acc, 0, tile_rows)
    probe_acc[...] = jnp.zeros(probe_acc.shape, jnp.float32)
    fill_corners(corner, mine)
    total = put_in_order(order, own_marks(mine, meta[0], edge, tile_rows)[0])
    lay_patches(wide, wait, spec, (), meta[1])
    wait("planes")
    lay_tables(planes, tables)
    wait("rest")
    refs = (corner, probe, amp, tables, wide, acc, probe_acc)
    run_pairs(order, total, meta[0], refs, (work[:5], work[5:]))


def middle_kernel(
    meta,
    mine,
    probe_any,
    spec_any,
    rim_own_any,
    rim_other_any,
    acc_any,
    probe_acc_any,
    amp_any,
    planes_any,
    acc,
    probe_acc,
    order,
    corner,
    sems,
    probe,
    spec,
    amp,
    planes,
    la,
    ra,
    lf,
    rf,
    wide,
    rim_own,
    rim_other,
    *work,
):
    edge, tile_rows = probe.shape[1], spec.shape[2]
    wait = fetch(
        [
            ("spec", spec_any, spec),
            ("planes", planes_any, planes),
            ("rim", rim_own_any, rim_own),
            ("rim", rim_other_any, rim_other),
            ("acc", acc_any, acc.at[:, :, :, pl.ds(0, tile_rows), :]),
            ("acc", probe_acc_any, probe_acc),
            ("rest", probe_any, probe),
            ("rest", amp_any, amp),
        ],
        sems,
    )
    tables = (la, ra, lf, rf)
    zero_rows(acc, tile_rows, edge)
    fill_corners(corner, mine)
    total = put_in_order(order, own_marks(mine, meta[0], edge, tile_rows)[1])
    lay_patches(wide, wait, spec, (rim_own, rim_other), meta[1])
    wait("planes")
    lay_tables(planes, tables)
    wait("acc")
    wait("rest")
    refs = (corner, probe, amp, tables, wide, acc, probe_acc)
    run_pairs(order, total, meta[0], refs, (work[:5], work[5:]))


def late_kernel(
    meta,
    mine,
    across,
    probe_any,
    spec_any,
    rim_own_any,
    rim_other_any,
    acc_any,
    probe_acc_any,
    amp_any,
    across_amp_any,
    planes_any,
    send_first,
    send_rows,
    keep_rim,
    keep_low,
    keep_top,
    keep_probe,
    order,
    corner,
    sems,
    probe,
    spec,
    amp,
    planes,
    la,
    ra,
    lf,
    rf,
    wide,
    rim_own,
    rim_other,
    acc,
    probe_acc,
    *work,
):
    tile_rows, width = spec.shape[2:]
    edge = probe.shape[1]
    slots = mine.shape[0] - 1
    wait = fetch(
        [
            ("spec", spec_any, spec),
            ("planes", planes_any, planes),
            ("rim", rim_own_any, rim_own),
            ("rim", rim_other_any, rim_other),
            ("acc", acc_any, acc),
            ("acc", probe_acc_any, probe_acc),
            ("rest", probe_any, probe),
            ("rest", amp_any, amp.at[pl.ds(0, slots)]),
            ("rest", across_amp_any, amp.at[pl.ds(slots, slots)]),
        ],
        sems,
    )
    tables = (la, ra, lf, rf)
    half = meta[1]
    other = 1 - half
    col_tiles = width // LANES
    total = list_late(order, corner, mine, across, meta[0], edge, tile_rows)
    lay_patches(wide, wait, spec, (rim_own, rim_other), half)
    wait("planes")
    lay_tables(planes, tables)
    wait("acc")
    wait("rest")
    refs = (corner, probe, amp, tables, wide, acc, probe_acc)
    run_pairs(order, total, meta[0], refs, (work[:5], work[5:]))

    below = pl.ds(tile_rows, edge)
    low = pl.ds(edge, tile_rows - edge)
    top = pl.ds(0, edge)
    rows = pl.ds(0, tile_rows)
    for part in range(2):
        sign = 1.0 if part == 0 else -1.0
        for t in range(col_tiles):
            cols = pl.ds(t * LANES, LANES)
            send_first[pl.ds(part * edge, edge), cols] = (
                sign * acc[part, other, t, below, :]
            ).astype(jnp.bfloat16)
            send_rows[part, :, cols] = (sign * acc[part, other, t, rows, :]).astype(jnp.bfloat16)
            keep_rim[part, :, cols] = sign * acc[part, half, t, below, :]
            keep_low[part, :, cols] = sign * acc[part, half, t, low, :]
            keep_top[part, :, cols] = sign * acc[part, half, t, top, :]
    deep = keep_probe.shape[0]
    flip = jnp.where(other == 1, -1.0, 1.0)
    for piece in range(width // edge):
        piece_rows, cols = pl.ds(piece * deep, deep), pl.ds(piece * edge, edge)
        send_first[pl.ds(2 * edge, deep), cols] = (flip * probe_acc[other, piece_rows, :]).astype(
            jnp.bfloat16
        )
        keep_probe[:, cols] = -flip * probe_acc[half, piece_rows, :]


VMEM = pl.BlockSpec(memory_space=pltpu.VMEM)
SMEM = pl.BlockSpec(memory_space=pltpu.SMEM)
ANY = pl.BlockSpec(memory_space=pl.ANY)


def scratch(entries, slices, width, tile_rows, rows, edge, copies):
    planes = pltpu.VMEM((2, edge, edge), jnp.float32)
    table = pltpu.VMEM((2 * edge, 2 * edge), jnp.bfloat16)
    stack = pltpu.VMEM((2 * edge, edge), jnp.bfloat16)
    joined = pltpu.VMEM((edge, 2 * edge), jnp.bfloat16)
    lead = [
        pltpu.SMEM((entries + 1,), jnp.int32),
        pltpu.SMEM((entries, 2), jnp.int32),
        pltpu.SemaphoreType.DMA((copies,)),
        planes,
        pltpu.VMEM((2, slices, tile_rows, width), jnp.bfloat16),
        pltpu.VMEM((entries, edge, edge), jnp.bfloat16),
        pltpu.VMEM((6, edge, edge), jnp.bfloat16),
        table,
        table,
        table,
        table,
        pltpu.VMEM((2, slices, width // LANES, rows, LANES), jnp.float32),
    ]
    return lead, [planes, planes, planes, stack, joined] * 2


def run_early(meta, mine, probe, spec, amp, planes):
    edge = probe.shape[1]
    _, slices, tile_rows, width = spec.shape
    lead, work = scratch(amp.shape[0], slices, width, tile_rows, tile_rows, edge, 4)
    return pl.pallas_call(
        early_kernel,
        out_shape=(
            jax.ShapeDtypeStruct((2, slices, width // LANES, tile_rows, LANES), jnp.float32),
            jax.ShapeDtypeStruct((2, edge, edge), jnp.float32),
        ),
        in_specs=[SMEM] * 2 + [ANY] * 4,
        out_specs=(VMEM, VMEM),
        scratch_shapes=lead + work,
        compiler_params=pltpu.CompilerParams(vmem_limit_bytes=20 * 1024 * 1024),
        name="early_slots",
    )(meta, mine, probe, spec, amp, planes)


def run_middle(meta, mine, probe, spec, rims, accs, amp, planes):
    edge = probe.shape[1]
    _, slices, tile_rows, width = spec.shape
    total = tile_rows + edge
    operands = (probe, spec, *rims, *accs, amp, planes)
    lead, work = scratch(amp.shape[0], slices, width, tile_rows, total, edge, len(operands))
    rim = pltpu.VMEM((2, 1, edge, width), jnp.bfloat16)
    return pl.pallas_call(
        middle_kernel,
        out_shape=(
            jax.ShapeDtypeStruct((2, slices, width // LANES, total, LANES), jnp.float32),
            jax.ShapeDtypeStruct((2, edge, edge), jnp.float32),
        ),
        in_specs=[SMEM] * 2 + [ANY] * len(operands),
        out_specs=(VMEM, VMEM),
        scratch_shapes=lead + [rim, rim] + work,
        compiler_params=pltpu.CompilerParams(vmem_limit_bytes=24 * 1024 * 1024),
        name="middle_slots",
    )(meta, mine, *operands)


def run_late(meta, lists, probe, spec, rims, accs, amps, planes):
    edge = probe.shape[1]
    _, slices, tile_rows, width = spec.shape
    total = tile_rows + edge
    deep = edge * edge // width
    operands = (probe, spec, *rims, *accs, *amps, planes)
    entries = sum(amp.shape[0] for amp in amps)
    lead, work = scratch(entries, slices, width, tile_rows, total, edge, len(operands))
    rim = pltpu.VMEM((2, 1, edge, width), jnp.bfloat16)
    return pl.pallas_call(
        late_kernel,
        out_shape=(
            jax.ShapeDtypeStruct((2 * edge + deep, width), jnp.bfloat16),
            jax.ShapeDtypeStruct((2, tile_rows, width), jnp.bfloat16),
            jax.ShapeDtypeStruct((2, edge, width), jnp.float32),
            jax.ShapeDtypeStruct((2, tile_rows - edge, width), jnp.float32),
            jax.ShapeDtypeStruct((2, edge, width), jnp.float32),
            jax.ShapeDtypeStruct((deep, width), jnp.float32),
        ),
        in_specs=[SMEM] * 3 + [ANY] * len(operands),
        out_specs=(VMEM,) * 6,
        scratch_shapes=lead
        + [
            rim,
            rim,
            pltpu.VMEM((2, slices, width // LANES, total, LANES), jnp.float32),
            pltpu.VMEM((2, edge, edge), jnp.float32),
        ]
        + work,
        compiler_params=pltpu.CompilerParams(vmem_limit_bytes=28 * 1024 * 1024),
        name="late_slots",
    )(meta, *lists, *operands)


def write_rows(meta, own, theirs, start, shape, base=None):
    slices, rows, width = shape[1], own.shape[1], own.shape[2]

    def kernel(meta, own, theirs, *rest):
        out, wide, sems = rest[-3:]
        half = meta[1]
        copies = []
        for s, source in ((half, own), (1 - half, theirs)):
            for part in range(2):
                wide[s, part] = source[part].astype(jnp.float32)
                copy = pltpu.make_async_copy(
                    wide.at[s, part],
                    out.at[part, s, pl.ds(start, rows), :],
                    sems.at[len(copies)],
                )
                copy.start()
                copies.append(copy)
        for copy in copies:
            copy.wait()

    extra = [] if base is None else [base]
    return pl.pallas_call(
        kernel,
        out_shape=jax.ShapeDtypeStruct(shape, jnp.float32),
        in_specs=[SMEM, VMEM, VMEM] + [ANY] * len(extra),
        out_specs=ANY,
        input_output_aliases={} if base is None else {3: 0},
        scratch_shapes=[
            pltpu.VMEM((slices, 2, rows, width), jnp.float32),
            pltpu.SemaphoreType.DMA((2 * slices,)),
        ],
        compiler_params=pltpu.CompilerParams(vmem_limit_bytes=16 * 1024 * 1024),
        cost_estimate=pl.CostEstimate(
            flops=0, bytes_accessed=2 * slices * rows * width * 6, transcendentals=0
        ),
        name="write_rows",
    )(meta, own, theirs, *extra)


def traded(value, axis, distance):
    count = lax.axis_size(axis)
    return lax.ppermute(value, axis, [(i, i ^ distance) for i in range(count)])


def passed_along(value, axis, steps):
    count = lax.axis_size(axis)
    initial, last = (max(0, -steps), min(count, count - steps))
    return lax.ppermute(value, axis, [(source, source + steps) for source in range(initial, last)])


def narrow_sum(own, got):
    return (own.astype(jnp.float32) + got.astype(jnp.float32)).astype(jnp.bfloat16)


def early_sum(own, got):
    def kernel(own, got, out):
        total = own[...].astype(jnp.float32) + got[...].astype(jnp.float32)
        out[...] = total.astype(jnp.bfloat16)

    return pl.pallas_call(
        kernel,
        out_shape=jax.ShapeDtypeStruct(own.shape, own.dtype),
        in_specs=[VMEM, VMEM],
        out_specs=VMEM,
        cost_estimate=pl.CostEstimate(flops=10**10, bytes_accessed=10**8, transcendentals=0),
        compiler_params=pltpu.CompilerParams(vmem_limit_bytes=8 * 1024 * 1024),
        name="early_sum",
    )(own, got)


def unfolded(value, edge):
    return jnp.concatenate([value[:, k : k + edge] for k in range(0, value.shape[1], edge)], 0)


def body(probe_field, specimen, amplitude, scan_anchor, counts):
    edge = probe_field.shape[1]
    _, slices, tile_rows, width = specimen.shape
    half = lax.axis_index("pos") % 2
    base_row = lax.axis_index("tile") * tile_rows
    meta = jnp.stack([base_row, half]).astype(jnp.int32)
    planes = fixed_tables(edge)
    rim_own = passed_along(
        lax.dynamic_slice(specimen, (0, half, 0, 0), (2, 1, edge, width)), "tile", -1
    )
    across_amp = traded(amplitude, "pos", 2)
    mine = jnp.concatenate([scan_anchor, jnp.broadcast_to(counts, (1, 2))], 0)
    across = traded(mine, "pos", 2)
    accs = run_early(meta, mine, probe_field, specimen, amplitude, planes)
    rim_own, accs = lax.optimization_barrier((rim_own, accs))
    rims = (rim_own, traded(rim_own, "pos", 1))
    accs = run_middle(meta, mine, probe_field, specimen, rims, accs, amplitude, planes)
    sent_first, sent_rows, kept_rim, kept_low, kept_top, kept_probe = run_late(
        meta,
        (mine, across),
        probe_field,
        specimen,
        rims,
        accs,
        (amplitude, across_amp),
        planes,
    )
    got_first = traded(sent_first, "pos", 1)
    got_first, sent_rows = lax.optimization_barrier((got_first, sent_rows))
    got_rows = traded(sent_rows, "pos", 1)
    below = kept_rim + got_first[: 2 * edge].reshape(kept_rim.shape).astype(jnp.float32)
    below = passed_along(below.astype(jnp.bfloat16), "tile", 1)
    probe_part = (kept_probe + got_first[2 * edge :].astype(jnp.float32)).astype(jnp.bfloat16)
    distance = lax.axis_size("tile")
    while distance > 4:
        distance //= 2
        probe_part = early_sum(probe_part, traded(probe_part, "tile", distance))
    got_probe = traded(probe_part, "tile", 2)
    lower = (kept_low + got_rows[:, edge:].astype(jnp.float32)).astype(jnp.bfloat16)
    tile_grad = write_rows(meta, lower, traded(lower, "pos", 1), edge, specimen.shape)
    top = kept_top + got_rows[:, :edge].astype(jnp.float32)
    below, top, tile_grad = lax.optimization_barrier((below, top, tile_grad))
    upper = (top + below.astype(jnp.float32)).astype(jnp.bfloat16)
    upper_theirs = traded(upper, "pos", 1)
    _, got_probe = lax.optimization_barrier((upper, got_probe))
    probe_part = narrow_sum(probe_part, got_probe)
    probe_part = narrow_sum(probe_part, traded(probe_part, "tile", 1))
    tile_grad = write_rows(meta, upper, upper_theirs, 0, specimen.shape, tile_grad)
    probe_theirs, tile_grad = lax.optimization_barrier((traded(probe_part, "pos", 1), tile_grad))
    probe_own, probe_theirs = [unfolded(value, edge) for value in (probe_part, probe_theirs)]
    probe_total = jnp.where(
        half == 0, jnp.stack([probe_own, probe_theirs]), jnp.stack([probe_theirs, probe_own])
    ).astype(jnp.float32)
    return (tile_grad, probe_total)


def solution(mesh):
    return jax.shard_map(
        body,
        mesh=mesh,
        in_specs=(
            P(),
            P(None, None, "tile", None),
            P(("tile", "pos"), None, None),
            P(("tile", "pos"), None),
            P(("tile", "pos")),
        ),
        out_specs=(P(None, None, "tile", None), P()),
        check_vma=False,
    )
```

```python
import math

import jax
import jax.numpy as jnp
import ml_dtypes
import numpy as np
from jax import lax
from jax.experimental import pallas as pl
from jax.experimental.pallas import tpu as pltpu
from jax.sharding import PartitionSpec as P

PROP_COEF = 0.5
AMP_EPS = 0.05
LANES = 128
CHUNK = 32
EARLY = 4
MIDDLE = 4


def fixed_tables(edge):
    index = np.arange(edge)
    angles = (np.outer(index, index) % edge) * (2.0 * math.pi / edge)
    cosine = (np.cos(angles) / math.sqrt(edge)).astype(ml_dtypes.bfloat16).astype(np.float64)
    sine = (np.sin(angles) / math.sqrt(edge)).astype(ml_dtypes.bfloat16).astype(np.float64)
    forward = cosine - 1j * sine
    centred = np.where(index < edge // 2, index, index - edge)
    ramp = np.exp(-1j * (PROP_COEF * math.pi / edge) * centred * centred)
    spread = (np.conj(forward) * ramp[None, :]) @ forward
    planes = [
        plane for matrix in (spread, forward) for plane in (matrix.real, matrix.imag, -matrix.imag)
    ]
    return jnp.asarray(np.stack(planes).astype(ml_dtypes.bfloat16))


def lay_tables(planes, tables):
    edge = planes.shape[1]
    lo, hi = pl.ds(0, edge), pl.ds(edge, edge)
    for k in range(2):
        real, imag, negated = (planes[3 * k + i] for i in range(3))
        left, right = tables[2 * k : 2 * k + 2]
        left[lo, lo], left[lo, hi], left[hi, lo], left[hi, hi] = real, negated, imag, real
        right[lo, lo], right[lo, hi], right[hi, lo], right[hi, hi] = real, imag, negated, real


def interleaved(first, second):
    marks = [(k / len(first), 0, k) for k in range(len(first))]
    marks += [((k + 0.5) / len(second), 1, k) for k in range(len(second))]
    for _, which, k in sorted(marks):
        (first, second)[which][k]()


def slot_stages(slot, alive, base_row, refs, work):
    corner, probe, amp, tables, wide, acc, probe_acc = refs
    rolled, arriving, field, stack, joined = work
    left_a, right_a, left_f, right_f = tables
    edge = probe.shape[1]
    col_tiles = wide.shape[2]
    parts = edge // LANES
    lane = lax.broadcasted_iota(jnp.int32, (CHUNK, LANES), 1)
    row = corner[slot, 0] - base_row
    col = corner[slot, 1]
    first = jnp.minimum(col // LANES, col_tiles - parts - 1)
    shift = col - first * LANES
    turn = jnp.where(shift >= LANES, 0, shift)
    back = jnp.where(turn == 0, 0, LANES - turn)
    own = lane >= shift
    near = lane < LANES - shift

    def patch(part, s, i, j):
        rows = pl.ds(row + i, CHUNK)
        main = wide[part, s, first + j, rows, :]
        if j > 0:
            return main
        return jnp.where(own, main, wide[part, s, first + parts, rows, :])

    def place(part, s, i, j, value):
        rows = pl.ds(row + i, CHUNK)
        if j > 0:
            acc[part, s, first + j, rows, :] += value
        else:
            acc[part, s, first, rows, :] += jnp.where(own, value, 0.0)
            acc[part, s, first + parts, rows, :] += jnp.where(own, 0.0, value)

    def put(i, j, re, im):
        cols = pl.ds(j * LANES, LANES)
        stack[pl.ds(i, CHUNK), cols] = re.astype(jnp.bfloat16)
        stack[pl.ds(edge + i, CHUNK), cols] = im.astype(jnp.bfloat16)

    def halves():
        return [(j, pl.ds(j * LANES, LANES)) for j in range(parts)]

    def enter(i):
        rows = pl.ds(i, CHUNK)
        turned = [
            [pltpu.roll(probe[part, rows, cols], turn, 1) for j, cols in halves()]
            for part in range(2)
        ]
        for j, cols in halves():
            u_re, u_im = [
                jnp.where(own, turned[part][j], turned[part][j - 1]) for part in range(2)
            ]
            rolled[0, rows, cols] = u_re
            rolled[1, rows, cols] = u_im
            o_re, o_im = patch(0, 0, i, j), patch(1, 0, i, j)
            put(i, j, u_re * o_re - u_im * o_im, u_re * o_im + u_im * o_re)

    def second_slice(i):
        rows = pl.ds(i, CHUNK)
        for j, cols in halves():
            u_re, u_im = arriving[0, rows, cols], arriving[1, rows, cols]
            o_re, o_im = patch(0, 1, i, j), patch(1, 1, i, j)
            put(i, j, u_re * o_re - u_im * o_im, u_re * o_im + u_im * o_re)

    def residual(i):
        rows = pl.ds(i, CHUNK)
        for j, cols in halves():
            far_re, far_im = field[0, rows, cols], field[1, rows, cols]
            measured = amp[slot, rows, cols].astype(jnp.float32) * alive
            ratio = measured * lax.rsqrt(far_re * far_re + far_im * far_im + AMP_EPS)
            put(i, j, (alive - ratio) * far_re, (ratio - alive) * far_im)

    def second_grad(i):
        rows = pl.ds(i, CHUNK)
        for j, cols in halves():
            u_re, u_im = arriving[0, rows, cols], arriving[1, rows, cols]
            w_re, w_im = field[0, rows, cols], field[1, rows, cols]
            place(0, 1, i, j, u_re * w_re - u_im * w_im)
            place(1, 1, i, j, u_re * w_im + u_im * w_re)
            o_re, o_im = patch(0, 1, i, j), patch(1, 1, i, j)
            put(i, j, o_re * w_re - o_im * w_im, o_re * w_im + o_im * w_re)

    def first_grad(i):
        rows = pl.ds(i, CHUNK)
        turned = [[None] * parts for _ in range(2)]
        for j, cols in halves():
            u_re, u_im = rolled[0, rows, cols], rolled[1, rows, cols]
            w_re, w_im = field[0, rows, cols], field[1, rows, cols]
            place(0, 0, i, j, u_re * w_re - u_im * w_im)
            place(1, 0, i, j, u_re * w_im + u_im * w_re)
            o_re, o_im = patch(0, 0, i, j), patch(1, 0, i, j)
            turned[0][j] = pltpu.roll(o_re * w_re - o_im * w_im, back, 1)
            turned[1][j] = pltpu.roll(o_re * w_im + o_im * w_re, back, 1)
        for part in range(2):
            for j, cols in halves():
                after = turned[part][(j + 1) % parts]
                probe_acc[part, rows, cols] += jnp.where(near, turned[part][j], after)

    def two_sided(left, right, out):
        def both_rows():
            middle = jnp.dot(left[...], stack[...], preferred_element_type=jnp.float32)
            joined[:, pl.ds(0, edge)] = middle[:edge].astype(jnp.bfloat16)
            joined[:, pl.ds(edge, edge)] = middle[edge:].astype(jnp.bfloat16)

        def cols_of(part):
            out[part] = jnp.dot(
                joined[...],
                right[:, pl.ds(part * edge, edge)],
                preferred_element_type=jnp.float32,
            )

        return [both_rows] + [lambda p=p: cols_of(p) for p in range(2)]

    def each(step):
        return [lambda i=i: step(i) for i in range(0, edge, CHUNK)]

    return [
        each(enter),
        two_sided(left_a, right_a, arriving),
        each(second_slice),
        two_sided(left_f, right_f, field),
        each(residual),
        two_sided(left_f, right_f, field),
        each(second_grad),
        two_sided(left_a, right_a, field),
        each(first_grad),
    ]


def own_marks(part, base_row, edge, tile_rows):
    slots = part.shape[0] - 1
    first, second, left = [], [], []
    ranks = [jnp.int32(0), jnp.int32(0)]
    for q in range(slots):
        live = jnp.where(q < part[slots, 0], 1, 0)
        inner = jnp.where(part[q, 0] - base_row + edge <= tile_rows, live, 0)
        first.append(jnp.where(ranks[0] < EARLY, inner, 0))
        ranks[0] = ranks[0] + inner
        rest = live - first[q]
        second.append(jnp.where(ranks[1] < MIDDLE, rest, 0))
        ranks[1] = ranks[1] + rest
        left.append(rest - second[q])
    return first, second, left


def put_in_order(order, marks):
    taken = jnp.int32(0)
    order[0] = 0
    for q, mark in enumerate(marks):
        order[taken] = q
        taken = taken + mark
    return taken


def fill_corners(corner, part):
    for q in range(part.shape[0] - 1):
        corner[q, 0] = part[q, 0]
        corner[q, 1] = part[q, 1]


def list_late(order, corner, mine, across, base_row, edge, tile_rows):
    slots = mine.shape[0] - 1
    fill_corners(corner, mine)
    marks = own_marks(mine, base_row, edge, tile_rows)[2]
    for q in range(slots):
        corner[slots + q, 0] = across[q, 0]
        corner[slots + q, 1] = across[q, 1]
        marks.append(jnp.where(q < across[slots, 0], 1, 0))
    return put_in_order(order, marks)


def run_pairs(order, total, base_row, refs, work):
    def visit(step, carry):
        a = order[2 * step]
        b_lives = 2 * step + 1 < total
        b = jnp.where(b_lives, order[2 * step + 1], a)
        ones = slot_stages(a, 1.0, base_row, refs, work[0])
        twos = slot_stages(b, jnp.where(b_lives, 1.0, 0.0), base_row, refs, work[1])
        for step_now in ones[0]:
            step_now()
        for k in range(1, len(ones)):
            if k % 2:
                interleaved(ones[k], twos[k - 1])
            else:
                interleaved(twos[k - 1], ones[k])
        for step_now in twos[-1]:
            step_now()
        return carry

    lax.fori_loop(0, (total + 1) // 2, visit, 0)


def widen(wide, source, start, part, s_from, s_to):
    rows = source.shape[-2]
    for t in range(wide.shape[2]):
        wide[part, s_to, t, pl.ds(start, rows), :] = source[
            part, s_from, :, pl.ds(t * LANES, LANES)
        ].astype(jnp.float32)


def fetch(copies, sems):
    started = {}
    for k, (group, source, target) in enumerate(copies):
        copy = pltpu.make_async_copy(source, target, sems.at[k])
        copy.start()
        started.setdefault(group, []).append(copy)

    def wait(group):
        for copy in started[group]:
            copy.wait()

    return wait


def zero_rows(acc, start, rows):
    for part in range(2):
        for s in range(acc.shape[1]):
            for t in range(acc.shape[2]):
                acc[part, s, t, pl.ds(start, rows), :] = jnp.zeros((rows, LANES), jnp.float32)


def lay_patches(wide, wait, spec, rims, half):
    slices, tile_rows = spec.shape[1:3]
    wait("spec")
    for part in range(2):
        for s in range(slices):
            widen(wide, spec, 0, part, s, s)
    if rims:
        wait("rim")
        for part in range(2):
            widen(wide, rims[0], tile_rows, part, 0, half)
            widen(wide, rims[1], tile_rows, part, 0, 1 - half)


def early_kernel(
    meta,
    mine,
    probe_any,
    spec_any,
    amp_any,
    planes_any,
    acc,
    probe_acc,
    order,
    corner,
    sems,
    probe,
    spec,
    amp,
    planes,
    la,
    ra,
    lf,
    rf,
    wide,
    *work,
):
    wait = fetch(
        [
            ("spec", spec_any, spec),
            ("planes", planes_any, planes),
            ("rest", probe_any, probe),
            ("rest", amp_any, amp),
        ],
        sems,
    )
    tables = (la, ra, lf, rf)
    edge, tile_rows = probe.shape[1], spec.shape[2]
    zero_rows(acc, 0, tile_rows)
    probe_acc[...] = jnp.zeros(probe_acc.shape, jnp.float32)
    fill_corners(corner, mine)
    total = put_in_order(order, own_marks(mine, meta[0], edge, tile_rows)[0])
    lay_patches(wide, wait, spec, (), meta[1])
    wait("planes")
    lay_tables(planes, tables)
    wait("rest")
    refs = (corner, probe, amp, tables, wide, acc, probe_acc)
    run_pairs(order, total, meta[0], refs, (work[:5], work[5:]))


def middle_kernel(
    meta,
    mine,
    probe_any,
    spec_any,
    rim_own_any,
    rim_other_any,
    acc_any,
    probe_acc_any,
    amp_any,
    planes_any,
    acc,
    probe_acc,
    order,
    corner,
    sems,
    probe,
    spec,
    amp,
    planes,
    la,
    ra,
    lf,
    rf,
    wide,
    rim_own,
    rim_other,
    *work,
):
    edge, tile_rows = probe.shape[1], spec.shape[2]
    wait = fetch(
        [
            ("spec", spec_any, spec),
            ("planes", planes_any, planes),
            ("rim", rim_own_any, rim_own),
            ("rim", rim_other_any, rim_other),
            ("acc", acc_any, acc.at[:, :, :, pl.ds(0, tile_rows), :]),
            ("acc", probe_acc_any, probe_acc),
            ("rest", probe_any, probe),
            ("rest", amp_any, amp),
        ],
        sems,
    )
    tables = (la, ra, lf, rf)
    zero_rows(acc, tile_rows, edge)
    fill_corners(corner, mine)
    total = put_in_order(order, own_marks(mine, meta[0], edge, tile_rows)[1])
    lay_patches(wide, wait, spec, (rim_own, rim_other), meta[1])
    wait("planes")
    lay_tables(planes, tables)
    wait("acc")
    wait("rest")
    refs = (corner, probe, amp, tables, wide, acc, probe_acc)
    run_pairs(order, total, meta[0], refs, (work[:5], work[5:]))


def late_kernel(
    meta,
    mine,
    across,
    probe_any,
    spec_any,
    rim_own_any,
    rim_other_any,
    acc_any,
    probe_acc_any,
    amp_any,
    across_amp_any,
    planes_any,
    send_first,
    send_rows,
    keep_rim,
    keep_low,
    keep_top,
    keep_probe,
    order,
    corner,
    sems,
    probe,
    spec,
    amp,
    planes,
    la,
    ra,
    lf,
    rf,
    wide,
    rim_own,
    rim_other,
    acc,
    probe_acc,
    *work,
):
    tile_rows, width = spec.shape[2:]
    edge = probe.shape[1]
    slots = mine.shape[0] - 1
    wait = fetch(
        [
            ("spec", spec_any, spec),
            ("planes", planes_any, planes),
            ("rim", rim_own_any, rim_own),
            ("rim", rim_other_any, rim_other),
            ("acc", acc_any, acc),
            ("acc", probe_acc_any, probe_acc),
            ("rest", probe_any, probe),
            ("rest", amp_any, amp.at[pl.ds(0, slots)]),
            ("rest", across_amp_any, amp.at[pl.ds(slots, slots)]),
        ],
        sems,
    )
    tables = (la, ra, lf, rf)
    half = meta[1]
    other = 1 - half
    col_tiles = width // LANES
    total = list_late(order, corner, mine, across, meta[0], edge, tile_rows)
    lay_patches(wide, wait, spec, (rim_own, rim_other), half)
    wait("planes")
    lay_tables(planes, tables)
    wait("acc")
    wait("rest")
    refs = (corner, probe, amp, tables, wide, acc, probe_acc)
    run_pairs(order, total, meta[0], refs, (work[:5], work[5:]))

    below = pl.ds(tile_rows, edge)
    low = pl.ds(edge, tile_rows - edge)
    top = pl.ds(0, edge)
    rows = pl.ds(0, tile_rows)
    for part in range(2):
        sign = 1.0 if part == 0 else -1.0
        for t in range(col_tiles):
            cols = pl.ds(t * LANES, LANES)
            send_first[pl.ds(part * edge, edge), cols] = (
                sign * acc[part, other, t, below, :]
            ).astype(jnp.bfloat16)
            send_rows[part, :, cols] = (sign * acc[part, other, t, rows, :]).astype(jnp.bfloat16)
            keep_rim[part, :, cols] = sign * acc[part, half, t, below, :]
            keep_low[part, :, cols] = sign * acc[part, half, t, low, :]
            keep_top[part, :, cols] = sign * acc[part, half, t, top, :]
    deep = keep_probe.shape[0]
    flip = jnp.where(other == 1, -1.0, 1.0)
    for piece in range(width // edge):
        piece_rows, cols = pl.ds(piece * deep, deep), pl.ds(piece * edge, edge)
        send_first[pl.ds(2 * edge, deep), cols] = (flip * probe_acc[other, piece_rows, :]).astype(
            jnp.bfloat16
        )
        keep_probe[:, cols] = -flip * probe_acc[half, piece_rows, :]


VMEM = pl.BlockSpec(memory_space=pltpu.VMEM)
SMEM = pl.BlockSpec(memory_space=pltpu.SMEM)
ANY = pl.BlockSpec(memory_space=pl.ANY)


def scratch(entries, slices, width, tile_rows, rows, edge, copies):
    planes = pltpu.VMEM((2, edge, edge), jnp.float32)
    table = pltpu.VMEM((2 * edge, 2 * edge), jnp.bfloat16)
    stack = pltpu.VMEM((2 * edge, edge), jnp.bfloat16)
    joined = pltpu.VMEM((edge, 2 * edge), jnp.bfloat16)
    lead = [
        pltpu.SMEM((entries + 1,), jnp.int32),
        pltpu.SMEM((entries, 2), jnp.int32),
        pltpu.SemaphoreType.DMA((copies,)),
        planes,
        pltpu.VMEM((2, slices, tile_rows, width), jnp.bfloat16),
        pltpu.VMEM((entries, edge, edge), jnp.bfloat16),
        pltpu.VMEM((6, edge, edge), jnp.bfloat16),
        table,
        table,
        table,
        table,
        pltpu.VMEM((2, slices, width // LANES, rows, LANES), jnp.float32),
    ]
    return lead, [planes, planes, planes, stack, joined] * 2


def run_early(meta, mine, probe, spec, amp, planes):
    edge = probe.shape[1]
    _, slices, tile_rows, width = spec.shape
    lead, work = scratch(amp.shape[0], slices, width, tile_rows, tile_rows, edge, 4)
    return pl.pallas_call(
        early_kernel,
        out_shape=(
            jax.ShapeDtypeStruct((2, slices, width // LANES, tile_rows, LANES), jnp.float32),
            jax.ShapeDtypeStruct((2, edge, edge), jnp.float32),
        ),
        in_specs=[SMEM] * 2 + [ANY] * 4,
        out_specs=(VMEM, VMEM),
        scratch_shapes=lead + work,
        compiler_params=pltpu.CompilerParams(vmem_limit_bytes=20 * 1024 * 1024),
        name="early_slots",
    )(meta, mine, probe, spec, amp, planes)


def run_middle(meta, mine, probe, spec, rims, accs, amp, planes):
    edge = probe.shape[1]
    _, slices, tile_rows, width = spec.shape
    total = tile_rows + edge
    operands = (probe, spec, *rims, *accs, amp, planes)
    lead, work = scratch(amp.shape[0], slices, width, tile_rows, total, edge, len(operands))
    rim = pltpu.VMEM((2, 1, edge, width), jnp.bfloat16)
    return pl.pallas_call(
        middle_kernel,
        out_shape=(
            jax.ShapeDtypeStruct((2, slices, width // LANES, total, LANES), jnp.float32),
            jax.ShapeDtypeStruct((2, edge, edge), jnp.float32),
        ),
        in_specs=[SMEM] * 2 + [ANY] * len(operands),
        out_specs=(VMEM, VMEM),
        scratch_shapes=lead + [rim, rim] + work,
        compiler_params=pltpu.CompilerParams(vmem_limit_bytes=24 * 1024 * 1024),
        name="middle_slots",
    )(meta, mine, *operands)


def run_late(meta, lists, probe, spec, rims, accs, amps, planes):
    edge = probe.shape[1]
    _, slices, tile_rows, width = spec.shape
    total = tile_rows + edge
    deep = edge * edge // width
    operands = (probe, spec, *rims, *accs, *amps, planes)
    entries = sum(amp.shape[0] for amp in amps)
    lead, work = scratch(entries, slices, width, tile_rows, total, edge, len(operands))
    rim = pltpu.VMEM((2, 1, edge, width), jnp.bfloat16)
    return pl.pallas_call(
        late_kernel,
        out_shape=(
            jax.ShapeDtypeStruct((2 * edge + deep, width), jnp.bfloat16),
            jax.ShapeDtypeStruct((2, tile_rows, width), jnp.bfloat16),
            jax.ShapeDtypeStruct((2, edge, width), jnp.float32),
            jax.ShapeDtypeStruct((2, tile_rows - edge, width), jnp.float32),
            jax.ShapeDtypeStruct((2, edge, width), jnp.float32),
            jax.ShapeDtypeStruct((deep, width), jnp.float32),
        ),
        in_specs=[SMEM] * 3 + [ANY] * len(operands),
        out_specs=(VMEM,) * 6,
        scratch_shapes=lead
        + [
            rim,
            rim,
            pltpu.VMEM((2, slices, width // LANES, total, LANES), jnp.float32),
            pltpu.VMEM((2, edge, edge), jnp.float32),
        ]
        + work,
        compiler_params=pltpu.CompilerParams(vmem_limit_bytes=28 * 1024 * 1024),
        name="late_slots",
    )(meta, *lists, *operands)


def write_rows(meta, own, theirs, start, shape, base=None):
    slices, rows, width = shape[1], own.shape[1], own.shape[2]

    def kernel(meta, own, theirs, *rest):
        out, wide, sems = rest[-3:]
        half = meta[1]
        copies = []
        for s, source in ((half, own), (1 - half, theirs)):
            for part in range(2):
                wide[s, part] = source[part].astype(jnp.float32)
                copy = pltpu.make_async_copy(
                    wide.at[s, part],
                    out.at[part, s, pl.ds(start, rows), :],
                    sems.at[len(copies)],
                )
                copy.start()
                copies.append(copy)
        for copy in copies:
            copy.wait()

    extra = [] if base is None else [base]
    return pl.pallas_call(
        kernel,
        out_shape=jax.ShapeDtypeStruct(shape, jnp.float32),
        in_specs=[SMEM, VMEM, VMEM] + [ANY] * len(extra),
        out_specs=ANY,
        input_output_aliases={} if base is None else {3: 0},
        scratch_shapes=[
            pltpu.VMEM((slices, 2, rows, width), jnp.float32),
            pltpu.SemaphoreType.DMA((2 * slices,)),
        ],
        compiler_params=pltpu.CompilerParams(vmem_limit_bytes=16 * 1024 * 1024),
        cost_estimate=pl.CostEstimate(
            flops=0, bytes_accessed=2 * slices * rows * width * 6, transcendentals=0
        ),
        name="write_rows",
    )(meta, own, theirs, *extra)


def traded(value, axis, distance):
    count = lax.axis_size(axis)
    return lax.ppermute(value, axis, [(i, i ^ distance) for i in range(count)])


def passed_along(value, axis, steps):
    count = lax.axis_size(axis)
    initial, last = (max(0, -steps), min(count, count - steps))
    return lax.ppermute(value, axis, [(source, source + steps) for source in range(initial, last)])


def narrow_sum(own, got):
    return (own.astype(jnp.float32) + got.astype(jnp.float32)).astype(jnp.bfloat16)


def early_sum(own, got):
    def kernel(own, got, out):
        total = own[...].astype(jnp.float32) + got[...].astype(jnp.float32)
        out[...] = total.astype(jnp.bfloat16)

    return pl.pallas_call(
        kernel,
        out_shape=jax.ShapeDtypeStruct(own.shape, own.dtype),
        in_specs=[VMEM, VMEM],
        out_specs=VMEM,
        cost_estimate=pl.CostEstimate(flops=10**10, bytes_accessed=10**8, transcendentals=0),
        compiler_params=pltpu.CompilerParams(vmem_limit_bytes=8 * 1024 * 1024),
        name="early_sum",
    )(own, got)


def unfolded(value, edge):
    return jnp.concatenate([value[:, k : k + edge] for k in range(0, value.shape[1], edge)], 0)


def body(probe_field, specimen, amplitude, scan_anchor, counts):
    edge = probe_field.shape[1]
    _, slices, tile_rows, width = specimen.shape
    half = lax.axis_index("pos") % 2
    base_row = lax.axis_index("tile") * tile_rows
    meta = jnp.stack([base_row, half]).astype(jnp.int32)
    planes = fixed_tables(edge)
    rim_own = passed_along(
        lax.dynamic_slice(specimen, (0, half, 0, 0), (2, 1, edge, width)), "tile", -1
    )
    across_amp = traded(amplitude, "pos", 2)
    mine = jnp.concatenate([scan_anchor, jnp.broadcast_to(counts, (1, 2))], 0)
    across = traded(mine, "pos", 2)
    accs = run_early(meta, mine, probe_field, specimen, amplitude, planes)
    rim_own, accs = lax.optimization_barrier((rim_own, accs))
    rims = (rim_own, traded(rim_own, "pos", 1))
    accs = run_middle(meta, mine, probe_field, specimen, rims, accs, amplitude, planes)
    sent_first, sent_rows, kept_rim, kept_low, kept_top, kept_probe = run_late(
        meta,
        (mine, across),
        probe_field,
        specimen,
        rims,
        accs,
        (amplitude, across_amp),
        planes,
    )
    got_first = traded(sent_first, "pos", 1)
    got_first, sent_rows = lax.optimization_barrier((got_first, sent_rows))
    got_rows = traded(sent_rows, "pos", 1)
    below = kept_rim + got_first[: 2 * edge].reshape(kept_rim.shape).astype(jnp.float32)
    below = passed_along(below.astype(jnp.bfloat16), "tile", 1)
    probe_part = (kept_probe + got_first[2 * edge :].astype(jnp.float32)).astype(jnp.bfloat16)
    distance = lax.axis_size("tile")
    while distance > 4:
        distance //= 2
        probe_part = early_sum(probe_part, traded(probe_part, "tile", distance))
    got_probe = traded(probe_part, "tile", 2)
    lower = (kept_low + got_rows[:, edge:].astype(jnp.float32)).astype(jnp.bfloat16)
    tile_grad = write_rows(meta, lower, traded(lower, "pos", 1), edge, specimen.shape)
    top = kept_top + got_rows[:, :edge].astype(jnp.float32)
    below, top, tile_grad = lax.optimization_barrier((below, top, tile_grad))
    upper = (top + below.astype(jnp.float32)).astype(jnp.bfloat16)
    upper_theirs = traded(upper, "pos", 1)
    _, got_probe = lax.optimization_barrier((upper, got_probe))
    probe_part = narrow_sum(probe_part, got_probe)
    probe_part = narrow_sum(probe_part, traded(probe_part, "tile", 1))
    tile_grad = write_rows(meta, upper, upper_theirs, 0, specimen.shape, tile_grad)
    probe_theirs, tile_grad = lax.optimization_barrier((traded(probe_part, "pos", 1), tile_grad))
    probe_own, probe_theirs = [unfolded(value, edge) for value in (probe_part, probe_theirs)]
    probe_total = jnp.where(
        half == 0, jnp.stack([probe_own, probe_theirs]), jnp.stack([probe_theirs, probe_own])
    ).astype(jnp.float32)
    return (tile_grad, probe_total)


def solution(mesh):
    return jax.shard_map(
        body,
        mesh=mesh,
        in_specs=(
            P(),
            P(None, None, "tile", None),
            P(("tile", "pos"), None, None),
            P(("tile", "pos"), None),
            P(("tile", "pos")),
        ),
        out_specs=(P(None, None, "tile", None), P()),
        check_vma=False,
    )
```

```python
import math

import jax
import jax.numpy as jnp
import ml_dtypes
import numpy as np
from jax import lax
from jax.experimental import pallas as pl
from jax.experimental.pallas import tpu as pltpu
from jax.sharding import PartitionSpec as P

PROP_COEF = 0.5
AMP_EPS = 0.05
LANES = 128
CHUNK = 32
PIECE = 128
EARLY = 4
MIDDLE = 4


def fixed_tables(edge):
    index = np.arange(edge)
    angles = (np.outer(index, index) % edge) * (2.0 * math.pi / edge)
    cosine = (np.cos(angles) / math.sqrt(edge)).astype(ml_dtypes.bfloat16).astype(np.float64)
    sine = (np.sin(angles) / math.sqrt(edge)).astype(ml_dtypes.bfloat16).astype(np.float64)
    forward = cosine - 1j * sine
    centred = np.where(index < edge // 2, index, index - edge)
    ramp = np.exp(-1j * (PROP_COEF * math.pi / edge) * centred * centred)
    spread = (np.conj(forward) * ramp[None, :]) @ forward
    planes = [
        plane for matrix in (spread, forward) for plane in (matrix.real, matrix.imag, -matrix.imag)
    ]
    return jnp.asarray(np.stack(planes).astype(ml_dtypes.bfloat16))


def lay_tables(planes, tables):
    edge = planes.shape[1]
    lo, hi = pl.ds(0, edge), pl.ds(edge, edge)
    for k in range(2):
        real, imag, negated = (planes[3 * k + i] for i in range(3))
        left, right = tables[2 * k : 2 * k + 2]
        left[lo, lo], left[lo, hi], left[hi, lo], left[hi, hi] = real, negated, imag, real
        right[lo, lo], right[lo, hi], right[hi, lo], right[hi, hi] = real, imag, negated, real


def interleaved(first, second):
    marks = [(k / len(first), 0, k) for k in range(len(first))]
    marks += [((k + 0.5) / len(second), 1, k) for k in range(len(second))]
    for _, which, k in sorted(marks):
        (first, second)[which][k]()


def slot_stages(slot, alive, base_row, refs, work):
    corner, probe, amp, tables, wide, acc, probe_acc = refs
    rolled, arriving, field, stack, joined = work
    left_a, right_a, left_f, right_f = tables
    edge = probe.shape[1]
    col_tiles = wide.shape[2]
    parts = edge // LANES
    lane = lax.broadcasted_iota(jnp.int32, (CHUNK, LANES), 1)
    row = corner[slot, 0] - base_row
    col = corner[slot, 1]
    first = jnp.minimum(col // LANES, col_tiles - parts - 1)
    shift = col - first * LANES
    turn = jnp.where(shift >= LANES, 0, shift)
    back = jnp.where(turn == 0, 0, LANES - turn)
    own = lane >= shift
    near = lane < LANES - shift

    def patch(part, s, i, j):
        rows = pl.ds(row + i, CHUNK)
        main = wide[part, s, first + j, rows, :]
        if j > 0:
            return main
        return jnp.where(own, main, wide[part, s, first + parts, rows, :])

    def place(part, s, i, j, value):
        rows = pl.ds(row + i, CHUNK)
        if j > 0:
            acc[part, s, first + j, rows, :] += value
        else:
            acc[part, s, first, rows, :] += jnp.where(own, value, 0.0)
            acc[part, s, first + parts, rows, :] += jnp.where(own, 0.0, value)

    def put(i, j, re, im):
        cols = pl.ds(j * LANES, LANES)
        stack[pl.ds(i, CHUNK), cols] = re.astype(jnp.bfloat16)
        stack[pl.ds(edge + i, CHUNK), cols] = im.astype(jnp.bfloat16)

    def halves():
        return [(j, pl.ds(j * LANES, LANES)) for j in range(parts)]

    def enter(i):
        rows = pl.ds(i, CHUNK)
        turned = [
            [pltpu.roll(probe[part, rows, cols], turn, 1) for j, cols in halves()]
            for part in range(2)
        ]
        for j, cols in halves():
            u_re, u_im = [
                jnp.where(own, turned[part][j], turned[part][j - 1]) for part in range(2)
            ]
            rolled[0, rows, cols] = u_re
            rolled[1, rows, cols] = u_im
            o_re, o_im = patch(0, 0, i, j), patch(1, 0, i, j)
            put(i, j, u_re * o_re - u_im * o_im, u_re * o_im + u_im * o_re)

    def second_slice(i):
        rows = pl.ds(i, CHUNK)
        for j, cols in halves():
            u_re, u_im = arriving[0, rows, cols], arriving[1, rows, cols]
            o_re, o_im = patch(0, 1, i, j), patch(1, 1, i, j)
            put(i, j, u_re * o_re - u_im * o_im, u_re * o_im + u_im * o_re)

    def residual(i):
        rows = pl.ds(i, CHUNK)
        for j, cols in halves():
            far_re, far_im = field[0, rows, cols], field[1, rows, cols]
            measured = amp[slot, rows, cols].astype(jnp.float32) * alive
            ratio = measured * lax.rsqrt(far_re * far_re + far_im * far_im + AMP_EPS)
            put(i, j, (alive - ratio) * far_re, (ratio - alive) * far_im)

    def second_grad(i):
        rows = pl.ds(i, CHUNK)
        for j, cols in halves():
            u_re, u_im = arriving[0, rows, cols], arriving[1, rows, cols]
            w_re, w_im = field[0, rows, cols], field[1, rows, cols]
            place(0, 1, i, j, u_re * w_re - u_im * w_im)
            place(1, 1, i, j, u_re * w_im + u_im * w_re)
            o_re, o_im = patch(0, 1, i, j), patch(1, 1, i, j)
            put(i, j, o_re * w_re - o_im * w_im, o_re * w_im + o_im * w_re)

    def first_grad(i):
        rows = pl.ds(i, CHUNK)
        turned = [[None] * parts for _ in range(2)]
        for j, cols in halves():
            u_re, u_im = rolled[0, rows, cols], rolled[1, rows, cols]
            w_re, w_im = field[0, rows, cols], field[1, rows, cols]
            place(0, 0, i, j, u_re * w_re - u_im * w_im)
            place(1, 0, i, j, u_re * w_im + u_im * w_re)
            o_re, o_im = patch(0, 0, i, j), patch(1, 0, i, j)
            turned[0][j] = pltpu.roll(o_re * w_re - o_im * w_im, back, 1)
            turned[1][j] = pltpu.roll(o_re * w_im + o_im * w_re, back, 1)
        for part in range(2):
            for j, cols in halves():
                after = turned[part][(j + 1) % parts]
                probe_acc[part, rows, cols] += jnp.where(near, turned[part][j], after)

    def two_sided(left, right, out):
        def rows_of(part, start):
            joined[pl.ds(start, PIECE), pl.ds(part * edge, edge)] = jnp.dot(
                left[pl.ds(part * edge + start, PIECE), :],
                stack[...],
                preferred_element_type=jnp.float32,
            ).astype(jnp.bfloat16)

        def cols_of(part, start):
            rows = pl.ds(start, PIECE)
            out[part, rows, :] = jnp.dot(
                joined[rows, :],
                right[:, pl.ds(part * edge, edge)],
                preferred_element_type=jnp.float32,
            )

        return [
            lambda step=step, part=part, start=start: step(part, start)
            for step in (rows_of, cols_of)
            for part in range(2)
            for start in range(0, edge, PIECE)
        ]

    def each(step):
        return [lambda i=i: step(i) for i in range(0, edge, CHUNK)]

    return [
        each(enter),
        two_sided(left_a, right_a, arriving),
        each(second_slice),
        two_sided(left_f, right_f, field),
        each(residual),
        two_sided(left_f, right_f, field),
        each(second_grad),
        two_sided(left_a, right_a, field),
        each(first_grad),
    ]


def own_marks(part, base_row, edge, tile_rows):
    slots = part.shape[0] - 1
    first, second, left = [], [], []
    ranks = [jnp.int32(0), jnp.int32(0)]
    for q in range(slots):
        live = jnp.where(q < part[slots, 0], 1, 0)
        inner = jnp.where(part[q, 0] - base_row + edge <= tile_rows, live, 0)
        first.append(jnp.where(ranks[0] < EARLY, inner, 0))
        ranks[0] = ranks[0] + inner
        rest = live - first[q]
        second.append(jnp.where(ranks[1] < MIDDLE, rest, 0))
        ranks[1] = ranks[1] + rest
        left.append(rest - second[q])
    return first, second, left


def put_in_order(order, marks):
    taken = jnp.int32(0)
    order[0] = 0
    for q, mark in enumerate(marks):
        order[taken] = q
        taken = taken + mark
    return taken


def fill_corners(corner, part):
    for q in range(part.shape[0] - 1):
        corner[q, 0] = part[q, 0]
        corner[q, 1] = part[q, 1]


def list_late(order, corner, mine, across, base_row, edge, tile_rows):
    slots = mine.shape[0] - 1
    fill_corners(corner, mine)
    marks = own_marks(mine, base_row, edge, tile_rows)[2]
    for q in range(slots):
        corner[slots + q, 0] = across[q, 0]
        corner[slots + q, 1] = across[q, 1]
        marks.append(jnp.where(q < across[slots, 0], 1, 0))
    return put_in_order(order, marks)


def run_pairs(order, total, base_row, refs, work):
    def visit(step, carry):
        a = order[2 * step]
        b_lives = 2 * step + 1 < total
        b = jnp.where(b_lives, order[2 * step + 1], a)
        ones = slot_stages(a, 1.0, base_row, refs, work[0])
        twos = slot_stages(b, jnp.where(b_lives, 1.0, 0.0), base_row, refs, work[1])
        for step_now in ones[0]:
            step_now()
        for k in range(1, len(ones)):
            if k % 2:
                interleaved(ones[k], twos[k - 1])
            else:
                interleaved(twos[k - 1], ones[k])
        for step_now in twos[-1]:
            step_now()
        return carry

    lax.fori_loop(0, (total + 1) // 2, visit, 0)


def widen(wide, source, start, part, s_from, s_to):
    rows = source.shape[-2]
    for t in range(wide.shape[2]):
        wide[part, s_to, t, pl.ds(start, rows), :] = source[
            part, s_from, :, pl.ds(t * LANES, LANES)
        ].astype(jnp.float32)


def fetch(copies, sems):
    started = {}
    for k, (group, source, target) in enumerate(copies):
        copy = pltpu.make_async_copy(source, target, sems.at[k])
        copy.start()
        started.setdefault(group, []).append(copy)

    def wait(group):
        for copy in started[group]:
            copy.wait()

    return wait


def zero_rows(acc, start, rows):
    for part in range(2):
        for s in range(acc.shape[1]):
            for t in range(acc.shape[2]):
                acc[part, s, t, pl.ds(start, rows), :] = jnp.zeros((rows, LANES), jnp.float32)


def lay_patches(wide, wait, spec, rims, half):
    slices, tile_rows = spec.shape[1:3]
    wait("spec")
    for part in range(2):
        for s in range(slices):
            widen(wide, spec, 0, part, s, s)
    if rims:
        wait("rim")
        for part in range(2):
            widen(wide, rims[0], tile_rows, part, 0, half)
            widen(wide, rims[1], tile_rows, part, 0, 1 - half)


def early_kernel(
    meta,
    mine,
    probe_any,
    spec_any,
    amp_any,
    planes_any,
    acc,
    probe_acc,
    order,
    corner,
    sems,
    probe,
    spec,
    amp,
    planes,
    la,
    ra,
    lf,
    rf,
    wide,
    *work,
):
    wait = fetch(
        [
            ("spec", spec_any, spec),
            ("planes", planes_any, planes),
            ("rest", probe_any, probe),
            ("rest", amp_any, amp),
        ],
        sems,
    )
    tables = (la, ra, lf, rf)
    edge, tile_rows = probe.shape[1], spec.shape[2]
    zero_rows(acc, 0, tile_rows)
    probe_acc[...] = jnp.zeros(probe_acc.shape, jnp.float32)
    fill_corners(corner, mine)
    total = put_in_order(order, own_marks(mine, meta[0], edge, tile_rows)[0])
    lay_patches(wide, wait, spec, (), meta[1])
    wait("planes")
    lay_tables(planes, tables)
    wait("rest")
    refs = (corner, probe, amp, tables, wide, acc, probe_acc)
    run_pairs(order, total, meta[0], refs, (work[:5], work[5:]))


def middle_kernel(
    meta,
    mine,
    probe_any,
    spec_any,
    rim_own_any,
    rim_other_any,
    acc_any,
    probe_acc_any,
    amp_any,
    planes_any,
    acc,
    probe_acc,
    order,
    corner,
    sems,
    probe,
    spec,
    amp,
    planes,
    la,
    ra,
    lf,
    rf,
    wide,
    rim_own,
    rim_other,
    *work,
):
    edge, tile_rows = probe.shape[1], spec.shape[2]
    wait = fetch(
        [
            ("spec", spec_any, spec),
            ("planes", planes_any, planes),
            ("rim", rim_own_any, rim_own),
            ("rim", rim_other_any, rim_other),
            ("acc", acc_any, acc.at[:, :, :, pl.ds(0, tile_rows), :]),
            ("acc", probe_acc_any, probe_acc),
            ("rest", probe_any, probe),
            ("rest", amp_any, amp),
        ],
        sems,
    )
    tables = (la, ra, lf, rf)
    zero_rows(acc, tile_rows, edge)
    fill_corners(corner, mine)
    total = put_in_order(order, own_marks(mine, meta[0], edge, tile_rows)[1])
    lay_patches(wide, wait, spec, (rim_own, rim_other), meta[1])
    wait("planes")
    lay_tables(planes, tables)
    wait("acc")
    wait("rest")
    refs = (corner, probe, amp, tables, wide, acc, probe_acc)
    run_pairs(order, total, meta[0], refs, (work[:5], work[5:]))


def late_kernel(
    meta,
    mine,
    across,
    probe_any,
    spec_any,
    rim_own_any,
    rim_other_any,
    acc_any,
    probe_acc_any,
    amp_any,
    across_amp_any,
    planes_any,
    send_first,
    send_rows,
    keep_rim,
    keep_low,
    keep_top,
    keep_probe,
    order,
    corner,
    sems,
    probe,
    spec,
    amp,
    planes,
    la,
    ra,
    lf,
    rf,
    wide,
    rim_own,
    rim_other,
    acc,
    probe_acc,
    *work,
):
    tile_rows, width = spec.shape[2:]
    edge = probe.shape[1]
    slots = mine.shape[0] - 1
    wait = fetch(
        [
            ("spec", spec_any, spec),
            ("planes", planes_any, planes),
            ("rim", rim_own_any, rim_own),
            ("rim", rim_other_any, rim_other),
            ("acc", acc_any, acc),
            ("acc", probe_acc_any, probe_acc),
            ("rest", probe_any, probe),
            ("rest", amp_any, amp.at[pl.ds(0, slots)]),
            ("rest", across_amp_any, amp.at[pl.ds(slots, slots)]),
        ],
        sems,
    )
    tables = (la, ra, lf, rf)
    half = meta[1]
    other = 1 - half
    col_tiles = width // LANES
    total = list_late(order, corner, mine, across, meta[0], edge, tile_rows)
    lay_patches(wide, wait, spec, (rim_own, rim_other), half)
    wait("planes")
    lay_tables(planes, tables)
    wait("acc")
    wait("rest")
    refs = (corner, probe, amp, tables, wide, acc, probe_acc)
    run_pairs(order, total, meta[0], refs, (work[:5], work[5:]))

    below = pl.ds(tile_rows, edge)
    low = pl.ds(edge, tile_rows - edge)
    top = pl.ds(0, edge)
    rows = pl.ds(0, tile_rows)
    for part in range(2):
        sign = 1.0 if part == 0 else -1.0
        for t in range(col_tiles):
            cols = pl.ds(t * LANES, LANES)
            send_first[pl.ds(part * edge, edge), cols] = (
                sign * acc[part, other, t, below, :]
            ).astype(jnp.bfloat16)
            send_rows[part, :, cols] = (sign * acc[part, other, t, rows, :]).astype(jnp.bfloat16)
            keep_rim[part, :, cols] = sign * acc[part, half, t, below, :]
            keep_low[part, :, cols] = sign * acc[part, half, t, low, :]
            keep_top[part, :, cols] = sign * acc[part, half, t, top, :]
    deep = keep_probe.shape[0]
    flip = jnp.where(other == 1, -1.0, 1.0)
    for piece in range(width // edge):
        piece_rows, cols = pl.ds(piece * deep, deep), pl.ds(piece * edge, edge)
        send_first[pl.ds(2 * edge, deep), cols] = (flip * probe_acc[other, piece_rows, :]).astype(
            jnp.bfloat16
        )
        keep_probe[:, cols] = -flip * probe_acc[half, piece_rows, :]


VMEM = pl.BlockSpec(memory_space=pltpu.VMEM)
SMEM = pl.BlockSpec(memory_space=pltpu.SMEM)
ANY = pl.BlockSpec(memory_space=pl.ANY)


def scratch(entries, slices, width, tile_rows, rows, edge, copies):
    planes = pltpu.VMEM((2, edge, edge), jnp.float32)
    table = pltpu.VMEM((2 * edge, 2 * edge), jnp.bfloat16)
    stack = pltpu.VMEM((2 * edge, edge), jnp.bfloat16)
    joined = pltpu.VMEM((edge, 2 * edge), jnp.bfloat16)
    lead = [
        pltpu.SMEM((entries + 1,), jnp.int32),
        pltpu.SMEM((entries, 2), jnp.int32),
        pltpu.SemaphoreType.DMA((copies,)),
        planes,
        pltpu.VMEM((2, slices, tile_rows, width), jnp.bfloat16),
        pltpu.VMEM((entries, edge, edge), jnp.bfloat16),
        pltpu.VMEM((6, edge, edge), jnp.bfloat16),
        table,
        table,
        table,
        table,
        pltpu.VMEM((2, slices, width // LANES, rows, LANES), jnp.float32),
    ]
    return lead, [planes, planes, planes, stack, joined] * 2


def run_early(meta, mine, probe, spec, amp, planes):
    edge = probe.shape[1]
    _, slices, tile_rows, width = spec.shape
    lead, work = scratch(amp.shape[0], slices, width, tile_rows, tile_rows, edge, 4)
    return pl.pallas_call(
        early_kernel,
        out_shape=(
            jax.ShapeDtypeStruct((2, slices, width // LANES, tile_rows, LANES), jnp.float32),
            jax.ShapeDtypeStruct((2, edge, edge), jnp.float32),
        ),
        in_specs=[SMEM] * 2 + [ANY] * 4,
        out_specs=(VMEM, VMEM),
        scratch_shapes=lead + work,
        compiler_params=pltpu.CompilerParams(vmem_limit_bytes=20 * 1024 * 1024),
        name="early_slots",
    )(meta, mine, probe, spec, amp, planes)


def run_middle(meta, mine, probe, spec, rims, accs, amp, planes):
    edge = probe.shape[1]
    _, slices, tile_rows, width = spec.shape
    total = tile_rows + edge
    operands = (probe, spec, *rims, *accs, amp, planes)
    lead, work = scratch(amp.shape[0], slices, width, tile_rows, total, edge, len(operands))
    rim = pltpu.VMEM((2, 1, edge, width), jnp.bfloat16)
    return pl.pallas_call(
        middle_kernel,
        out_shape=(
            jax.ShapeDtypeStruct((2, slices, width // LANES, total, LANES), jnp.float32),
            jax.ShapeDtypeStruct((2, edge, edge), jnp.float32),
        ),
        in_specs=[SMEM] * 2 + [ANY] * len(operands),
        out_specs=(VMEM, VMEM),
        scratch_shapes=lead + [rim, rim] + work,
        compiler_params=pltpu.CompilerParams(vmem_limit_bytes=24 * 1024 * 1024),
        name="middle_slots",
    )(meta, mine, *operands)


def run_late(meta, lists, probe, spec, rims, accs, amps, planes):
    edge = probe.shape[1]
    _, slices, tile_rows, width = spec.shape
    total = tile_rows + edge
    deep = edge * edge // width
    operands = (probe, spec, *rims, *accs, *amps, planes)
    entries = sum(amp.shape[0] for amp in amps)
    lead, work = scratch(entries, slices, width, tile_rows, total, edge, len(operands))
    rim = pltpu.VMEM((2, 1, edge, width), jnp.bfloat16)
    return pl.pallas_call(
        late_kernel,
        out_shape=(
            jax.ShapeDtypeStruct((2 * edge + deep, width), jnp.bfloat16),
            jax.ShapeDtypeStruct((2, tile_rows, width), jnp.bfloat16),
            jax.ShapeDtypeStruct((2, edge, width), jnp.float32),
            jax.ShapeDtypeStruct((2, tile_rows - edge, width), jnp.float32),
            jax.ShapeDtypeStruct((2, edge, width), jnp.float32),
            jax.ShapeDtypeStruct((deep, width), jnp.float32),
        ),
        in_specs=[SMEM] * 3 + [ANY] * len(operands),
        out_specs=(VMEM,) * 6,
        scratch_shapes=lead
        + [
            rim,
            rim,
            pltpu.VMEM((2, slices, width // LANES, total, LANES), jnp.float32),
            pltpu.VMEM((2, edge, edge), jnp.float32),
        ]
        + work,
        compiler_params=pltpu.CompilerParams(vmem_limit_bytes=28 * 1024 * 1024),
        name="late_slots",
    )(meta, *lists, *operands)


def write_rows(meta, own, theirs, start, shape, base=None):
    slices, rows, width = shape[1], own.shape[1], own.shape[2]

    def kernel(meta, own, theirs, *rest):
        out, wide, sems = rest[-3:]
        half = meta[1]
        copies = []
        for s, source in ((half, own), (1 - half, theirs)):
            for part in range(2):
                wide[s, part] = source[part].astype(jnp.float32)
                copy = pltpu.make_async_copy(
                    wide.at[s, part],
                    out.at[part, s, pl.ds(start, rows), :],
                    sems.at[len(copies)],
                )
                copy.start()
                copies.append(copy)
        for copy in copies:
            copy.wait()

    extra = [] if base is None else [base]
    return pl.pallas_call(
        kernel,
        out_shape=jax.ShapeDtypeStruct(shape, jnp.float32),
        in_specs=[SMEM, VMEM, VMEM] + [ANY] * len(extra),
        out_specs=ANY,
        input_output_aliases={} if base is None else {3: 0},
        scratch_shapes=[
            pltpu.VMEM((slices, 2, rows, width), jnp.float32),
            pltpu.SemaphoreType.DMA((2 * slices,)),
        ],
        compiler_params=pltpu.CompilerParams(vmem_limit_bytes=16 * 1024 * 1024),
        cost_estimate=pl.CostEstimate(
            flops=0, bytes_accessed=2 * slices * rows * width * 6, transcendentals=0
        ),
        name="write_rows",
    )(meta, own, theirs, *extra)


def traded(value, axis, distance):
    count = lax.axis_size(axis)
    return lax.ppermute(value, axis, [(i, i ^ distance) for i in range(count)])


def passed_along(value, axis, steps):
    count = lax.axis_size(axis)
    initial, last = (max(0, -steps), min(count, count - steps))
    return lax.ppermute(value, axis, [(source, source + steps) for source in range(initial, last)])


def narrow_sum(own, got):
    return (own.astype(jnp.float32) + got.astype(jnp.float32)).astype(jnp.bfloat16)


def early_sum(own, got):
    def kernel(own, got, out):
        total = own[...].astype(jnp.float32) + got[...].astype(jnp.float32)
        out[...] = total.astype(jnp.bfloat16)

    return pl.pallas_call(
        kernel,
        out_shape=jax.ShapeDtypeStruct(own.shape, own.dtype),
        in_specs=[VMEM, VMEM],
        out_specs=VMEM,
        cost_estimate=pl.CostEstimate(flops=10**10, bytes_accessed=10**8, transcendentals=0),
        compiler_params=pltpu.CompilerParams(vmem_limit_bytes=8 * 1024 * 1024),
        name="early_sum",
    )(own, got)


def unfolded(value, edge):
    return jnp.concatenate([value[:, k : k + edge] for k in range(0, value.shape[1], edge)], 0)


def body(probe_field, specimen, amplitude, scan_anchor, counts):
    edge = probe_field.shape[1]
    _, slices, tile_rows, width = specimen.shape
    half = lax.axis_index("pos") % 2
    base_row = lax.axis_index("tile") * tile_rows
    meta = jnp.stack([base_row, half]).astype(jnp.int32)
    planes = fixed_tables(edge)
    rim_own = passed_along(
        lax.dynamic_slice(specimen, (0, half, 0, 0), (2, 1, edge, width)), "tile", -1
    )
    across_amp = traded(amplitude, "pos", 2)
    mine = jnp.concatenate([scan_anchor, jnp.broadcast_to(counts, (1, 2))], 0)
    across = traded(mine, "pos", 2)
    accs = run_early(meta, mine, probe_field, specimen, amplitude, planes)
    rim_own, accs = lax.optimization_barrier((rim_own, accs))
    rims = (rim_own, traded(rim_own, "pos", 1))
    accs = run_middle(meta, mine, probe_field, specimen, rims, accs, amplitude, planes)
    sent_first, sent_rows, kept_rim, kept_low, kept_top, kept_probe = run_late(
        meta,
        (mine, across),
        probe_field,
        specimen,
        rims,
        accs,
        (amplitude, across_amp),
        planes,
    )
    got_first = traded(sent_first, "pos", 1)
    got_first, sent_rows = lax.optimization_barrier((got_first, sent_rows))
    got_rows = traded(sent_rows, "pos", 1)
    below = kept_rim + got_first[: 2 * edge].reshape(kept_rim.shape).astype(jnp.float32)
    below = passed_along(below.astype(jnp.bfloat16), "tile", 1)
    probe_part = (kept_probe + got_first[2 * edge :].astype(jnp.float32)).astype(jnp.bfloat16)
    distance = lax.axis_size("tile")
    while distance > 4:
        distance //= 2
        probe_part = early_sum(probe_part, traded(probe_part, "tile", distance))
    got_probe = traded(probe_part, "tile", 2)
    lower = (kept_low + got_rows[:, edge:].astype(jnp.float32)).astype(jnp.bfloat16)
    tile_grad = write_rows(meta, lower, traded(lower, "pos", 1), edge, specimen.shape)
    top = kept_top + got_rows[:, :edge].astype(jnp.float32)
    below, top, tile_grad = lax.optimization_barrier((below, top, tile_grad))
    upper = (top + below.astype(jnp.float32)).astype(jnp.bfloat16)
    upper_theirs = traded(upper, "pos", 1)
    _, got_probe = lax.optimization_barrier((upper, got_probe))
    probe_part = narrow_sum(probe_part, got_probe)
    probe_part = narrow_sum(probe_part, traded(probe_part, "tile", 1))
    tile_grad = write_rows(meta, upper, upper_theirs, 0, specimen.shape, tile_grad)
    probe_theirs, tile_grad = lax.optimization_barrier((traded(probe_part, "pos", 1), tile_grad))
    probe_own, probe_theirs = [unfolded(value, edge) for value in (probe_part, probe_theirs)]
    probe_total = jnp.where(
        half == 0, jnp.stack([probe_own, probe_theirs]), jnp.stack([probe_theirs, probe_own])
    ).astype(jnp.float32)
    return (tile_grad, probe_total)


def solution(mesh):
    return jax.shard_map(
        body,
        mesh=mesh,
        in_specs=(
            P(),
            P(None, None, "tile", None),
            P(("tile", "pos"), None, None),
            P(("tile", "pos"), None),
            P(("tile", "pos")),
        ),
        out_specs=(P(None, None, "tile", None), P()),
        check_vma=False,
    )
```

```python
import math

import jax
import jax.numpy as jnp
import ml_dtypes
import numpy as np
from jax import lax
from jax.experimental import pallas as pl
from jax.experimental.pallas import tpu as pltpu
from jax.sharding import PartitionSpec as P

PROP_COEF = 0.5
AMP_EPS = 0.05
LANES = 128
CHUNK = 16
EARLY = 4
MIDDLE = 4


def fixed_tables(edge):
    index = np.arange(edge)
    angles = (np.outer(index, index) % edge) * (2.0 * math.pi / edge)
    cosine = (np.cos(angles) / math.sqrt(edge)).astype(ml_dtypes.bfloat16).astype(np.float64)
    sine = (np.sin(angles) / math.sqrt(edge)).astype(ml_dtypes.bfloat16).astype(np.float64)
    forward = cosine - 1j * sine
    centred = np.where(index < edge // 2, index, index - edge)
    ramp = np.exp(-1j * (PROP_COEF * math.pi / edge) * centred * centred)
    spread = (np.conj(forward) * ramp[None, :]) @ forward
    planes = [
        plane for matrix in (spread, forward) for plane in (matrix.real, matrix.imag, -matrix.imag)
    ]
    return jnp.asarray(np.stack(planes).astype(ml_dtypes.bfloat16))


def lay_tables(planes, tables):
    edge = planes.shape[1]
    lo, hi = pl.ds(0, edge), pl.ds(edge, edge)
    for k in range(2):
        real, imag, negated = (planes[3 * k + i] for i in range(3))
        left, right = tables[2 * k : 2 * k + 2]
        left[lo, lo], left[lo, hi], left[hi, lo], left[hi, hi] = real, negated, imag, real
        right[lo, lo], right[lo, hi], right[hi, lo], right[hi, hi] = real, imag, negated, real


def interleaved(first, second):
    marks = [(k / len(first), 0, k) for k in range(len(first))]
    marks += [((k + 0.5) / len(second), 1, k) for k in range(len(second))]
    for _, which, k in sorted(marks):
        (first, second)[which][k]()


def slot_stages(slot, alive, base_row, refs, work):
    corner, probe, amp, tables, wide, acc, probe_acc = refs
    rolled, arriving, field, stack, joined = work
    left_a, right_a, left_f, right_f = tables
    edge = probe.shape[1]
    col_tiles = wide.shape[2]
    parts = edge // LANES
    lane = lax.broadcasted_iota(jnp.int32, (CHUNK, LANES), 1)
    row = corner[slot, 0] - base_row
    col = corner[slot, 1]
    first = jnp.minimum(col // LANES, col_tiles - parts - 1)
    shift = col - first * LANES
    turn = jnp.where(shift >= LANES, 0, shift)
    back = jnp.where(turn == 0, 0, LANES - turn)
    own = lane >= shift
    near = lane < LANES - shift

    def patch(part, s, i, j):
        rows = pl.ds(row + i, CHUNK)
        main = wide[part, s, first + j, rows, :]
        if j > 0:
            return main
        return jnp.where(own, main, wide[part, s, first + parts, rows, :])

    def place(part, s, i, j, value):
        rows = pl.ds(row + i, CHUNK)
        if j > 0:
            acc[part, s, first + j, rows, :] += value
        else:
            acc[part, s, first, rows, :] += jnp.where(own, value, 0.0)
            acc[part, s, first + parts, rows, :] += jnp.where(own, 0.0, value)

    def put(i, j, re, im):
        cols = pl.ds(j * LANES, LANES)
        stack[pl.ds(i, CHUNK), cols] = re.astype(jnp.bfloat16)
        stack[pl.ds(edge + i, CHUNK), cols] = im.astype(jnp.bfloat16)

    def halves():
        return [(j, pl.ds(j * LANES, LANES)) for j in range(parts)]

    def enter(i):
        rows = pl.ds(i, CHUNK)
        turned = [
            [pltpu.roll(probe[part, rows, cols], turn, 1) for j, cols in halves()]
            for part in range(2)
        ]
        for j, cols in halves():
            u_re, u_im = [
                jnp.where(own, turned[part][j], turned[part][j - 1]) for part in range(2)
            ]
            rolled[0, rows, cols] = u_re
            rolled[1, rows, cols] = u_im
            o_re, o_im = patch(0, 0, i, j), patch(1, 0, i, j)
            put(i, j, u_re * o_re - u_im * o_im, u_re * o_im + u_im * o_re)

    def second_slice(i):
        rows = pl.ds(i, CHUNK)
        for j, cols in halves():
            u_re, u_im = arriving[0, rows, cols], arriving[1, rows, cols]
            o_re, o_im = patch(0, 1, i, j), patch(1, 1, i, j)
            put(i, j, u_re * o_re - u_im * o_im, u_re * o_im + u_im * o_re)

    def residual(i):
        rows = pl.ds(i, CHUNK)
        for j, cols in halves():
            far_re, far_im = field[0, rows, cols], field[1, rows, cols]
            measured = amp[slot, rows, cols].astype(jnp.float32) * alive
            ratio = measured * lax.rsqrt(far_re * far_re + far_im * far_im + AMP_EPS)
            put(i, j, (alive - ratio) * far_re, (ratio - alive) * far_im)

    def second_grad(i):
        rows = pl.ds(i, CHUNK)
        for j, cols in halves():
            u_re, u_im = arriving[0, rows, cols], arriving[1, rows, cols]
            w_re, w_im = field[0, rows, cols], field[1, rows, cols]
            place(0, 1, i, j, u_re * w_re - u_im * w_im)
            place(1, 1, i, j, u_re * w_im + u_im * w_re)
            o_re, o_im = patch(0, 1, i, j), patch(1, 1, i, j)
            put(i, j, o_re * w_re - o_im * w_im, o_re * w_im + o_im * w_re)

    def first_grad(i):
        rows = pl.ds(i, CHUNK)
        turned = [[None] * parts for _ in range(2)]
        for j, cols in halves():
            u_re, u_im = rolled[0, rows, cols], rolled[1, rows, cols]
            w_re, w_im = field[0, rows, cols], field[1, rows, cols]
            place(0, 0, i, j, u_re * w_re - u_im * w_im)
            place(1, 0, i, j, u_re * w_im + u_im * w_re)
            o_re, o_im = patch(0, 0, i, j), patch(1, 0, i, j)
            turned[0][j] = pltpu.roll(o_re * w_re - o_im * w_im, back, 1)
            turned[1][j] = pltpu.roll(o_re * w_im + o_im * w_re, back, 1)
        for part in range(2):
            for j, cols in halves():
                after = turned[part][(j + 1) % parts]
                probe_acc[part, rows, cols] += jnp.where(near, turned[part][j], after)

    def two_sided(left, right, out):
        def rows_of(part):
            span = pl.ds(part * edge, edge)
            joined[:, span] = jnp.dot(
                left[span, :], stack[...], preferred_element_type=jnp.float32
            ).astype(jnp.bfloat16)

        def cols_of(part):
            out[part] = jnp.dot(
                joined[...],
                right[:, pl.ds(part * edge, edge)],
                preferred_element_type=jnp.float32,
            )

        return [lambda p=p: rows_of(p) for p in range(2)] + [
            lambda p=p: cols_of(p) for p in range(2)
        ]

    def each(step):
        return [lambda i=i: step(i) for i in range(0, edge, CHUNK)]

    return [
        each(enter),
        two_sided(left_a, right_a, arriving),
        each(second_slice),
        two_sided(left_f, right_f, field),
        each(residual),
        two_sided(left_f, right_f, field),
        each(second_grad),
        two_sided(left_a, right_a, field),
        each(first_grad),
    ]


def own_marks(part, base_row, edge, tile_rows):
    slots = part.shape[0] - 1
    first, second, left = [], [], []
    ranks = [jnp.int32(0), jnp.int32(0)]
    for q in range(slots):
        live = jnp.where(q < part[slots, 0], 1, 0)
        inner = jnp.where(part[q, 0] - base_row + edge <= tile_rows, live, 0)
        first.append(jnp.where(ranks[0] < EARLY, inner, 0))
        ranks[0] = ranks[0] + inner
        rest = live - first[q]
        second.append(jnp.where(ranks[1] < MIDDLE, rest, 0))
        ranks[1] = ranks[1] + rest
        left.append(rest - second[q])
    return first, second, left


def put_in_order(order, marks):
    taken = jnp.int32(0)
    order[0] = 0
    for q, mark in enumerate(marks):
        order[taken] = q
        taken = taken + mark
    return taken


def fill_corners(corner, part):
    for q in range(part.shape[0] - 1):
        corner[q, 0] = part[q, 0]
        corner[q, 1] = part[q, 1]


def list_late(order, corner, mine, across, base_row, edge, tile_rows):
    slots = mine.shape[0] - 1
    fill_corners(corner, mine)
    marks = own_marks(mine, base_row, edge, tile_rows)[2]
    for q in range(slots):
        corner[slots + q, 0] = across[q, 0]
        corner[slots + q, 1] = across[q, 1]
        marks.append(jnp.where(q < across[slots, 0], 1, 0))
    return put_in_order(order, marks)


def run_pairs(order, total, base_row, refs, work):
    def visit(step, carry):
        a = order[2 * step]
        b_lives = 2 * step + 1 < total
        b = jnp.where(b_lives, order[2 * step + 1], a)
        ones = slot_stages(a, 1.0, base_row, refs, work[0])
        twos = slot_stages(b, jnp.where(b_lives, 1.0, 0.0), base_row, refs, work[1])
        for step_now in ones[0]:
            step_now()
        for k in range(1, len(ones)):
            if k % 2:
                interleaved(ones[k], twos[k - 1])
            else:
                interleaved(twos[k - 1], ones[k])
        for step_now in twos[-1]:
            step_now()
        return carry

    lax.fori_loop(0, (total + 1) // 2, visit, 0)


def widen(wide, source, start, part, s_from, s_to):
    rows = source.shape[-2]
    for t in range(wide.shape[2]):
        wide[part, s_to, t, pl.ds(start, rows), :] = source[
            part, s_from, :, pl.ds(t * LANES, LANES)
        ].astype(jnp.float32)


def fetch(copies, sems):
    started = {}
    for k, (group, source, target) in enumerate(copies):
        copy = pltpu.make_async_copy(source, target, sems.at[k])
        copy.start()
        started.setdefault(group, []).append(copy)

    def wait(group):
        for copy in started[group]:
            copy.wait()

    return wait


def zero_rows(acc, start, rows):
    for part in range(2):
        for s in range(acc.shape[1]):
            for t in range(acc.shape[2]):
                acc[part, s, t, pl.ds(start, rows), :] = jnp.zeros((rows, LANES), jnp.float32)


def lay_patches(wide, wait, spec, rims, half):
    slices, tile_rows = spec.shape[1:3]
    wait("spec")
    for part in range(2):
        for s in range(slices):
            widen(wide, spec, 0, part, s, s)
    if rims:
        wait("rim")
        for part in range(2):
            widen(wide, rims[0], tile_rows, part, 0, half)
            widen(wide, rims[1], tile_rows, part, 0, 1 - half)


def early_kernel(
    meta,
    mine,
    probe_any,
    spec_any,
    amp_any,
    planes_any,
    acc,
    probe_acc,
    order,
    corner,
    sems,
    probe,
    spec,
    amp,
    planes,
    la,
    ra,
    lf,
    rf,
    wide,
    *work,
):
    wait = fetch(
        [
            ("spec", spec_any, spec),
            ("planes", planes_any, planes),
            ("rest", probe_any, probe),
            ("rest", amp_any, amp),
        ],
        sems,
    )
    tables = (la, ra, lf, rf)
    edge, tile_rows = probe.shape[1], spec.shape[2]
    zero_rows(acc, 0, tile_rows)
    probe_acc[...] = jnp.zeros(probe_acc.shape, jnp.float32)
    fill_corners(corner, mine)
    total = put_in_order(order, own_marks(mine, meta[0], edge, tile_rows)[0])
    lay_patches(wide, wait, spec, (), meta[1])
    wait("planes")
    lay_tables(planes, tables)
    wait("rest")
    refs = (corner, probe, amp, tables, wide, acc, probe_acc)
    run_pairs(order, total, meta[0], refs, (work[:5], work[5:]))


def middle_kernel(
    meta,
    mine,
    probe_any,
    spec_any,
    rim_own_any,
    rim_other_any,
    acc_any,
    probe_acc_any,
    amp_any,
    planes_any,
    acc,
    probe_acc,
    order,
    corner,
    sems,
    probe,
    spec,
    amp,
    planes,
    la,
    ra,
    lf,
    rf,
    wide,
    rim_own,
    rim_other,
    *work,
):
    edge, tile_rows = probe.shape[1], spec.shape[2]
    wait = fetch(
        [
            ("spec", spec_any, spec),
            ("planes", planes_any, planes),
            ("rim", rim_own_any, rim_own),
            ("rim", rim_other_any, rim_other),
            ("acc", acc_any, acc.at[:, :, :, pl.ds(0, tile_rows), :]),
            ("acc", probe_acc_any, probe_acc),
            ("rest", probe_any, probe),
            ("rest", amp_any, amp),
        ],
        sems,
    )
    tables = (la, ra, lf, rf)
    zero_rows(acc, tile_rows, edge)
    fill_corners(corner, mine)
    total = put_in_order(order, own_marks(mine, meta[0], edge, tile_rows)[1])
    lay_patches(wide, wait, spec, (rim_own, rim_other), meta[1])
    wait("planes")
    lay_tables(planes, tables)
    wait("acc")
    wait("rest")
    refs = (corner, probe, amp, tables, wide, acc, probe_acc)
    run_pairs(order, total, meta[0], refs, (work[:5], work[5:]))


def late_kernel(
    meta,
    mine,
    across,
    probe_any,
    spec_any,
    rim_own_any,
    rim_other_any,
    acc_any,
    probe_acc_any,
    amp_any,
    across_amp_any,
    planes_any,
    send_first,
    send_rows,
    keep_rim,
    keep_low,
    keep_top,
    keep_probe,
    order,
    corner,
    sems,
    probe,
    spec,
    amp,
    planes,
    la,
    ra,
    lf,
    rf,
    wide,
    rim_own,
    rim_other,
    acc,
    probe_acc,
    *work,
):
    tile_rows, width = spec.shape[2:]
    edge = probe.shape[1]
    slots = mine.shape[0] - 1
    wait = fetch(
        [
            ("spec", spec_any, spec),
            ("planes", planes_any, planes),
            ("rim", rim_own_any, rim_own),
            ("rim", rim_other_any, rim_other),
            ("acc", acc_any, acc),
            ("acc", probe_acc_any, probe_acc),
            ("rest", probe_any, probe),
            ("rest", amp_any, amp.at[pl.ds(0, slots)]),
            ("rest", across_amp_any, amp.at[pl.ds(slots, slots)]),
        ],
        sems,
    )
    tables = (la, ra, lf, rf)
    half = meta[1]
    other = 1 - half
    col_tiles = width // LANES
    total = list_late(order, corner, mine, across, meta[0], edge, tile_rows)
    lay_patches(wide, wait, spec, (rim_own, rim_other), half)
    wait("planes")
    lay_tables(planes, tables)
    wait("acc")
    wait("rest")
    refs = (corner, probe, amp, tables, wide, acc, probe_acc)
    run_pairs(order, total, meta[0], refs, (work[:5], work[5:]))

    below = pl.ds(tile_rows, edge)
    low = pl.ds(edge, tile_rows - edge)
    top = pl.ds(0, edge)
    rows = pl.ds(0, tile_rows)
    for part in range(2):
        sign = 1.0 if part == 0 else -1.0
        for t in range(col_tiles):
            cols = pl.ds(t * LANES, LANES)
            send_first[pl.ds(part * edge, edge), cols] = (
                sign * acc[part, other, t, below, :]
            ).astype(jnp.bfloat16)
            send_rows[part, :, cols] = (sign * acc[part, other, t, rows, :]).astype(jnp.bfloat16)
            keep_rim[part, :, cols] = sign * acc[part, half, t, below, :]
            keep_low[part, :, cols] = sign * acc[part, half, t, low, :]
            keep_top[part, :, cols] = sign * acc[part, half, t, top, :]
    deep = keep_probe.shape[0]
    flip = jnp.where(other == 1, -1.0, 1.0)
    for piece in range(width // edge):
        piece_rows, cols = pl.ds(piece * deep, deep), pl.ds(piece * edge, edge)
        send_first[pl.ds(2 * edge, deep), cols] = (flip * probe_acc[other, piece_rows, :]).astype(
            jnp.bfloat16
        )
        keep_probe[:, cols] = -flip * probe_acc[half, piece_rows, :]


VMEM = pl.BlockSpec(memory_space=pltpu.VMEM)
SMEM = pl.BlockSpec(memory_space=pltpu.SMEM)
ANY = pl.BlockSpec(memory_space=pl.ANY)


def scratch(entries, slices, width, tile_rows, rows, edge, copies):
    planes = pltpu.VMEM((2, edge, edge), jnp.float32)
    table = pltpu.VMEM((2 * edge, 2 * edge), jnp.bfloat16)
    stack = pltpu.VMEM((2 * edge, edge), jnp.bfloat16)
    joined = pltpu.VMEM((edge, 2 * edge), jnp.bfloat16)
    lead = [
        pltpu.SMEM((entries + 1,), jnp.int32),
        pltpu.SMEM((entries, 2), jnp.int32),
        pltpu.SemaphoreType.DMA((copies,)),
        planes,
        pltpu.VMEM((2, slices, tile_rows, width), jnp.bfloat16),
        pltpu.VMEM((entries, edge, edge), jnp.bfloat16),
        pltpu.VMEM((6, edge, edge), jnp.bfloat16),
        table,
        table,
        table,
        table,
        pltpu.VMEM((2, slices, width // LANES, rows, LANES), jnp.float32),
    ]
    return lead, [planes, planes, planes, stack, joined] * 2


def run_early(meta, mine, probe, spec, amp, planes):
    edge = probe.shape[1]
    _, slices, tile_rows, width = spec.shape
    lead, work = scratch(amp.shape[0], slices, width, tile_rows, tile_rows, edge, 4)
    return pl.pallas_call(
        early_kernel,
        out_shape=(
            jax.ShapeDtypeStruct((2, slices, width // LANES, tile_rows, LANES), jnp.float32),
            jax.ShapeDtypeStruct((2, edge, edge), jnp.float32),
        ),
        in_specs=[SMEM] * 2 + [ANY] * 4,
        out_specs=(VMEM, VMEM),
        scratch_shapes=lead + work,
        compiler_params=pltpu.CompilerParams(vmem_limit_bytes=20 * 1024 * 1024),
        name="early_slots",
    )(meta, mine, probe, spec, amp, planes)


def run_middle(meta, mine, probe, spec, rims, accs, amp, planes):
    edge = probe.shape[1]
    _, slices, tile_rows, width = spec.shape
    total = tile_rows + edge
    operands = (probe, spec, *rims, *accs, amp, planes)
    lead, work = scratch(amp.shape[0], slices, width, tile_rows, total, edge, len(operands))
    rim = pltpu.VMEM((2, 1, edge, width), jnp.bfloat16)
    return pl.pallas_call(
        middle_kernel,
        out_shape=(
            jax.ShapeDtypeStruct((2, slices, width // LANES, total, LANES), jnp.float32),
            jax.ShapeDtypeStruct((2, edge, edge), jnp.float32),
        ),
        in_specs=[SMEM] * 2 + [ANY] * len(operands),
        out_specs=(VMEM, VMEM),
        scratch_shapes=lead + [rim, rim] + work,
        compiler_params=pltpu.CompilerParams(vmem_limit_bytes=24 * 1024 * 1024),
        name="middle_slots",
    )(meta, mine, *operands)


def run_late(meta, lists, probe, spec, rims, accs, amps, planes):
    edge = probe.shape[1]
    _, slices, tile_rows, width = spec.shape
    total = tile_rows + edge
    deep = edge * edge // width
    operands = (probe, spec, *rims, *accs, *amps, planes)
    entries = sum(amp.shape[0] for amp in amps)
    lead, work = scratch(entries, slices, width, tile_rows, total, edge, len(operands))
    rim = pltpu.VMEM((2, 1, edge, width), jnp.bfloat16)
    return pl.pallas_call(
        late_kernel,
        out_shape=(
            jax.ShapeDtypeStruct((2 * edge + deep, width), jnp.bfloat16),
            jax.ShapeDtypeStruct((2, tile_rows, width), jnp.bfloat16),
            jax.ShapeDtypeStruct((2, edge, width), jnp.float32),
            jax.ShapeDtypeStruct((2, tile_rows - edge, width), jnp.float32),
            jax.ShapeDtypeStruct((2, edge, width), jnp.float32),
            jax.ShapeDtypeStruct((deep, width), jnp.float32),
        ),
        in_specs=[SMEM] * 3 + [ANY] * len(operands),
        out_specs=(VMEM,) * 6,
        scratch_shapes=lead
        + [
            rim,
            rim,
            pltpu.VMEM((2, slices, width // LANES, total, LANES), jnp.float32),
            pltpu.VMEM((2, edge, edge), jnp.float32),
        ]
        + work,
        compiler_params=pltpu.CompilerParams(vmem_limit_bytes=28 * 1024 * 1024),
        name="late_slots",
    )(meta, *lists, *operands)


def write_rows(meta, own, theirs, start, shape, base=None):
    slices, rows, width = shape[1], own.shape[1], own.shape[2]

    def kernel(meta, own, theirs, *rest):
        out, wide, sems = rest[-3:]
        half = meta[1]
        copies = []
        for s, source in ((half, own), (1 - half, theirs)):
            for part in range(2):
                wide[s, part] = source[part].astype(jnp.float32)
                copy = pltpu.make_async_copy(
                    wide.at[s, part],
                    out.at[part, s, pl.ds(start, rows), :],
                    sems.at[len(copies)],
                )
                copy.start()
                copies.append(copy)
        for copy in copies:
            copy.wait()

    extra = [] if base is None else [base]
    return pl.pallas_call(
        kernel,
        out_shape=jax.ShapeDtypeStruct(shape, jnp.float32),
        in_specs=[SMEM, VMEM, VMEM] + [ANY] * len(extra),
        out_specs=ANY,
        input_output_aliases={} if base is None else {3: 0},
        scratch_shapes=[
            pltpu.VMEM((slices, 2, rows, width), jnp.float32),
            pltpu.SemaphoreType.DMA((2 * slices,)),
        ],
        compiler_params=pltpu.CompilerParams(vmem_limit_bytes=16 * 1024 * 1024),
        cost_estimate=pl.CostEstimate(
            flops=0, bytes_accessed=2 * slices * rows * width * 6, transcendentals=0
        ),
        name="write_rows",
    )(meta, own, theirs, *extra)


def traded(value, axis, distance):
    count = lax.axis_size(axis)
    return lax.ppermute(value, axis, [(i, i ^ distance) for i in range(count)])


def passed_along(value, axis, steps):
    count = lax.axis_size(axis)
    initial, last = (max(0, -steps), min(count, count - steps))
    return lax.ppermute(value, axis, [(source, source + steps) for source in range(initial, last)])


def narrow_sum(own, got):
    return (own.astype(jnp.float32) + got.astype(jnp.float32)).astype(jnp.bfloat16)


def early_sum(own, got):
    def kernel(own, got, out):
        total = own[...].astype(jnp.float32) + got[...].astype(jnp.float32)
        out[...] = total.astype(jnp.bfloat16)

    return pl.pallas_call(
        kernel,
        out_shape=jax.ShapeDtypeStruct(own.shape, own.dtype),
        in_specs=[VMEM, VMEM],
        out_specs=VMEM,
        cost_estimate=pl.CostEstimate(flops=10**10, bytes_accessed=10**8, transcendentals=0),
        compiler_params=pltpu.CompilerParams(vmem_limit_bytes=8 * 1024 * 1024),
        name="early_sum",
    )(own, got)


def unfolded(value, edge):
    return jnp.concatenate([value[:, k : k + edge] for k in range(0, value.shape[1], edge)], 0)


def body(probe_field, specimen, amplitude, scan_anchor, counts):
    edge = probe_field.shape[1]
    _, slices, tile_rows, width = specimen.shape
    half = lax.axis_index("pos") % 2
    base_row = lax.axis_index("tile") * tile_rows
    meta = jnp.stack([base_row, half]).astype(jnp.int32)
    planes = fixed_tables(edge)
    rim_own = passed_along(
        lax.dynamic_slice(specimen, (0, half, 0, 0), (2, 1, edge, width)), "tile", -1
    )
    across_amp = traded(amplitude, "pos", 2)
    mine = jnp.concatenate([scan_anchor, jnp.broadcast_to(counts, (1, 2))], 0)
    across = traded(mine, "pos", 2)
    accs = run_early(meta, mine, probe_field, specimen, amplitude, planes)
    rim_own, accs = lax.optimization_barrier((rim_own, accs))
    rims = (rim_own, traded(rim_own, "pos", 1))
    accs = run_middle(meta, mine, probe_field, specimen, rims, accs, amplitude, planes)
    sent_first, sent_rows, kept_rim, kept_low, kept_top, kept_probe = run_late(
        meta,
        (mine, across),
        probe_field,
        specimen,
        rims,
        accs,
        (amplitude, across_amp),
        planes,
    )
    got_first = traded(sent_first, "pos", 1)
    got_first, sent_rows = lax.optimization_barrier((got_first, sent_rows))
    got_rows = traded(sent_rows, "pos", 1)
    below = kept_rim + got_first[: 2 * edge].reshape(kept_rim.shape).astype(jnp.float32)
    below = passed_along(below.astype(jnp.bfloat16), "tile", 1)
    probe_part = (kept_probe + got_first[2 * edge :].astype(jnp.float32)).astype(jnp.bfloat16)
    distance = lax.axis_size("tile")
    while distance > 4:
        distance //= 2
        probe_part = early_sum(probe_part, traded(probe_part, "tile", distance))
    got_probe = traded(probe_part, "tile", 2)
    lower = (kept_low + got_rows[:, edge:].astype(jnp.float32)).astype(jnp.bfloat16)
    tile_grad = write_rows(meta, lower, traded(lower, "pos", 1), edge, specimen.shape)
    top = kept_top + got_rows[:, :edge].astype(jnp.float32)
    below, top, tile_grad = lax.optimization_barrier((below, top, tile_grad))
    upper = (top + below.astype(jnp.float32)).astype(jnp.bfloat16)
    upper_theirs = traded(upper, "pos", 1)
    _, got_probe = lax.optimization_barrier((upper, got_probe))
    probe_part = narrow_sum(probe_part, got_probe)
    probe_part = narrow_sum(probe_part, traded(probe_part, "tile", 1))
    tile_grad = write_rows(meta, upper, upper_theirs, 0, specimen.shape, tile_grad)
    probe_theirs, tile_grad = lax.optimization_barrier((traded(probe_part, "pos", 1), tile_grad))
    probe_own, probe_theirs = [unfolded(value, edge) for value in (probe_part, probe_theirs)]
    probe_total = jnp.where(
        half == 0, jnp.stack([probe_own, probe_theirs]), jnp.stack([probe_theirs, probe_own])
    ).astype(jnp.float32)
    return (tile_grad, probe_total)


def solution(mesh):
    return jax.shard_map(
        body,
        mesh=mesh,
        in_specs=(
            P(),
            P(None, None, "tile", None),
            P(("tile", "pos"), None, None),
            P(("tile", "pos"), None),
            P(("tile", "pos")),
        ),
        out_specs=(P(None, None, "tile", None), P()),
        check_vma=False,
    )
```
